32 devices in a mesh: groups: 2 (over x), ctx: 16 (over z, y, core).
Axes of the slice: x: 2, y: 2, z: 4, core: 2. Of those that a mesh axis runs over, the one named last changes fastest.
Arguments:
- queries: bfloat16 [128, 8192], P(('groups', 'ctx')), parts along dimension 0
- cache_keys: bfloat16 [49152, 512], P(('groups', 'ctx')), parts along dimension 0
- cached_value_rows: bfloat16 [49152, 512], P(('groups', 'ctx')), parts along dimension 0, may hold values from -5 to 5
- new_keys: bfloat16 [128, 512], P(('groups', 'ctx')), parts along dimension 0
- prompt_value_rows: bfloat16 [128, 512], P(('groups', 'ctx')), parts along dimension 0, may hold values from -5 to 5
- cache_len: int32 [32], P(('groups', 'ctx')), parts along dimension 0, may hold values from 1 to 1536, 15360 in all
- prompt_start: int32 [2], P('groups'), parts along dimension 0, may hold values from 7680 to 15360
Outputs:
- attended: bfloat16 [128, 8192], P(('groups', 'ctx')), parts along dimension 0
The draws below stay inside these ranges and needn't reach their ends.
There are 2 independent parts, one for each index of `groups`. The reference program is written for one: setup_inputs(seed, part) draws one part's arguments, and reference() takes and returns one part's arrays. A program takes and returns all parts, laid end to end along the dimension named above; each array names one. Nothing has to cross between parts.
Inputs may be any that keep to these rules, and one draw needn't show every extreme that they name: cache_len sums to 15360; some shard is full.
All inputs are finite; a program needn't handle non-finite values.
Results may differ from the reference program's by a relative error of at most 0.0024.
Values may be sent and summed in bfloat16 or wider, within the bound.
No kernel may reach another device: no remote copies, remote signals or barrier semaphores. Data moves between devices by JAX's collectives and lax.ppermute only.
A program may use at most 64 MiB of HBM per device.

```python
import math
import jax
import jax.numpy as jnp
import numpy as np
from jax import lax

QUERY_HEADS = 64
KEY_VALUE_HEADS = 4
HEAD_SIZE = 128
Q_DEV = 4
CACHE_DEV = 1536
PROMPT_TOKENS = 64
CACHE_SLOTS = 24576
LIVE = 15360
N_CTX = 16


def shared_keys(key):
    return jax.random.truncated_normal(key, -4.0, 4.0, (CACHE_SLOTS, KEY_VALUE_HEADS * HEAD_SIZE), jnp.float32)


def draw_cache_keys(key, part):
    return shared_keys(key).astype(jnp.bfloat16)


def draw_queries(key, part):
    key = jax.random.fold_in(key, 7)
    value_rows = 2.5 * jax.random.truncated_normal(key, -4.0, 4.0, (PROMPT_TOKENS, QUERY_HEADS * HEAD_SIZE), jnp.float32)
    return value_rows.astype(jnp.bfloat16)


def draw_new_keys(key, part):
    key = jax.random.fold_in(key, 9)
    value_rows = jax.random.truncated_normal(key, -4.0, 4.0, (PROMPT_TOKENS, KEY_VALUE_HEADS * HEAD_SIZE), jnp.float32)
    return value_rows.astype(jnp.bfloat16)


def block_levels(key, shape, pieces, least, high):
    factor_of, own = 1.0, jax.random.fold_in(key, 6)
    for position, blocks in pieces:
        heights = jnp.exp(jax.random.uniform(jax.random.fold_in(own, position), (blocks,), jnp.float32, least / len(pieces), high / len(pieces)))
        factor_of = factor_of * jnp.repeat(heights, shape[position] // blocks).reshape([-1 if axis == position else 1 for axis in range(len(shape))])
    return factor_of


def length_profile(count, total, bound, lean):
    loads = [(1 << 20) // math.isqrt(standing ** lean) + 1 for standing in range(2, count + 1)]
    rest, counts = total - bound - (count - 1), [1] * (count - 1)
    while rest > 0:
        free = [i for i in range(count - 1) if counts[i] < bound]
        whole, remaining = sum([loads[i] for i in free]), rest
        for i in free:
            addition = min(bound - counts[i], max(1, remaining * loads[i] // whole), rest)
            counts[i] = counts[i] + addition
            rest = rest - addition
    return np.array([bound] + counts)


def uneven(own_key, number_of, total, limit, skew):
    if number_of == 2:
        one = jax.random.randint(own_key, (), max(1, total - limit), min(limit, total - 1) + 1)
        return jnp.stack([one, total - one])
    sizes = jnp.asarray(length_profile(number_of, total, limit, skew), jnp.int32)
    couples = (number_of - 1) // 2
    source_of, taker = sizes[1:1 + 2 * couples:2], sizes[2:2 + 2 * couples:2]
    margin = jnp.minimum(source_of - 1, limit - taker)
    shifted = jax.random.randint(jax.random.fold_in(own_key, 1), (couples,), 0, 1 << 20) % (margin + 1)
    sizes = sizes.at[1:1 + 2 * couples:2].set(source_of - shifted).at[2:2 + 2 * couples:2].set(taker + shifted)
    return sizes[jax.random.permutation(jax.random.fold_in(own_key, 2), number_of)]


def noise(key, dims, width, reach, pieces=(), kind=jnp.bfloat16):
    result = width * jax.random.normal(key, dims, jnp.float32)
    if pieces:
        result = result * block_levels(key, dims, pieces, -0.22, 0.18)
    return jnp.clip(result, -reach, reach).astype(kind)


def setup_inputs(seed: int = 0, part: int = 0) -> dict:
    key_list = jax.random.split(jax.random.key(seed), 8)
    part_keys = jax.random.split(jax.random.fold_in(key_list[7], part), 8)
    return {
        "queries": draw_queries(jax.random.fold_in(jax.random.fold_in(key_list[7], part), 71), part),
        "cache_keys": draw_cache_keys(jax.random.fold_in(jax.random.fold_in(key_list[7], part), 71), part),
        "cached_value_rows": noise(part_keys[2], (CACHE_SLOTS, KEY_VALUE_HEADS * HEAD_SIZE), 1.0, 5.0, ((0, 16),)),
        "new_keys": draw_new_keys(jax.random.fold_in(jax.random.fold_in(key_list[7], part), 71), part),
        "prompt_value_rows": noise(part_keys[4], (PROMPT_TOKENS, KEY_VALUE_HEADS * HEAD_SIZE), 1.0, 5.0, ((0, 16),)),
        "cache_len": uneven(part_keys[5], N_CTX, LIVE, CACHE_DEV, 2).astype(jnp.int32),
        "prompt_start": jax.random.randint(part_keys[6], (1,), LIVE // 2, LIVE + 1).astype(jnp.int32),
    }


floor_score = -1e+30

def shard_attention(queries, key_rows, value_rows, visible_mask):
    count = queries.shape[0]
    length = key_rows.shape[0]
    head_dim = HEAD_SIZE
    heads = QUERY_HEADS
    key_value_heads = KEY_VALUE_HEADS
    group = heads // key_value_heads
    block_rows = min(count, max(1, 1024 // heads))
    blocks = count // block_rows
    grouped = queries.reshape(blocks, block_rows, key_value_heads, group, head_dim)
    key_heads = key_rows.reshape(length, key_value_heads, head_dim).astype(jnp.float32)
    value_heads = value_rows.reshape(length, key_value_heads, head_dim).astype(jnp.float32)
    masks = visible_mask.reshape(blocks, block_rows, length)
    scale = 1.0 / math.sqrt(head_dim)

    def one_block(inputs):
        query_block, mask_block = inputs
        scores = jnp.einsum('qhgd,khd->qhgk', query_block.astype(jnp.float32), key_heads) * scale
        allowed = mask_block[:, None, None, :]
        top = lax.optimization_barrier(jnp.max(jnp.where(allowed, scores, floor_score), axis=3))
        weights = jnp.where(allowed, jnp.exp(scores - top[..., None]), 0.0)
        total = lax.optimization_barrier(jnp.sum(weights, axis=3))
        rounded = lax.optimization_barrier(weights.astype(jnp.bfloat16)).astype(jnp.float32)
        summed = jnp.einsum('qhgk,khd->qhgd', rounded, value_heads)
        return (top, total, summed)
    top_scores, total_weights, sum_rows = lax.map(one_block, (grouped, masks))
    return (top_scores.reshape(count, heads), total_weights.reshape(count, heads), sum_rows.reshape(count, heads, head_dim))

def reference(queries, cache_keys, cached_value_rows, new_keys, prompt_value_rows, cache_len, prompt_start):
    starts = (jnp.cumsum(cache_len) - cache_len).astype(jnp.int32)
    row_ids = jnp.arange(PROMPT_TOKENS, dtype=jnp.int32)
    slot_ids = jnp.arange(CACHE_DEV, dtype=jnp.int32)
    fresh_ids = jnp.arange(Q_DEV, dtype=jnp.int32)

    def step(carry, shard):
        best, denom, numer = carry
        cache_from = (shard * CACHE_DEV).astype(jnp.int32)
        fresh_from = (shard * Q_DEV).astype(jnp.int32)
        key_rows = jnp.concatenate([lax.dynamic_slice_in_dim(cache_keys, cache_from, CACHE_DEV, 0), lax.dynamic_slice_in_dim(new_keys, fresh_from, Q_DEV, 0)], axis=0)
        value_rows = jnp.concatenate([lax.dynamic_slice_in_dim(cached_value_rows, cache_from, CACHE_DEV, 0), lax.dynamic_slice_in_dim(prompt_value_rows, fresh_from, Q_DEV, 0)], axis=0)
        live_slots = (slot_ids < cache_len[shard]) & (starts[shard] + slot_ids < prompt_start[0])
        causal = (fresh_from + fresh_ids)[None, :] <= row_ids[:, None]
        visible_mask = jnp.concatenate([jnp.broadcast_to(live_slots[None, :], (PROMPT_TOKENS, CACHE_DEV)), causal], axis=1)
        top, total, summed = shard_attention(queries, key_rows, value_rows, visible_mask)
        merged_best = jnp.maximum(best, top)
        old_factor = jnp.exp(best - merged_best)
        new_factor = jnp.exp(top - merged_best)
        denom = denom * old_factor + total * new_factor
        numer = numer * old_factor[..., None] + summed * new_factor[..., None]
        return ((merged_best, denom, numer), None)
    start_state = (jnp.full((PROMPT_TOKENS, QUERY_HEADS), floor_score, jnp.float32), jnp.zeros((PROMPT_TOKENS, QUERY_HEADS), jnp.float32), jnp.zeros((PROMPT_TOKENS, QUERY_HEADS, HEAD_SIZE), jnp.float32))
    final, unused = lax.scan(step, start_state, jnp.arange(N_CTX, dtype=jnp.int32))
    best, denom, numer = final
    return (numer / denom[..., None]).astype(jnp.bfloat16).reshape(PROMPT_TOKENS, QUERY_HEADS * HEAD_SIZE)
```

```python
import functools
import math

import jax
import jax.numpy as jnp
from jax import lax
from jax.experimental import pallas as pl
from jax.experimental.pallas import tpu as pltpu
from jax.sharding import PartitionSpec as P

KEY_VALUE_HEADS = 4
LANES = 128
CORES = 2
FLOOR = -1e30
KEY_TILE = 256
STEP = 2.0**15
F32 = jnp.float32
BF16 = jnp.bfloat16
I16 = jnp.int16
I32 = jnp.int32


def lane_ids(rows):
    return lax.broadcasted_iota(I32, (rows, LANES), 1)


def row_ids(rows):
    return lax.broadcasted_iota(I32, (rows, LANES), 0)


def encode_stats(top, total, exponent, heads):
    size = jnp.abs(top)
    level = jnp.zeros_like(top)
    scaled = top
    for i in range(1, 9):
        above = size >= STEP**i
        level = level + jnp.where(above, 1.0, 0.0)
        scaled = scaled * jnp.where(above, 1.0 / STEP, 1.0)
    a = jnp.floor(scaled)
    rest = (scaled - a) * STEP
    b = jnp.floor(rest)
    c = jnp.floor((rest - b) * STEP)
    scaled_log = jnp.log2(total) * 1024.0
    la = jnp.floor(scaled_log)
    lb = jnp.floor((scaled_log - la) * STEP)
    live = lane_ids(top.shape[0]) < heads

    def place(parts):
        out = None
        for i, part in enumerate(parts):
            part = jnp.where(live, part, 0.0)
            part = part if i == 0 else pltpu.roll(part, i * heads, 1)
            out = part if out is None else out + part
        return out.astype(I32).astype(I16)

    return place([level, a, b, c]), place([exponent, la, lb])


def decode_stats(first, second, heads):
    first = first.astype(I32).astype(F32)
    second = second.astype(I32).astype(F32)

    def part(plane, i):
        return plane if i == 0 else pltpu.roll(plane, LANES - i * heads, 1)

    level = part(first, 0)
    top = part(first, 1) + (part(first, 2) + part(first, 3) * (1.0 / STEP)) * (1.0 / STEP)
    for i in range(1, 9):
        top = top * jnp.where(level >= i, STEP, 1.0)
    total = jnp.exp2((part(second, 1) + part(second, 2) * (1.0 / STEP)) * (1.0 / 1024.0))
    return top, total, part(second, 0)


def exponent_of(peak):
    return jnp.clip(jnp.floor(jnp.log2(jnp.maximum(peak, 1e-30))) + 1.0, -100.0, 15.0)


def to_fixed(rows, exponent):
    return jnp.clip(jnp.floor(rows * jnp.exp2(15.0 - exponent) + 0.5), -32767.0, 32767.0).astype(I32).astype(I16)


def pack_kernel(info, length, queries, new_keys, new_values, mine, other):
    rows = queries.shape[0]
    half, half_kv = queries.shape[1] // CORES, new_keys.shape[1] // CORES
    core = info[0]
    lane = lane_ids(rows)
    count = jnp.full((rows, LANES), length[0], I32)
    coded = jnp.where(lane == 0, count // LANES, jnp.where(lane == 1, count % LANES, 0))
    coded = coded.astype(F32).astype(BF16)
    for out, side in ((mine, core), (other, 1 - core)):
        out[:, :half] = queries[:, pl.ds(pl.multiple_of(side * half, LANES), half)]
        out[:, half : half + LANES] = coded
        at = half + LANES
        out[:, at : at + half_kv] = new_keys[:, pl.ds(pl.multiple_of(side * half_kv, LANES), half_kv)]
        at = at + half_kv
        out[:, at : at + half_kv] = new_values[:, pl.ds(pl.multiple_of(side * half_kv, LANES), half_kv)]


def pack(info, length, queries, new_keys, new_values):
    rows = queries.shape[0]
    wide = queries.shape[1] // CORES + LANES + 2 * new_keys.shape[1] // CORES
    shape = jax.ShapeDtypeStruct((rows, wide), BF16)
    smem = pl.BlockSpec(memory_space=pltpu.SMEM)
    vmem = pl.BlockSpec(memory_space=pltpu.VMEM)
    return pl.pallas_call(
        pack_kernel,
        out_shape=(shape, shape),
        in_specs=[smem, smem, vmem, vmem, vmem],
        out_specs=(vmem, vmem),
    )(info, length, queries, new_keys, new_values)


def chip_offsets(info, block, stages):
    off = jnp.zeros_like(block)
    for i in range(stages):
        off = off ^ jnp.where((block >> i) & 1 == 1, info[4 + i], 0)
    return off


def attend_kernel(
    sizes, info, queries, extra_low, extra_high, fresh, keys_a, keys_b, values_a, values_b, out, top_plane,
    total_plane, scale_plane, scores, peak, mass, sums
):
    own_rows, stages, first_block, group, kv_heads, slots = sizes
    chip_rows = CORES * own_rows
    tokens = queries.shape[0]
    head = pl.program_id(1)
    core, chip, me, start = info[0], info[1], info[2], info[3]
    factor = math.log2(math.e) / math.sqrt(LANES)

    def token_parts(rows, base_row):
        row = row_ids(rows) + base_row
        place = chip ^ chip_offsets(info, row // chip_rows, stages)
        inside = row % chip_rows
        return place * CORES + (core ^ (inside // own_rows)), inside % own_rows

    all_low, all_high = extra_low.shape[0], extra_high.shape[0]
    before = [0.0, 0.0]
    length = [0.0, 0.0]
    for ref, rows, base in ((extra_low, all_low, 0), (extra_high, all_high, all_low)):
        shard, inner = token_parts(rows, base)
        coded = ref[...].astype(F32)
        lane = lane_ids(rows)
        counts = jnp.where(lane == 0, coded * float(LANES), jnp.where(lane == 1, coded, 0.0))
        counts = jnp.where(inner == 0, counts, 0.0)
        for s, holder in enumerate((me, me ^ 1)):
            before[s] = before[s] + jnp.sum(jnp.where(shard < holder, counts, 0.0))
            length[s] = length[s] + jnp.sum(jnp.where(shard == holder, counts, 0.0))
    limits = []
    for s in range(2):
        limit = jnp.minimum(length[s].astype(I32), start - before[s].astype(I32))
        limits.append(jnp.clip(limit, 0, slots))

    first = head * group
    wide = group * LANES
    q_rows = queries[:, pl.ds(pl.multiple_of(first * LANES, LANES), wide)]
    q = jnp.concatenate([q_rows[:, g * LANES : (g + 1) * LANES] for g in range(group)], axis=0)
    rows = group * tokens
    nt = (((1,), (1,)), ((), ()))

    pad = jnp.zeros((LANES - chip_rows, LANES), F32)
    half_kv = fresh.shape[1] // 2
    at = pl.multiple_of(head * LANES, LANES)
    fresh_keys = jnp.concatenate([fresh[:, pl.ds(at, LANES)].astype(F32), pad], 0).astype(BF16)
    fresh_values = jnp.concatenate(
        [fresh[:, pl.ds(pl.multiple_of(half_kv + head * LANES, LANES), LANES)].astype(F32), pad], 0
    ).astype(BF16)
    fresh_scores = lax.dot_general(q, fresh_keys, nt, preferred_element_type=F32)
    shard, inner = token_parts(tokens, first_block * chip_rows + pl.program_id(0) * tokens)
    token = shard * own_rows + inner
    lane = lane_ids(tokens)

    parts = []
    for s, (keys, values, holder) in enumerate(((keys_a, values_a, me), (keys_b, values_b, me ^ 1))):
        limit = limits[s]
        whole = limit // KEY_TILE
        tail = limit - whole * KEY_TILE
        in_shard = (lane >= s * own_rows) & (lane < (s + 1) * own_rows)
        seen = in_shard & (holder * own_rows + lane - s * own_rows <= token)
        seen = jnp.concatenate([seen.astype(F32)] * group, axis=0) > 0.5
        peak[...] = jnp.where(seen, fresh_scores, FLOOR)

        def score(j):
            at = pl.multiple_of(j * KEY_TILE, KEY_TILE)
            return lax.dot_general(q, keys[pl.ds(at, KEY_TILE), :], nt, preferred_element_type=F32)

        def raise_peak(tile):
            best = peak[...]
            for i in range(KEY_TILE // LANES):
                best = jnp.maximum(best, tile[:, i * LANES : (i + 1) * LANES])
            peak[...] = best

        def first_pass(j, carry):
            tile = score(j)
            scores[j] = tile
            raise_peak(tile)
            return carry

        lax.fori_loop(0, whole, first_pass, 0)
        slot = lax.broadcasted_iota(I32, (rows, KEY_TILE), 1)

        @pl.when(tail > 0)
        def _():
            tile = jnp.where(slot < tail, score(whole), FLOOR)
            scores[whole] = tile
            raise_peak(tile)

        top = jnp.max(peak[...], axis=1, keepdims=True)
        weight = jnp.where(seen, jnp.exp2((fresh_scores - top) * factor), 0.0)
        mass[...] = weight
        sums[s] = lax.dot_general(
            weight.astype(BF16), fresh_values, (((1,), (0,)), ((), ())), preferred_element_type=F32
        )

        def add(j, weight):
            more = mass[...]
            for i in range(KEY_TILE // LANES):
                more = more + weight[:, i * LANES : (i + 1) * LANES]
            mass[...] = more
            at = pl.multiple_of(j * KEY_TILE, KEY_TILE)
            sums[s] += lax.dot_general(
                weight.astype(BF16), values[pl.ds(at, KEY_TILE), :], (((1,), (0,)), ((), ())),
                preferred_element_type=F32,
            )

        def second_pass(j, carry):
            add(j, jnp.exp2((scores[j] - top) * factor))
            return carry

        lax.fori_loop(0, whole, second_pass, 0)

        @pl.when(tail > 0)
        def _():
            add(whole, jnp.where(slot < tail, jnp.exp2((scores[whole] - top) * factor), 0.0))

        parts.append((top, jnp.sum(mass[...], axis=1, keepdims=True)))

    (top_a, mass_a), (top_b, mass_b) = parts
    top = jnp.maximum(top_a, top_b)
    scale_a = jnp.exp2((top_a - top) * factor)
    scale_b = jnp.exp2((top_b - top) * factor)
    total = jnp.maximum(mass_a * scale_a + mass_b * scale_b, 1.0)
    merged = (sums[0] * scale_a + sums[1] * scale_b) / total
    exponent = exponent_of(jnp.max(jnp.abs(merged), axis=1, keepdims=True))
    fixed = to_fixed(merged, exponent)
    for g in range(group):
        at = pl.multiple_of((first + g) * LANES, LANES)
        out[:, pl.ds(at, LANES)] = fixed[g * tokens : (g + 1) * tokens]

    @pl.when(head == 0)
    def _():
        top_plane[...] = jnp.full(top_plane.shape, FLOOR, F32)
        total_plane[...] = jnp.ones(total_plane.shape, F32)
        scale_plane[...] = jnp.zeros(scale_plane.shape, F32)

    tops, totals, scales = top_plane[...], total_plane[...], scale_plane[...]
    for g in range(group):
        here = lane == first + g
        cut = slice(g * tokens, (g + 1) * tokens)
        tops = jnp.where(here, top[cut], tops)
        totals = jnp.where(here, total[cut], totals)
        scales = jnp.where(here, exponent[cut], scales)
    top_plane[...] = tops
    total_plane[...] = totals
    scale_plane[...] = scales

    @pl.when(head == kv_heads - 1)
    def _():
        heads = group * kv_heads
        left, right = encode_stats(tops, totals, scales, heads)
        out[:, heads * LANES : (heads + 1) * LANES] = left
        out[:, (heads + 1) * LANES :] = right


def attend(info, queries, low, high, fresh, keys_a, keys_b, values_a, values_b, *, own_rows, stages, first_block):
    count = queries.shape[0]
    tokens = min(count, 32)
    slots = keys_a.shape[0]
    kv_heads = keys_a.shape[1] // LANES // CORES
    heads = queries.shape[1] // LANES - 1
    group = heads // kv_heads
    tiles = -(-slots // KEY_TILE)
    sizes = (own_rows, stages, first_block, group, kv_heads, slots)
    half_kv = kv_heads * LANES
    kv = pl.BlockSpec((slots, LANES), lambda i, h, info: (0, info[0] * kv_heads + h))
    return pl.pallas_call(
        functools.partial(attend_kernel, sizes),
        out_shape=jax.ShapeDtypeStruct((count, (heads + 2) * LANES), I16),
        grid_spec=pltpu.PrefetchScalarGridSpec(
            num_scalar_prefetch=1,
            grid=(count // tokens, kv_heads),
            in_specs=[
                pl.BlockSpec((tokens, (heads + 1) * LANES), lambda i, h, info: (i, 0)),
                pl.BlockSpec((low.shape[0], LANES), lambda i, h, info: (0, heads)),
                pl.BlockSpec((high.shape[0], LANES), lambda i, h, info: (0, heads)),
                pl.BlockSpec((CORES * own_rows, 2 * half_kv), lambda i, h, info: (0, 0)),
                kv, kv, kv, kv,
            ],
            out_specs=pl.BlockSpec((tokens, (heads + 2) * LANES), lambda i, h, info: (i, 0)),
            scratch_shapes=[
                pltpu.VMEM((tokens, LANES), F32),
                pltpu.VMEM((tokens, LANES), F32),
                pltpu.VMEM((tokens, LANES), F32),
                pltpu.VMEM((tiles, group * tokens, KEY_TILE), F32),
                pltpu.VMEM((group * tokens, LANES), F32),
                pltpu.VMEM((group * tokens, LANES), F32),
                pltpu.VMEM((2, group * tokens, LANES), F32),
            ],
        ),
        compiler_params=pltpu.CompilerParams(vmem_limit_bytes=40 << 20),
    )(info, queries, low, high, fresh, keys_a, keys_b, values_a, values_b)


def merge_kernel(last, left, right, *outs):
    rows = left.shape[0]
    heads = left.shape[1] // LANES - 2
    factor = math.log2(math.e) / math.sqrt(LANES)

    def stats(ref):
        return decode_stats(ref[:, heads * LANES : (heads + 1) * LANES], ref[:, (heads + 1) * LANES :], heads)

    top_a, total_a, exp_a = stats(left)
    top_b, total_b, exp_b = stats(right)
    top = jnp.maximum(top_a, top_b)
    mass_a = total_a * jnp.exp2((top_a - top) * factor)
    mass_b = total_b * jnp.exp2((top_b - top) * factor)
    total = mass_a + mass_b
    part_a = mass_a / total * jnp.exp2(exp_a - 15.0)
    part_b = mass_b / total * jnp.exp2(exp_b - 15.0)
    lane = lane_ids(rows)
    scales = jnp.zeros((rows, LANES), F32)
    cut = rows // 2
    for h in range(heads):
        at = slice(h * LANES, (h + 1) * LANES)
        value = left[:, at].astype(I32).astype(F32) * part_a[:, h : h + 1]
        value = value + right[:, at].astype(I32).astype(F32) * part_b[:, h : h + 1]
        if last:
            outs[0][:, at] = value[:cut].astype(BF16)
            outs[1][:, at] = value[cut:].astype(BF16)
        else:
            exponent = exponent_of(jnp.max(jnp.abs(value), axis=1, keepdims=True))
            fixed = jnp.clip(jnp.floor(value * jnp.exp2(15.0 - exponent) + 0.5), -32767.0, 32767.0).astype(I32)
            outs[0][:, at] = fixed[:cut].astype(I16)
            outs[1][:, at] = fixed[cut:].astype(I16)
            scales = jnp.where(lane == h, exponent, scales)
    if not last:
        first, second = encode_stats(top, total, scales, heads)
        first, second = first.astype(I32), second.astype(I32)
        for out, part in ((outs[0], slice(0, cut)), (outs[1], slice(cut, rows))):
            out[:, heads * LANES : (heads + 1) * LANES] = first[part].astype(I16)
            out[:, (heads + 1) * LANES :] = second[part].astype(I16)


def merge(left, right, last):
    rows, wide = left.shape
    shape = (
        jax.ShapeDtypeStruct((rows // 2, wide - 2 * LANES), BF16)
        if last
        else jax.ShapeDtypeStruct((rows // 2, wide), I16)
    )
    vmem = pl.BlockSpec(memory_space=pltpu.VMEM)
    return pl.pallas_call(
        functools.partial(merge_kernel, last),
        out_shape=(shape, shape),
        in_specs=[vmem, vmem],
        out_specs=(vmem, vmem),
    )(left, right)


def per_device(
    queries, cache_keys, cached_value_rows, new_keys, prompt_value_rows, cache_len, prompt_start
):
    width = lax.axis_size("ctx")
    me = lax.axis_index("ctx")
    core = me % CORES
    own_rows = queries.shape[0]
    bits = [CORES << i for i in range((width // CORES).bit_length() - 1)][::-1]
    orders = [bits, bits[-1:] + bits[:-1]]
    stages = len(bits)

    def swap(x):
        return lax.ppermute(x, "ctx", [(i, i ^ 1) for i in range(width)])

    def exchange(x, stage):
        return lax.ppermute(x, "ctx", [(i, i ^ orders[i % CORES][stage]) for i in range(width)])

    steps = [jnp.where(core == 0, a // CORES, b // CORES) for a, b in zip(*orders)]
    info = jnp.stack([core, me // CORES, me, prompt_start[0]] + steps).astype(I32)

    mine, other = pack(info, cache_len, queries, new_keys, prompt_value_rows)
    both = jnp.concatenate([mine, swap(other)], axis=0)
    keys_b, values_b = swap(cache_keys), swap(cached_value_rows)
    wide = queries.shape[1] // CORES + LANES
    held, fresh = both[:, :wide], both[:, wide:]
    for stage in range(stages - 1):
        held = jnp.concatenate([held, exchange(held, stage)], axis=0)
    far = exchange(held, stages - 1)
    run = functools.partial(attend, own_rows=own_rows, stages=stages)
    blocks = width // CORES // 2
    rest = (held, far, fresh, cache_keys, keys_b, cached_value_rows, values_b)
    sent = run(info, far, *rest, first_block=blocks)
    kept = run(info, held, *rest, first_block=0)
    for stage in reversed(range(stages)):
        kept, sent = merge(kept, exchange(sent, stage), stage == 0)
    theirs = swap(sent)
    pair = jnp.concatenate([kept, theirs], axis=1)
    flipped = jnp.concatenate([theirs, kept], axis=1)
    return jnp.where(core == 0, pair, flipped)


def solution(mesh):
    return jax.shard_map(
        per_device,
        mesh=mesh,
        in_specs=(
            P(("groups", "ctx"), None),
            P(("groups", "ctx"), None),
            P(("groups", "ctx"), None),
            P(("groups", "ctx"), None),
            P(("groups", "ctx"), None),
            P(("groups", "ctx")),
            P("groups"),
        ),
        out_specs=P(("groups", "ctx"), None),
        check_vma=False,
    )
```

```python
import functools
import math

import jax
import jax.numpy as jnp
from jax import lax
from jax.experimental import pallas as pl
from jax.experimental.pallas import tpu as pltpu
from jax.sharding import PartitionSpec as P

KEY_VALUE_HEADS = 4
LANES = 128
CORES = 2
FLOOR = -1e30
KEY_TILE = 256
STAT_ROWS = 16
CHUNK_BLOCKS = 4
STEP = 2.0**15
MARGIN = 0.9998
F32 = jnp.float32
BF16 = jnp.bfloat16
I16 = jnp.int16
I32 = jnp.int32
VMEM = pl.BlockSpec(memory_space=pltpu.VMEM)
SMEM = pl.BlockSpec(memory_space=pltpu.SMEM)
HBM = pl.BlockSpec(memory_space=pltpu.HBM)
SMALL = pltpu.CompilerParams(vmem_limit_bytes=8 << 20)


def encode(out, at, values, top, total):
    dims, width = values.shape
    largest = jnp.max(jnp.abs(values), axis=0, keepdims=True)
    exponent = jnp.floor(jnp.log2(jnp.maximum(largest, 1e-30))) + 1.0
    fixed = jnp.floor(values * (jnp.exp2(15.0 - exponent) * MARGIN) + 0.5)
    size = jnp.abs(top)
    level = jnp.zeros_like(top)
    scaled = top
    for i in range(1, 9):
        above = size >= STEP**i
        level = level + jnp.where(above, 1.0, 0.0)
        scaled = scaled * jnp.where(above, 1.0 / STEP, 1.0)
    a = jnp.floor(scaled)
    rest = (scaled - a) * STEP
    b = jnp.floor(rest)
    c = jnp.floor((rest - b) * STEP)
    logs = jnp.log2(total) * 1024.0
    la = jnp.floor(logs)
    lb = jnp.floor((logs - la) * STEP)
    row = lax.broadcasted_iota(I32, (STAT_ROWS, width), 0)
    stats = jnp.zeros((STAT_ROWS, width), F32)
    for i, part in enumerate((level, a, b, c, exponent, la, lb)):
        stats = jnp.where(row == i, part, stats)
    out[:dims, at : at + width] = fixed.astype(I32).astype(I16)
    out[dims:, at : at + width] = stats.astype(I32).astype(I16)


def decode_stats(ref, dims, at):
    stats = ref[dims:, at].astype(I32).astype(F32)

    def part(i):
        return stats[i : i + 1, :]

    top = part(1) + (part(2) + part(3) * (1.0 / STEP)) * (1.0 / STEP)
    for i in range(1, 9):
        top = top * jnp.where(part(0) >= i, STEP, 1.0)
    total = jnp.exp2((part(5) + part(6) * (1.0 / STEP)) * (1.0 / 1024.0))
    return top, total, jnp.exp2(part(4) - 15.0) * (1.0 / MARGIN)


def join_kernel(length, length_other, queries, queries_other, out):
    rows = queries.shape[0]
    half = queries.shape[1] // CORES
    core = lax.axis_index("ctx") % CORES
    at = pl.multiple_of(core * half, LANES)
    mine = queries[:, pl.ds(at, half)].astype(F32)
    other = queries_other[:, pl.ds(at, half)].astype(F32)
    out[:, :half] = jnp.concatenate([mine, other], axis=0).astype(BF16)
    lane = lax.broadcasted_iota(I32, (CORES * rows, LANES), 1)
    row = lax.broadcasted_iota(I32, (CORES * rows, LANES), 0)
    count = jnp.where(row < rows, length[0], length_other[0])
    coded = jnp.where(lane == 0, count // LANES, jnp.where(lane == 1, count % LANES, 0))
    out[:, half:] = coded.astype(F32).astype(BF16)


def join(length, length_other, queries, queries_other):
    rows, wide = queries.shape
    return pl.pallas_call(
        join_kernel,
        out_shape=jax.ShapeDtypeStruct((CORES * rows, wide // CORES + LANES), BF16),
        in_specs=[SMEM, SMEM, VMEM, VMEM],
        out_specs=VMEM,
        compiler_params=SMALL,
    )(length, length_other, queries, queries_other)


def attend_kernel(
    sizes, start, queries, low, high, fresh_keys_a, fresh_keys_b, fresh_values_a, fresh_values_b,
    keys_a, keys_b, values_a, values_b, out, query_t, scores, sums, kv, arrived
):
    own_rows, orders, first_block, group, kv_heads = sizes
    chip_rows = CORES * own_rows
    slots = keys_a.shape[0]
    tokens = queries.shape[0]
    blocks = tokens // chip_rows
    lanes = blocks * group * chip_rows
    me = lax.axis_index("ctx")
    core, chip = me % CORES, me // CORES
    factor = math.log2(math.e) / math.sqrt(LANES)
    chunk = pl.program_id(0)

    def copy(h, i):
        at = pl.multiple_of((core * kv_heads + h) * LANES, LANES)
        source = (keys_a, keys_b, values_a, values_b)[i]
        return pltpu.make_async_copy(source.at[:, pl.ds(at, LANES)], kv.at[h, i], arrived.at[h, i])

    @pl.when(chunk == 0)
    def _():
        for h in range(kv_heads):
            for i in range(4):
                copy(h, i).start()

    steps = [jnp.where(core == 0, a // CORES, b // CORES) for a, b in zip(*orders)]

    def origin(block):
        off = jnp.zeros_like(block)
        for i, step in enumerate(steps):
            off = off ^ jnp.where((block >> i) & 1 == 1, step, 0)
        return chip ^ off

    before, length = 0.0, [0.0, 0.0]
    base = 0
    for ref in (low, high):
        rows = ref.shape[0]
        lane = lax.broadcasted_iota(I32, (rows, LANES), 1)
        row = lax.broadcasted_iota(I32, (rows, LANES), 0)
        place = origin((row + base) // chip_rows)
        inside = row % chip_rows
        counts = jnp.where(lane == 0, float(LANES), 1.0) * ref[...].astype(F32)
        counts = jnp.where((inside % own_rows == 0) & (lane < 2), counts, 0.0)
        before = before + jnp.sum(jnp.where(place < chip, counts, 0.0))
        for s in range(2):
            length[s] = length[s] + jnp.sum(jnp.where((place == chip) & (inside // own_rows == s), counts, 0.0))
        base = base + rows
    length = [x.astype(I32) for x in length]
    before = before.astype(I32)
    begins = [
        before + jnp.where(core == 1, length[1], 0),
        before + jnp.where(core == 0, length[0], 0),
    ]
    limits = [jnp.clip(jnp.minimum(n, start[0] - at), 0, slots) for n, at in zip(length, begins)]

    key_row = lax.broadcasted_iota(I32, (chip_rows, lanes), 0)
    lane = lax.broadcasted_iota(I32, (chip_rows, lanes), 1)
    part = key_row // own_rows
    key_id = (chip * CORES + (core ^ part)) * own_rows + key_row % own_rows
    inside = lane % chip_rows
    block = lane // (group * chip_rows) + (first_block + chunk * blocks)
    token = (origin(block) * CORES + (core ^ (inside // own_rows))) * own_rows + inside % own_rows
    causal = key_id <= token
    key_slot = lax.broadcasted_iota(I32, (KEY_TILE, lanes), 0)
    nothing = jnp.zeros((16 - chip_rows % 16, LANES), F32)

    for h in range(kv_heads):
        first = h * group
        q = jnp.concatenate(
            [
                queries[b * chip_rows : (b + 1) * chip_rows, (first + g) * LANES : (first + g + 1) * LANES].astype(F32)
                for b in range(blocks)
                for g in range(group)
            ],
            axis=0,
        )
        query_t[...] = q.T.astype(BF16)
        at = pl.multiple_of((core * kv_heads + h) * LANES, LANES)

        def fresh(a, b):
            return jnp.concatenate([a[:, pl.ds(at, LANES)].astype(F32), b[:, pl.ds(at, LANES)].astype(F32), nothing], 0)

        new_keys = fresh(fresh_keys_a, fresh_keys_b).astype(BF16)
        new_values = fresh(fresh_values_a, fresh_values_b).astype(BF16)
        new_scores = jnp.dot(new_keys, query_t[...], preferred_element_type=F32)[:chip_rows] * factor

        @pl.when(chunk == 0)
        def _():
            for i in range(2):
                copy(h, i).wait()

        def fold(tile, combine):
            return combine(tile.reshape(KEY_TILE // 8, 8, lanes), axis=0)

        tops = []
        for s in range(2):
            limit = limits[s]
            whole = limit // KEY_TILE
            seen = causal & (part == s)
            peak = jnp.where(seen, new_scores, FLOOR)

            def score(j):
                at = pl.multiple_of(j * KEY_TILE, KEY_TILE)
                return jnp.dot(kv[h, s, pl.ds(at, KEY_TILE), :], query_t[...], preferred_element_type=F32) * factor

            def first_pass(j, peak):
                tile = score(j)
                scores[s, j] = tile
                return jnp.maximum(peak, fold(tile, jnp.max))

            peak = lax.fori_loop(0, whole, first_pass, peak)

            def last_tile(peak):
                tile = jnp.where(key_slot < limit - whole * KEY_TILE, score(whole), FLOOR)
                scores[s, whole] = tile
                return jnp.maximum(peak, fold(tile, jnp.max))

            peak = lax.cond(limit > whole * KEY_TILE, last_tile, lambda peak: peak, peak)
            tops.append(jnp.max(peak, axis=0, keepdims=True))

        @pl.when(chunk == 0)
        def _():
            for i in range(2, 4):
                copy(h, i).wait()

        masses = []
        for s in range(2):
            limit = limits[s]
            whole = limit // KEY_TILE
            seen = causal & (part == s)
            top = tops[s]
            weight = jnp.where(seen, jnp.exp2(new_scores - top), 0.0)
            padded = jnp.concatenate([weight, jnp.zeros((16 - chip_rows % 16, lanes), F32)], 0).astype(BF16)
            tn = (((0,), (0,)), ((), ()))
            sums[s] = lax.dot_general(new_values, padded, tn, preferred_element_type=F32)

            def add(j, weight):
                at = pl.multiple_of(j * KEY_TILE, KEY_TILE)
                sums[s] += lax.dot_general(
                    kv[h, 2 + s, pl.ds(at, KEY_TILE), :], weight.astype(BF16), tn, preferred_element_type=F32
                )

            def second_pass(j, mass):
                weight = jnp.exp2(scores[s, j] - top)
                add(j, weight)
                return mass + fold(weight, jnp.sum)

            mass = lax.fori_loop(0, whole, second_pass, weight)

            def last_tile(mass):
                weight = jnp.where(
                    key_slot < limit - whole * KEY_TILE, jnp.exp2(scores[s, whole] - top), 0.0
                )
                add(whole, weight)
                return mass + fold(weight, jnp.sum)

            mass = lax.cond(limit > whole * KEY_TILE, last_tile, lambda mass: mass, mass)
            masses.append(jnp.sum(mass, axis=0, keepdims=True))

        top = jnp.maximum(tops[0], tops[1])
        scale_a = jnp.exp2(tops[0] - top)
        scale_b = jnp.exp2(tops[1] - top)
        total = jnp.maximum(masses[0] * scale_a + masses[1] * scale_b, 1.0)
        merged = sums[0] * (scale_a / total) + sums[1] * (scale_b / total)
        width = group * chip_rows
        for b in range(blocks):
            cut = slice(b * width, (b + 1) * width)
            encode(out, (b * kv_heads + h) * width, merged[:, cut], top[:, cut], total[:, cut])


def attend(
    start, queries, low, high, fresh, cache, *, own_rows, orders, first_block
):
    count = queries.shape[0]
    chip_rows = CORES * own_rows
    tokens = min(count, CHUNK_BLOCKS * chip_rows)
    slots = cache[0].shape[0]
    kv_heads = cache[0].shape[1] // LANES // CORES
    heads = queries.shape[1] // LANES - 1
    group = heads // kv_heads
    lanes = tokens * group
    tiles = -(-slots // KEY_TILE)
    sizes = (own_rows, orders, first_block, group, kv_heads)
    return pl.pallas_call(
        functools.partial(attend_kernel, sizes),
        out_shape=jax.ShapeDtypeStruct((LANES + STAT_ROWS, count * heads), I16),
        grid=(count // tokens,),
        in_specs=[
            SMEM,
            pl.BlockSpec((tokens, heads * LANES), lambda i: (i, 0)),
            pl.BlockSpec((low.shape[0], LANES), lambda i: (0, heads)),
            pl.BlockSpec((high.shape[0], LANES), lambda i: (0, heads)),
            VMEM, VMEM, VMEM, VMEM,
            HBM, HBM, HBM, HBM,
        ],
        out_specs=pl.BlockSpec((LANES + STAT_ROWS, tokens * heads), lambda i: (0, i)),
        scratch_shapes=[
            pltpu.VMEM((LANES, lanes), BF16),
            pltpu.VMEM((2, tiles, KEY_TILE, lanes), F32),
            pltpu.VMEM((2, LANES, lanes), F32),
            pltpu.VMEM((kv_heads, 4, tiles * KEY_TILE, LANES), BF16),
            pltpu.SemaphoreType.DMA((kv_heads, 4)),
        ],
        compiler_params=pltpu.CompilerParams(vmem_limit_bytes=32 << 20),
    )(start, queries, low, high, *fresh, *cache)


def merged_part(left, right, dims, at):
    top_a, total_a, unit_a = decode_stats(left, dims, at)
    top_b, total_b, unit_b = decode_stats(right, dims, at)
    top = jnp.maximum(top_a, top_b)
    mass_a = total_a * jnp.exp2(top_a - top)
    mass_b = total_b * jnp.exp2(top_b - top)
    total = mass_a + mass_b
    values = left[:dims, at].astype(I32).astype(F32) * (mass_a / total * unit_a)
    values = values + right[:dims, at].astype(I32).astype(F32) * (mass_b / total * unit_b)
    return values, top, total


def merge_kernel(left, right, kept, sent):
    dims = left.shape[0] - STAT_ROWS
    half = kept.shape[1]
    step = min(half, 2 * LANES)
    for out, base in ((sent, half), (kept, 0)):
        for at in range(0, half, step):
            encode(out, at, *merged_part(left, right, dims, slice(base + at, base + at + step)))


def merge(left, right):
    rows, width = left.shape
    shape = jax.ShapeDtypeStruct((rows, width // 2), I16)
    return pl.pallas_call(
        merge_kernel,
        out_shape=(shape, shape),
        in_specs=[VMEM, VMEM],
        out_specs=(VMEM, VMEM),
        compiler_params=SMALL,
    )(left, right)


def finish_kernel(group, left, right, mine, other):
    dims = left.shape[0] - STAT_ROWS
    own_rows = mine.shape[0]
    chip_rows = CORES * own_rows
    width = group * chip_rows
    for h in range(left.shape[1] // width):
        values, _, _ = merged_part(left, right, dims, slice(h * width, (h + 1) * width))
        rows = values.T
        for g in range(group):
            at = (h * group + g) * dims
            tokens = rows[g * chip_rows : (g + 1) * chip_rows]
            mine[:, at : at + dims] = tokens[:own_rows].astype(BF16)
            other[:, at : at + dims] = tokens[own_rows:].astype(BF16)


def finish(left, right, own_rows, group):
    dims = left.shape[0] - STAT_ROWS
    shape = jax.ShapeDtypeStruct((own_rows, left.shape[1] // (CORES * own_rows) * dims), BF16)
    return pl.pallas_call(
        functools.partial(finish_kernel, group),
        out_shape=(shape, shape),
        in_specs=[VMEM, VMEM],
        out_specs=(VMEM, VMEM),
        compiler_params=SMALL,
    )(left, right)


def place_kernel(mine, theirs, out):
    half = mine.shape[1]
    core = lax.axis_index("ctx") % CORES
    out[:, pl.ds(pl.multiple_of(core * half, LANES), half)] = mine[...]
    out[:, pl.ds(pl.multiple_of((1 - core) * half, LANES), half)] = theirs[...]


def place(mine, theirs):
    rows, half = mine.shape
    return pl.pallas_call(
        place_kernel,
        out_shape=jax.ShapeDtypeStruct((rows, CORES * half), BF16),
        in_specs=[VMEM, VMEM],
        out_specs=VMEM,
        compiler_params=SMALL,
    )(mine, theirs)


def per_device(
    queries, cache_keys, cached_value_rows, new_keys, prompt_value_rows, cache_len, prompt_start
):
    width = lax.axis_size("ctx")
    own_rows = queries.shape[0]
    group = queries.shape[1] // cache_keys.shape[1]
    bits = [CORES << i for i in range((width // CORES).bit_length() - 1)][::-1]
    orders = (tuple(bits), tuple(bits[-1:] + bits[:-1]))
    stages = len(bits)

    def swap(x):
        return lax.ppermute(x, "ctx", [(i, i ^ 1) for i in range(width)])

    def exchange(x, stage):
        return lax.ppermute(x, "ctx", [(i, i ^ orders[i % CORES][stage]) for i in range(width)])

    held = join(cache_len, swap(cache_len), queries, swap(queries))
    fresh = (new_keys, swap(new_keys), prompt_value_rows, swap(prompt_value_rows))
    cache = (cache_keys, swap(cache_keys), cached_value_rows, swap(cached_value_rows))
    for stage in range(stages - 1):
        held = jnp.concatenate([held, exchange(held, stage)], axis=0)
    far = exchange(held, stages - 1)
    run = functools.partial(attend, own_rows=own_rows, orders=orders)
    sent = run(prompt_start, far, held, far, fresh, cache, first_block=width // CORES // 2)
    kept = run(prompt_start, held, held, far, fresh, cache, first_block=0)
    for stage in reversed(range(1, stages)):
        kept, sent = merge(kept, exchange(sent, stage))
    mine, other = finish(kept, exchange(sent, 0), own_rows, group)
    return place(mine, swap(other))


def solution(mesh):
    return jax.shard_map(
        per_device,
        mesh=mesh,
        in_specs=(
            P(("groups", "ctx"), None),
            P(("groups", "ctx"), None),
            P(("groups", "ctx"), None),
            P(("groups", "ctx"), None),
            P(("groups", "ctx"), None),
            P(("groups", "ctx")),
            P("groups"),
        ),
        out_specs=P(("groups", "ctx"), None),
        check_vma=False,
    )
```

```python
import functools
import math

import jax
import jax.numpy as jnp
from jax import lax
from jax.experimental import pallas as pl
from jax.experimental.pallas import tpu as pltpu
from jax.sharding import PartitionSpec as P

KEY_VALUE_HEADS = 4
LANES = 128
CORES = 2
FLOOR = -1e30
TILES = (1024, 512)
TAIL = 256
STAT_ROWS = 16
CHUNK_BLOCKS = 4
STEP = 2.0**15
MARGIN = 0.9998
F32 = jnp.float32
BF16 = jnp.bfloat16
I16 = jnp.int16
I32 = jnp.int32
VMEM = pl.BlockSpec(memory_space=pltpu.VMEM)
SMEM = pl.BlockSpec(memory_space=pltpu.SMEM)
HBM = pl.BlockSpec(memory_space=pltpu.HBM)
ANY = pl.BlockSpec(memory_space=pl.ANY)
SMALL = pltpu.CompilerParams(vmem_limit_bytes=8 << 20)


def encode(out, at, values, top, total):
    dims, width = values.shape
    largest = jnp.max(jnp.abs(values), axis=0, keepdims=True)
    exponent = jnp.floor(jnp.log2(jnp.maximum(largest, 1e-30))) + 1.0
    fixed = jnp.floor(values * (jnp.exp2(15.0 - exponent) * MARGIN) + 0.5)
    size = jnp.abs(top)
    level = jnp.zeros_like(top)
    scaled = top
    for i in range(1, 9):
        above = size >= STEP**i
        level = level + jnp.where(above, 1.0, 0.0)
        scaled = scaled * jnp.where(above, 1.0 / STEP, 1.0)
    a = jnp.floor(scaled)
    rest = (scaled - a) * STEP
    b = jnp.floor(rest)
    c = jnp.floor((rest - b) * STEP)
    logs = jnp.log2(total) * 1024.0
    la = jnp.floor(logs)
    lb = jnp.floor((logs - la) * STEP)
    row = lax.broadcasted_iota(I32, (STAT_ROWS, width), 0)
    stats = jnp.zeros((STAT_ROWS, width), F32)
    for i, part in enumerate((level, a, b, c, exponent, la, lb)):
        stats = jnp.where(row == i, part, stats)
    out[:dims, at : at + width] = fixed.astype(I32).astype(I16)
    out[dims:, at : at + width] = stats.astype(I32).astype(I16)


def decode_stats(ref, dims, at):
    stats = ref[dims:, at].astype(I32).astype(F32)

    def part(i):
        return stats[i : i + 1, :]

    top = part(1) + (part(2) + part(3) * (1.0 / STEP)) * (1.0 / STEP)
    for i in range(1, 9):
        top = top * jnp.where(part(0) >= i, STEP, 1.0)
    total = jnp.exp2((part(5) + part(6) * (1.0 / STEP)) * (1.0 / 1024.0))
    return top, total, jnp.exp2(part(4) - 15.0) * (1.0 / MARGIN)


def join_kernel(length, length_other, queries, queries_other, out, mine, other, arrived):
    rows, half = mine.shape
    core = lax.axis_index("ctx") % CORES
    at = pl.multiple_of(core * half, LANES)
    copies = [
        pltpu.make_async_copy(source.at[:, pl.ds(at, half)], target, arrived.at[i])
        for i, (source, target) in enumerate(((queries, mine), (queries_other, other)))
    ]
    for copy in copies:
        copy.start()
    lane = lax.broadcasted_iota(I32, (CORES * rows, LANES), 1)
    row = lax.broadcasted_iota(I32, (CORES * rows, LANES), 0)
    count = jnp.where(row < rows, length[0], length_other[0])
    coded = jnp.where(lane == 0, count // LANES, jnp.where(lane == 1, count % LANES, 0))
    out[:, half:] = coded.astype(F32).astype(BF16)
    for copy in copies:
        copy.wait()
    out[:, :half] = jnp.concatenate([mine[...].astype(F32), other[...].astype(F32)], axis=0).astype(BF16)


def join(length, length_other, queries, queries_other):
    rows, wide = queries.shape
    return pl.pallas_call(
        join_kernel,
        out_shape=jax.ShapeDtypeStruct((CORES * rows, wide // CORES + LANES), BF16),
        in_specs=[SMEM, SMEM, HBM, ANY],
        out_specs=VMEM,
        scratch_shapes=[
            pltpu.VMEM((rows, wide // CORES), BF16),
            pltpu.VMEM((rows, wide // CORES), BF16),
            pltpu.SemaphoreType.DMA((2,)),
        ],
        compiler_params=SMALL,
    )(length, length_other, queries, queries_other)


def attend_kernel(
    sizes, start, queries, low, high, new_keys_a, new_keys_b, new_values_a, new_values_b,
    keys_a, keys_b, values_a, values_b, out, query_t, scores, sums, tops, totals, fresh, kv, fresh_arrived, arrived
):
    own_rows, orders, first_block, group, kv_heads = sizes
    chip_rows = CORES * own_rows
    slots = keys_a.shape[0]
    tokens = queries.shape[0]
    blocks = tokens // chip_rows
    lanes = blocks * group * chip_rows
    me = lax.axis_index("ctx")
    core, chip = me % CORES, me // CORES
    factor = math.log2(math.e) / math.sqrt(LANES)
    chunk = pl.program_id(0)

    def copy(h, i):
        at = pl.multiple_of((core * kv_heads + h) * LANES, LANES)
        source = (keys_a, keys_b, values_a, values_b)[i]
        return pltpu.make_async_copy(source.at[:, pl.ds(at, LANES)], kv.at[h, i], arrived.at[h, i])

    fresh_copies = [
        pltpu.make_async_copy(source, fresh.at[i], fresh_arrived.at[i])
        for i, source in enumerate((new_keys_a, new_keys_b, new_values_a, new_values_b))
    ]

    @pl.when(chunk == 0)
    def _():
        for fresh_copy in fresh_copies:
            fresh_copy.start()
        for h in range(kv_heads):
            for i in range(4):
                copy(h, i).start()

    steps = [jnp.where(core == 0, a // CORES, b // CORES) for a, b in zip(*orders)]

    def origin(block):
        off = jnp.zeros_like(block)
        for i, step in enumerate(steps):
            off = off ^ jnp.where((block >> i) & 1 == 1, step, 0)
        return chip ^ off

    before, length = 0.0, [0.0, 0.0]
    base = 0
    for ref in (low, high):
        rows = ref.shape[0]
        lane = lax.broadcasted_iota(I32, (rows, LANES), 1)
        row = lax.broadcasted_iota(I32, (rows, LANES), 0)
        place = origin((row + base) // chip_rows)
        inside = row % chip_rows
        counts = jnp.where(lane == 0, float(LANES), 1.0) * ref[...].astype(F32)
        counts = jnp.where((inside % own_rows == 0) & (lane < 2), counts, 0.0)
        before = before + jnp.sum(jnp.where(place < chip, counts, 0.0))
        for s in range(2):
            length[s] = length[s] + jnp.sum(jnp.where((place == chip) & (inside // own_rows == s), counts, 0.0))
        base = base + rows
    length = [x.astype(I32) for x in length]
    before = before.astype(I32)
    begins = [
        before + jnp.where(core == 1, length[1], 0),
        before + jnp.where(core == 0, length[0], 0),
    ]
    limits = [jnp.clip(jnp.minimum(n, start[0] - at), 0, slots) for n, at in zip(length, begins)]

    key_row = lax.broadcasted_iota(I32, (chip_rows, lanes), 0)
    lane = lax.broadcasted_iota(I32, (chip_rows, lanes), 1)
    part = key_row // own_rows
    key_id = (chip * CORES + (core ^ part)) * own_rows + key_row % own_rows
    inside = lane % chip_rows
    block = lane // (group * chip_rows) + (first_block + chunk * blocks)
    token = (origin(block) * CORES + (core ^ (inside // own_rows))) * own_rows + inside % own_rows
    causal = key_id <= token
    nothing = jnp.zeros((16 - chip_rows % 16, LANES), F32)
    heads = range(kv_heads)
    fresh_scores, fresh_values = [], []

    @pl.when(chunk == 0)
    def _():
        for fresh_copy in fresh_copies:
            fresh_copy.wait()

    for h in heads:
        first = h * group
        q = jnp.concatenate(
            [
                queries[b * chip_rows : (b + 1) * chip_rows, (first + g) * LANES : (first + g + 1) * LANES].astype(F32)
                for b in range(blocks)
                for g in range(group)
            ],
            axis=0,
        )
        query_t[h] = q.T.astype(BF16)
        at = pl.multiple_of((core * kv_heads + h) * LANES, LANES)

        def both(i):
            rows = [fresh[i + s, :, pl.ds(at, LANES)].astype(F32) for s in range(2)]
            return jnp.concatenate(rows + [nothing], 0).astype(BF16)

        new_keys = both(0)
        fresh_values.append(both(2))
        fresh_scores.append(jnp.dot(new_keys, query_t[h], preferred_element_type=F32)[:chip_rows] * factor)

    @pl.when(chunk == 0)
    def _():
        for h in heads:
            for i in range(4):
                copy(h, i).wait()

    def fold(tile, combine):
        return combine(tile.reshape(tile.shape[0] // 8, 8, lanes), axis=0)

    def each_tile(limit, body, carry):
        base, rest = 0, limit
        for rows in TILES:
            count = rest // rows

            def whole(j, carry, rows=rows, base=base):
                return body(pl.multiple_of(base + j * rows, TILES[-1]), rows, None, carry)

            carry = lax.fori_loop(0, count, whole, carry)
            base, rest = base + count * rows, rest - count * rows
        base = pl.multiple_of(base, TILES[-1])
        for rows, need in ((TAIL, (rest > 0) & (rest <= TAIL)), (TILES[-1], rest > TAIL)):
            carry = lax.cond(need, lambda c, rows=rows: body(base, rows, rest, c), lambda c: c, carry)
        return carry

    tn = (((0,), (0,)), ((), ()))

    def shard(s, carry):
        limit = jnp.where(s == 0, limits[0], limits[1])
        seen = causal & (part == s)

        def first_pass(base, rows, filled, peaks):
            higher = []
            for h in heads:
                tile = jnp.dot(kv[h, s, pl.ds(base, rows), :], query_t[h], preferred_element_type=F32) * factor
                if filled is not None:
                    tile = jnp.where(lax.broadcasted_iota(I32, (rows, lanes), 0) < filled, tile, FLOOR)
                scores[h, pl.ds(base, rows), :] = tile
                higher.append(jnp.maximum(peaks[h], fold(tile, jnp.max)))
            return tuple(higher)

        peaks = each_tile(limit, first_pass, tuple(jnp.where(seen, x, FLOOR) for x in fresh_scores))
        top = [jnp.max(x, axis=0, keepdims=True) for x in peaks]
        masses = []
        for h in heads:
            weight = jnp.where(seen, jnp.exp2(fresh_scores[h] - top[h]), 0.0)
            padded = jnp.concatenate([weight, jnp.zeros((16 - chip_rows % 16, lanes), F32)], 0).astype(BF16)
            sums[s, h] = lax.dot_general(fresh_values[h], padded, tn, preferred_element_type=F32)
            masses.append(weight)

        def second_pass(base, rows, filled, masses):
            more = []
            for h in heads:
                weight = jnp.exp2(scores[h, pl.ds(base, rows), :] - top[h])
                if filled is not None:
                    weight = jnp.where(lax.broadcasted_iota(I32, (rows, lanes), 0) < filled, weight, 0.0)
                sums[s, h] += lax.dot_general(
                    kv[h, 2 + s, pl.ds(base, rows), :], weight.astype(BF16), tn, preferred_element_type=F32
                )
                more.append(masses[h] + fold(weight, jnp.sum))
            return tuple(more)

        masses = each_tile(limit, second_pass, tuple(masses))
        for h in heads:
            tops[s, h] = top[h]
            totals[s, h] = jnp.sum(masses[h], axis=0, keepdims=True)
        return carry

    lax.fori_loop(0, 2, shard, 0)
    for h in heads:
        top_a, top_b = tops[0, h], tops[1, h]
        top = jnp.maximum(top_a, top_b)
        scale_a = jnp.exp2(top_a - top)
        scale_b = jnp.exp2(top_b - top)
        total = jnp.maximum(totals[0, h] * scale_a + totals[1, h] * scale_b, 1.0)
        merged = sums[0, h] * (scale_a / total) + sums[1, h] * (scale_b / total)
        width = group * chip_rows
        for b in range(blocks):
            cut = slice(b * width, (b + 1) * width)
            encode(out, (b * kv_heads + h) * width, merged[:, cut], top[:, cut], total[:, cut])


def attend(
    start, queries, low, high, fresh, cache, *, own_rows, orders, first_block
):
    count = queries.shape[0]
    chip_rows = CORES * own_rows
    tokens = min(count, CHUNK_BLOCKS * chip_rows)
    slots = cache[0].shape[0]
    kv_heads = cache[0].shape[1] // LANES // CORES
    heads = queries.shape[1] // LANES - 1
    group = heads // kv_heads
    lanes = tokens * group
    padded = -(-slots // TILES[-1]) * TILES[-1]
    sizes = (own_rows, orders, first_block, group, kv_heads)
    return pl.pallas_call(
        functools.partial(attend_kernel, sizes),
        out_shape=jax.ShapeDtypeStruct((LANES + STAT_ROWS, count * heads), I16),
        grid=(count // tokens,),
        in_specs=[
            SMEM,
            pl.BlockSpec((tokens, heads * LANES), lambda i: (i, 0)),
            pl.BlockSpec((low.shape[0], LANES), lambda i: (0, heads)),
            pl.BlockSpec((high.shape[0], LANES), lambda i: (0, heads)),
            HBM, ANY, HBM, ANY,
            HBM, ANY, HBM, ANY,
        ],
        out_specs=pl.BlockSpec((LANES + STAT_ROWS, tokens * heads), lambda i: (0, i)),
        scratch_shapes=[
            pltpu.VMEM((kv_heads, LANES, lanes), BF16),
            pltpu.VMEM((kv_heads, padded, lanes), F32),
            pltpu.VMEM((2, kv_heads, LANES, lanes), F32),
            pltpu.VMEM((2, kv_heads, 1, lanes), F32),
            pltpu.VMEM((2, kv_heads, 1, lanes), F32),
            pltpu.VMEM((4,) + fresh[0].shape, BF16),
            pltpu.VMEM((kv_heads, 4, padded, LANES), BF16),
            pltpu.SemaphoreType.DMA((4,)),
            pltpu.SemaphoreType.DMA((kv_heads, 4)),
        ],
        compiler_params=pltpu.CompilerParams(vmem_limit_bytes=32 << 20),
    )(start, queries, low, high, *fresh, *cache)


def merged_part(left, right, dims, at):
    top_a, total_a, unit_a = decode_stats(left, dims, at)
    top_b, total_b, unit_b = decode_stats(right, dims, at)
    top = jnp.maximum(top_a, top_b)
    mass_a = total_a * jnp.exp2(top_a - top)
    mass_b = total_b * jnp.exp2(top_b - top)
    total = mass_a + mass_b
    values = left[:dims, at].astype(I32).astype(F32) * (mass_a / total * unit_a)
    values = values + right[:dims, at].astype(I32).astype(F32) * (mass_b / total * unit_b)
    return values, top, total


def merge_kernel(left, right, kept, sent):
    dims = left.shape[0] - STAT_ROWS
    half = kept.shape[1]
    step = min(half, 2 * LANES)
    for out, base in ((sent, half), (kept, 0)):
        for at in range(0, half, step):
            encode(out, at, *merged_part(left, right, dims, slice(base + at, base + at + step)))


def merge(left, right):
    rows, width = left.shape
    shape = jax.ShapeDtypeStruct((rows, width // 2), I16)
    return pl.pallas_call(
        merge_kernel,
        out_shape=(shape, shape),
        in_specs=[VMEM, VMEM],
        out_specs=(VMEM, VMEM),
        compiler_params=SMALL,
    )(left, right)


def finish_kernel(group, left, right, mine, other):
    dims = left.shape[0] - STAT_ROWS
    own_rows = mine.shape[0]
    chip_rows = CORES * own_rows
    width = group * chip_rows
    for h in range(left.shape[1] // width):
        values, _, _ = merged_part(left, right, dims, slice(h * width, (h + 1) * width))
        rows = values.T
        for g in range(group):
            at = (h * group + g) * dims
            tokens = rows[g * chip_rows : (g + 1) * chip_rows]
            mine[:, at : at + dims] = tokens[:own_rows].astype(BF16)
            other[:, at : at + dims] = tokens[own_rows:].astype(BF16)


def finish(left, right, own_rows, group):
    dims = left.shape[0] - STAT_ROWS
    shape = jax.ShapeDtypeStruct((own_rows, left.shape[1] // (CORES * own_rows) * dims), BF16)
    return pl.pallas_call(
        functools.partial(finish_kernel, group),
        out_shape=(shape, shape),
        in_specs=[VMEM, VMEM],
        out_specs=(VMEM, VMEM),
        compiler_params=SMALL,
    )(left, right)


def place_kernel(mine, theirs, out):
    half = mine.shape[1]
    core = lax.axis_index("ctx") % CORES
    out[:, pl.ds(pl.multiple_of(core * half, LANES), half)] = mine[...]
    out[:, pl.ds(pl.multiple_of((1 - core) * half, LANES), half)] = theirs[...]


def place(mine, theirs):
    rows, half = mine.shape
    return pl.pallas_call(
        place_kernel,
        out_shape=jax.ShapeDtypeStruct((rows, CORES * half), BF16),
        in_specs=[VMEM, VMEM],
        out_specs=VMEM,
        compiler_params=SMALL,
    )(mine, theirs)


def per_device(
    queries, cache_keys, cached_value_rows, new_keys, prompt_value_rows, cache_len, prompt_start
):
    width = lax.axis_size("ctx")
    own_rows = queries.shape[0]
    group = queries.shape[1] // cache_keys.shape[1]
    bits = [CORES << i for i in range((width // CORES).bit_length() - 1)][::-1]
    orders = (tuple(bits), tuple(bits[-1:] + bits[:-1]))
    stages = len(bits)

    def swap(x):
        return lax.ppermute(x, "ctx", [(i, i ^ 1) for i in range(width)])

    def exchange(x, stage):
        return lax.ppermute(x, "ctx", [(i, i ^ orders[i % CORES][stage]) for i in range(width)])

    held = join(cache_len, swap(cache_len), queries, swap(queries))
    fresh = (new_keys, swap(new_keys), prompt_value_rows, swap(prompt_value_rows))
    cache = (cache_keys, swap(cache_keys), cached_value_rows, swap(cached_value_rows))
    for stage in range(stages - 1):
        held = jnp.concatenate([held, exchange(held, stage)], axis=0)
    far = exchange(held, stages - 1)
    run = functools.partial(attend, own_rows=own_rows, orders=orders)
    sent = run(prompt_start, far, held, far, fresh, cache, first_block=width // CORES // 2)
    kept = run(prompt_start, held, held, far, fresh, cache, first_block=0)
    for stage in reversed(range(1, stages)):
        kept, sent = merge(kept, exchange(sent, stage))
    mine, other = finish(kept, exchange(sent, 0), own_rows, group)
    return place(mine, swap(other))


def solution(mesh):
    return jax.shard_map(
        per_device,
        mesh=mesh,
        in_specs=(
            P(("groups", "ctx"), None),
            P(("groups", "ctx"), None),
            P(("groups", "ctx"), None),
            P(("groups", "ctx"), None),
            P(("groups", "ctx"), None),
            P(("groups", "ctx")),
            P("groups"),
        ),
        out_specs=P(("groups", "ctx"), None),
        check_vma=False,
    )
```

```python
import functools
import math

import jax
import jax.numpy as jnp
from jax import lax
from jax.experimental import pallas as pl
from jax.experimental.pallas import tpu as pltpu
from jax.sharding import PartitionSpec as P

KEY_VALUE_HEADS = 4
LANES = 128
CORES = 2
FLOOR = -1e30
TILES = (512,)
TAIL = 256
ATTEND_BYTES = 32 << 20
STAT_ROWS = 16
CHUNK_BLOCKS = 2
STEP = 2.0**15
MARGIN = 0.9998
F32 = jnp.float32
BF16 = jnp.bfloat16
I16 = jnp.int16
I32 = jnp.int32
VMEM = pl.BlockSpec(memory_space=pltpu.VMEM)
SMEM = pl.BlockSpec(memory_space=pltpu.SMEM)
ANY = pl.BlockSpec(memory_space=pl.ANY)
SMALL = pltpu.CompilerParams(vmem_limit_bytes=8 << 20)


def encode(out, at, values, top, total):
    dims, width = values.shape
    largest = jnp.max(jnp.abs(values), axis=0, keepdims=True)
    exponent = jnp.floor(jnp.log2(jnp.maximum(largest, 1e-30))) + 1.0
    fixed = jnp.floor(values * (jnp.exp2(15.0 - exponent) * MARGIN) + 0.5)
    size = jnp.abs(top)
    level = jnp.zeros_like(top)
    scaled = top
    for i in range(1, 9):
        above = size >= STEP**i
        level = level + jnp.where(above, 1.0, 0.0)
        scaled = scaled * jnp.where(above, 1.0 / STEP, 1.0)
    a = jnp.floor(scaled)
    rest = (scaled - a) * STEP
    b = jnp.floor(rest)
    c = jnp.floor((rest - b) * STEP)
    logs = jnp.log2(total) * 1024.0
    la = jnp.floor(logs)
    lb = jnp.floor((logs - la) * STEP)
    row = lax.broadcasted_iota(I32, (STAT_ROWS, width), 0)
    stats = jnp.zeros((STAT_ROWS, width), F32)
    for i, part in enumerate((level, a, b, c, exponent, la, lb)):
        stats = jnp.where(row == i, part, stats)
    out[:dims, at : at + width] = fixed.astype(I32).astype(I16)
    out[dims:, at : at + width] = stats.astype(I32).astype(I16)


def decode_stats(ref, dims, at):
    stats = ref[dims:, at].astype(I32).astype(F32)

    def part(i):
        return stats[i : i + 1, :]

    top = part(1) + (part(2) + part(3) * (1.0 / STEP)) * (1.0 / STEP)
    for i in range(1, 9):
        top = top * jnp.where(part(0) >= i, STEP, 1.0)
    total = jnp.exp2((part(5) + part(6) * (1.0 / STEP)) * (1.0 / 1024.0))
    return top, total, jnp.exp2(part(4) - 15.0) * (1.0 / MARGIN)


def join_kernel(length, length_other, mine, queries_other, out):
    rows, half = mine.shape
    core = lax.axis_index("ctx") % CORES
    other = queries_other[:, pl.ds(pl.multiple_of(core * half, LANES), half)]
    out[:, :half] = jnp.concatenate([mine[...].astype(F32), other.astype(F32)], axis=0).astype(BF16)
    lane = lax.broadcasted_iota(I32, (CORES * rows, LANES), 1)
    row = lax.broadcasted_iota(I32, (CORES * rows, LANES), 0)
    count = jnp.where(row < rows, length[0], length_other[0])
    coded = jnp.where(lane == 0, count // LANES, jnp.where(lane == 1, count % LANES, 0))
    out[:, half:] = coded.astype(F32).astype(BF16)


def join(length, length_other, mine, queries_other):
    rows, half = mine.shape
    return pl.pallas_call(
        join_kernel,
        out_shape=jax.ShapeDtypeStruct((CORES * rows, half + LANES), BF16),
        in_specs=[SMEM, SMEM, VMEM, VMEM],
        out_specs=VMEM,
        compiler_params=SMALL,
    )(length, length_other, mine, queries_other)


def attend_kernel(sizes, *refs):
    own_rows, orders, group, kv_heads, sets = sizes
    start = refs[0]
    queries, extras = refs[1 : 1 + sets], refs[1 + sets : 1 + 2 * sets]
    rest = refs[1 + 2 * sets :]
    new_keys, new_values, keys_a, keys_b, values_a, values_b = rest[:6]
    outs = rest[6 : 6 + sets]
    query_t, scores, sums, tops, totals, kv, arrived = rest[6 + sets :]
    chip_rows = CORES * own_rows
    slots = keys_a.shape[0]
    tokens = queries[0].shape[0]
    blocks = tokens // chip_rows
    set_blocks = extras[0].shape[0] // chip_rows
    set_lanes = tokens * group
    lanes = sets * set_lanes
    me = lax.axis_index("ctx")
    core, chip = me % CORES, me // CORES
    factor = math.log2(math.e) / math.sqrt(LANES)
    chunk = pl.program_id(0)

    def copy(h, i):
        own = i % 2 == 0
        at = pl.multiple_of((0 if own else core * kv_heads * LANES) + h * LANES, LANES)
        source = (keys_a, keys_b, values_a, values_b)[i]
        return pltpu.make_async_copy(source.at[:, pl.ds(at, LANES)], kv.at[h, i], arrived.at[h, i])

    @pl.when(chunk == 0)
    def _():
        for h in range(kv_heads):
            for i in range(4):
                copy(h, i).start()

    steps = [jnp.where(core == 0, a // CORES, b // CORES) for a, b in zip(*orders)]

    def origin(block):
        off = jnp.zeros_like(block)
        for i, step in enumerate(steps):
            off = off ^ jnp.where((block >> i) & 1 == 1, step, 0)
        return chip ^ off

    found = [0.0, 0.0, 0.0]
    for i, ref in enumerate(extras):
        rows = ref.shape[0]
        lane = lax.broadcasted_iota(I32, (rows, LANES), 1)
        row = lax.broadcasted_iota(I32, (rows, LANES), 0)
        place = origin(row // chip_rows + i * set_blocks)
        inside = row % chip_rows
        counts = jnp.where(lane == 0, float(LANES), 1.0) * ref[...].astype(F32)
        counts = jnp.where((inside % own_rows == 0) & (lane < 2), counts, 0.0)
        here = place == chip
        second = inside >= own_rows
        for k, chosen in enumerate((place < chip, here & ~second, here & second)):
            found[k] = found[k] + jnp.sum(jnp.where(chosen, counts, 0.0), axis=0, keepdims=True)
    row = lax.broadcasted_iota(I32, (8, LANES), 0)
    found = jnp.where(row == 0, found[0], jnp.where(row == 1, found[1], found[2]))
    found = jnp.sum(found, axis=1, keepdims=True).astype(I32)
    before, length = found[0, 0], [found[1, 0], found[2, 0]]
    begins = [
        before + jnp.where(core == 1, length[1], 0),
        before + jnp.where(core == 0, length[0], 0),
    ]
    limits = [jnp.clip(jnp.minimum(n, start[0] - at), 0, slots) for n, at in zip(length, begins)]

    key_row = lax.broadcasted_iota(I32, (chip_rows, lanes), 0)
    lane = lax.broadcasted_iota(I32, (chip_rows, lanes), 1)
    part = key_row // own_rows
    key_id = (chip * CORES + (core ^ part)) * own_rows + key_row % own_rows
    inside = lane % chip_rows
    block = lane // set_lanes * set_blocks + lane % set_lanes // (group * chip_rows) + chunk * blocks
    token = (origin(block) * CORES + (core ^ (inside // own_rows))) * own_rows + inside % own_rows
    causal = key_id <= token
    nothing = jnp.zeros((16 - chip_rows % 16, LANES), F32)
    heads = range(kv_heads)
    fresh_scores, fresh_values = [], []

    for h in heads:
        first = h * group
        q = jnp.concatenate(
            [
                ref[b * chip_rows : (b + 1) * chip_rows, (first + g) * LANES : (first + g + 1) * LANES].astype(F32)
                for ref in queries
                for b in range(blocks)
                for g in range(group)
            ],
            axis=0,
        )
        query_t[h] = q.T.astype(BF16)
        at = pl.multiple_of((core * kv_heads + h) * LANES, LANES)

        def padded_rows(ref):
            return jnp.concatenate([ref[:, pl.ds(at, LANES)].astype(F32), nothing], 0).astype(BF16)

        fresh_values.append(padded_rows(new_values))
        fresh_scores.append(jnp.dot(padded_rows(new_keys), query_t[h], preferred_element_type=F32)[:chip_rows] * factor)

    @pl.when(chunk == 0)
    def _():
        for h in heads:
            for i in range(4):
                copy(h, i).wait()

    def fold(tile, combine):
        return combine(tile.reshape(tile.shape[0] // 8, 8, lanes), axis=0)

    def each_tile(limit, body, carry):
        base, rest = 0, limit
        for rows in TILES:
            count = rest // rows

            def whole(j, carry, rows=rows, base=base):
                return body(pl.multiple_of(base + j * rows, TILES[-1]), rows, None, carry)

            carry = lax.fori_loop(0, count, whole, carry)
            base, rest = base + count * rows, rest - count * rows
        base = pl.multiple_of(base, TILES[-1])
        for rows, need in ((TAIL, (rest > 0) & (rest <= TAIL)), (TILES[-1], rest > TAIL)):
            carry = lax.cond(need, lambda c, rows=rows: body(base, rows, rest, c), lambda c: c, carry)
        return carry

    tn = (((0,), (0,)), ((), ()))

    def shard(s, carry):
        limit = jnp.where(s == 0, limits[0], limits[1])
        seen = causal & (part == s)

        def first_pass(base, rows, filled, peaks):
            higher = []
            for h in heads:
                tile = jnp.dot(kv[h, s, pl.ds(base, rows), :], query_t[h], preferred_element_type=F32) * factor
                if filled is not None:
                    tile = jnp.where(lax.broadcasted_iota(I32, (rows, lanes), 0) < filled, tile, FLOOR)
                scores[h, pl.ds(base, rows), :] = tile
                higher.append(jnp.maximum(peaks[h], fold(tile, jnp.max)))
            return tuple(higher)

        peaks = each_tile(limit, first_pass, tuple(jnp.where(seen, x, FLOOR) for x in fresh_scores))
        top = [jnp.max(x, axis=0, keepdims=True) for x in peaks]
        masses = []
        for h in heads:
            weight = jnp.where(seen, jnp.exp2(fresh_scores[h] - top[h]), 0.0)
            padded = jnp.concatenate([weight, jnp.zeros((16 - chip_rows % 16, lanes), F32)], 0).astype(BF16)
            sums[s, h] = lax.dot_general(fresh_values[h], padded, tn, preferred_element_type=F32)
            masses.append(weight)

        def second_pass(base, rows, filled, masses):
            more = []
            for h in heads:
                weight = jnp.exp2(scores[h, pl.ds(base, rows), :] - top[h])
                if filled is not None:
                    weight = jnp.where(lax.broadcasted_iota(I32, (rows, lanes), 0) < filled, weight, 0.0)
                sums[s, h] += lax.dot_general(
                    kv[h, 2 + s, pl.ds(base, rows), :], weight.astype(BF16), tn, preferred_element_type=F32
                )
                more.append(masses[h] + fold(weight, jnp.sum))
            return tuple(more)

        masses = each_tile(limit, second_pass, tuple(masses))
        for h in heads:
            tops[s, h] = top[h]
            totals[s, h] = jnp.sum(masses[h], axis=0, keepdims=True)
        return carry

    lax.fori_loop(0, 2, shard, 0)
    for h in heads:
        top_a, top_b = tops[0, h], tops[1, h]
        top = jnp.maximum(top_a, top_b)
        scale_a = jnp.exp2(top_a - top)
        scale_b = jnp.exp2(top_b - top)
        total = jnp.maximum(totals[0, h] * scale_a + totals[1, h] * scale_b, 1.0)
        merged = sums[0, h] * (scale_a / total) + sums[1, h] * (scale_b / total)
        width = group * chip_rows
        for i, out in enumerate(outs):
            for b in range(blocks):
                at = i * set_lanes + b * width
                cut = slice(at, at + width)
                encode(out, (b * kv_heads + h) * width, merged[:, cut], top[:, cut], total[:, cut])


def attend(start, held, fresh, cache, *, own_rows, orders):
    sets = len(held)
    count = held[0].shape[0]
    chip_rows = CORES * own_rows
    tokens = min(count, CHUNK_BLOCKS * chip_rows)
    slots = cache[0].shape[0]
    kv_heads = cache[0].shape[1] // LANES
    heads = held[0].shape[1] // LANES - 1
    group = heads // kv_heads
    lanes = sets * tokens * group
    padded = -(-slots // TILES[-1]) * TILES[-1]
    sizes = (own_rows, orders, group, kv_heads, sets)
    shape = jax.ShapeDtypeStruct((LANES + STAT_ROWS, count * heads), I16)
    return pl.pallas_call(
        functools.partial(attend_kernel, sizes),
        out_shape=(shape,) * sets,
        grid=(count // tokens,),
        in_specs=[SMEM]
        + [pl.BlockSpec((tokens, heads * LANES), lambda i: (i, 0))] * sets
        + [pl.BlockSpec((count, LANES), lambda i: (0, heads))] * sets
        + [VMEM] * 2
        + [ANY] * 4,
        out_specs=(pl.BlockSpec((LANES + STAT_ROWS, tokens * heads), lambda i: (0, i)),) * sets,
        scratch_shapes=[
            pltpu.VMEM((kv_heads, LANES, lanes), BF16),
            pltpu.VMEM((kv_heads, padded, lanes), F32),
            pltpu.VMEM((2, kv_heads, LANES, lanes), F32),
            pltpu.VMEM((2, kv_heads, 1, lanes), F32),
            pltpu.VMEM((2, kv_heads, 1, lanes), F32),
            pltpu.VMEM((kv_heads, 4, padded, LANES), BF16),
            pltpu.SemaphoreType.DMA((kv_heads, 4)),
        ],
        compiler_params=pltpu.CompilerParams(vmem_limit_bytes=ATTEND_BYTES),
    )(start, *held, *held, *fresh, *cache)


def merged_part(refs, dims, at):
    stats = [decode_stats(ref, dims, at) for ref in refs]
    top = functools.reduce(jnp.maximum, [x[0] for x in stats])
    masses = [x[1] * jnp.exp2(x[0] - top) for x in stats]
    total = functools.reduce(jnp.add, masses)
    values = 0.0
    for ref, mass, (_, _, unit) in zip(refs, masses, stats):
        values = values + ref[:dims, at].astype(I32).astype(F32) * (mass / total * unit)
    return values, top, total


def merge_kernel(inputs, *refs):
    parts, outs = refs[:inputs], refs[inputs:]
    dims = parts[0].shape[0] - STAT_ROWS
    width = outs[0].shape[1]
    step = min(width, 2 * LANES)
    for i, out in reversed(list(enumerate(outs))):
        for at in range(0, width, step):
            encode(out, at, *merged_part(parts, dims, slice(i * width + at, i * width + at + step)))


def merge(parts, pieces):
    rows, width = parts[0].shape
    shape = jax.ShapeDtypeStruct((rows, width // pieces), I16)
    return pl.pallas_call(
        functools.partial(merge_kernel, len(parts)),
        out_shape=(shape,) * pieces,
        in_specs=[VMEM] * len(parts),
        out_specs=(VMEM,) * pieces,
        compiler_params=SMALL,
    )(*parts)


def finish_kernel(group, inputs, *refs):
    parts, (mine, other) = refs[:inputs], refs[inputs:]
    dims = parts[0].shape[0] - STAT_ROWS
    own_rows = mine.shape[0]
    chip_rows = CORES * own_rows
    width = group * chip_rows
    for h in range(parts[0].shape[1] // width):
        values, _, _ = merged_part(parts, dims, slice(h * width, (h + 1) * width))
        rows = values.T
        for g in range(group):
            at = (h * group + g) * dims
            tokens = rows[g * chip_rows : (g + 1) * chip_rows]
            mine[:, at : at + dims] = tokens[:own_rows].astype(BF16)
            other[:, at : at + dims] = tokens[own_rows:].astype(BF16)


def finish(parts, own_rows, group):
    rows, width = parts[0].shape
    shape = jax.ShapeDtypeStruct((own_rows, width // (CORES * own_rows) * (rows - STAT_ROWS)), BF16)
    return pl.pallas_call(
        functools.partial(finish_kernel, group, len(parts)),
        out_shape=(shape, shape),
        in_specs=[VMEM] * len(parts),
        out_specs=(VMEM, VMEM),
        compiler_params=SMALL,
    )(*parts)


def place_kernel(mine, theirs, out):
    half = mine.shape[1]
    core = lax.axis_index("ctx") % CORES
    out[:, pl.ds(pl.multiple_of(core * half, LANES), half)] = mine[...]
    out[:, pl.ds(pl.multiple_of((1 - core) * half, LANES), half)] = theirs[...]


def place(mine, theirs):
    rows, half = mine.shape
    return pl.pallas_call(
        place_kernel,
        out_shape=jax.ShapeDtypeStruct((rows, CORES * half), BF16),
        in_specs=[VMEM, VMEM],
        out_specs=VMEM,
        compiler_params=SMALL,
    )(mine, theirs)


def per_device(
    queries, cache_keys, cached_value_rows, new_keys, prompt_value_rows, cache_len, prompt_start
):
    width = lax.axis_size("ctx")
    own_rows = queries.shape[0]
    group = queries.shape[1] // cache_keys.shape[1]
    bits = [CORES << i for i in range((width // CORES).bit_length() - 1)]
    orders = (tuple(bits[-1:] + bits[:-1]), tuple(bits[-2:-1] + bits[:-2] + bits[-1:]))
    odd = len(bits) % 2
    stages = [(0,)] * odd + [(i, i + 1) for i in range(odd, len(bits), 2)]

    def swap(x):
        return lax.ppermute(x, "ctx", [(i, i ^ 1) for i in range(width)])

    def partners(stage):
        return [
            [sum(order[bit] for k, bit in enumerate(stage) if c >> k & 1) for order in orders]
            for c in range(1, 1 << len(stage))
        ]

    def exchange(x, distance):
        return lax.ppermute(x, "ctx", [(i, i ^ distance[i % CORES]) for i in range(width)])

    def own_half(x):
        half = x.shape[1] // CORES
        return lax.dynamic_slice_in_dim(x, core * half, half, 1)

    core = lax.axis_index("ctx") % CORES
    held = join(cache_len, swap(cache_len), own_half(queries), swap(queries))
    fresh = [jnp.concatenate([x, swap(x)], axis=0) for x in (new_keys, prompt_value_rows)]
    cache = [y for x in (cache_keys, cached_value_rows) for y in (own_half(x), swap(x))]
    for stage in stages:
        gathered = [held] + [exchange(held, distance) for distance in partners(stage)]
        if stage != stages[-1]:
            held = jnp.concatenate(gathered, axis=0)
    parts = attend(prompt_start, gathered, fresh, cache, own_rows=own_rows, orders=orders)
    for stage in reversed(stages):
        sent = [exchange(x, distance) for x, distance in zip(parts[1:], partners(stage))]
        parts = [parts[0]] + sent
        if stage != stages[0]:
            parts = merge(parts, 1 << len(stages[stages.index(stage) - 1]))
    mine, other = finish(parts, own_rows, group)
    return place(mine, swap(other))


def solution(mesh):
    return jax.shard_map(
        per_device,
        mesh=mesh,
        in_specs=(
            P(("groups", "ctx"), None),
            P(("groups", "ctx"), None),
            P(("groups", "ctx"), None),
            P(("groups", "ctx"), None),
            P(("groups", "ctx"), None),
            P(("groups", "ctx")),
            P("groups"),
        ),
        out_specs=P(("groups", "ctx"), None),
        check_vma=False,
    )
```

```python
import functools
import math

import jax
import jax.numpy as jnp
from jax import lax
from jax.experimental import pallas as pl
from jax.experimental.pallas import tpu as pltpu
from jax.sharding import PartitionSpec as P

KEY_VALUE_HEADS = 4
LANES = 128
CORES = 2
FLOOR = -1e30
TILES = (1024, 512)
TAIL = 256
ATTEND_BYTES = 32 << 20
STAT_ROWS = 16
CHUNK_BLOCKS = 2
STEP = 2.0**15
MARGIN = 0.9998
F32 = jnp.float32
BF16 = jnp.bfloat16
I16 = jnp.int16
I32 = jnp.int32
VMEM = pl.BlockSpec(memory_space=pltpu.VMEM)
SMEM = pl.BlockSpec(memory_space=pltpu.SMEM)
SMALL = pltpu.CompilerParams(vmem_limit_bytes=8 << 20)


def encode(out, at, values, top, total):
    dims, width = values.shape
    largest = jnp.max(jnp.abs(values), axis=0, keepdims=True)
    exponent = jnp.floor(jnp.log2(jnp.maximum(largest, 1e-30))) + 1.0
    fixed = jnp.floor(values * (jnp.exp2(15.0 - exponent) * MARGIN) + 0.5)
    size = jnp.abs(top)
    level = jnp.zeros_like(top)
    scaled = top
    for i in range(1, 9):
        above = size >= STEP**i
        level = level + jnp.where(above, 1.0, 0.0)
        scaled = scaled * jnp.where(above, 1.0 / STEP, 1.0)
    a = jnp.floor(scaled)
    rest = (scaled - a) * STEP
    b = jnp.floor(rest)
    c = jnp.floor((rest - b) * STEP)
    logs = jnp.log2(total) * 1024.0
    la = jnp.floor(logs)
    lb = jnp.floor((logs - la) * STEP)
    row = lax.broadcasted_iota(I32, (STAT_ROWS, width), 0)
    stats = jnp.zeros((STAT_ROWS, width), F32)
    for i, part in enumerate((level, a, b, c, exponent, la, lb)):
        stats = jnp.where(row == i, part, stats)
    if not isinstance(at, int):
        at = pl.multiple_of(at, LANES)
    out[:dims, pl.ds(at, width)] = fixed.astype(I32).astype(I16)
    out[dims:, pl.ds(at, width)] = stats.astype(I32).astype(I16)


def decode_stats(ref, dims, at):
    stats = ref[dims:, at].astype(I32).astype(F32)

    def part(i):
        return stats[i : i + 1, :]

    top = part(1) + (part(2) + part(3) * (1.0 / STEP)) * (1.0 / STEP)
    for i in range(1, 9):
        top = top * jnp.where(part(0) >= i, STEP, 1.0)
    total = jnp.exp2((part(5) + part(6) * (1.0 / STEP)) * (1.0 / 1024.0))
    return top, total, jnp.exp2(part(4) - 15.0) * (1.0 / MARGIN)


def join_kernel(length, length_other, mine, queries_other, out):
    rows, half = mine.shape
    core = lax.axis_index("ctx") % CORES
    other = queries_other[:, pl.ds(pl.multiple_of(core * half, LANES), half)]
    out[:, :half] = jnp.concatenate([mine[...].astype(F32), other.astype(F32)], axis=0).astype(BF16)
    lane = lax.broadcasted_iota(I32, (CORES * rows, LANES), 1)
    row = lax.broadcasted_iota(I32, (CORES * rows, LANES), 0)
    count = jnp.where(row < rows, length[0], length_other[0])
    coded = jnp.where(lane == 0, count // LANES, jnp.where(lane == 1, count % LANES, 0))
    out[:, half:] = coded.astype(F32).astype(BF16)


def join(length, length_other, mine, queries_other):
    rows, half = mine.shape
    return pl.pallas_call(
        join_kernel,
        out_shape=jax.ShapeDtypeStruct((CORES * rows, half + LANES), BF16),
        in_specs=[SMEM, SMEM, VMEM, VMEM],
        out_specs=VMEM,
        compiler_params=SMALL,
    )(length, length_other, mine, queries_other)


def attend_kernel(sizes, *refs):
    own_rows, orders, group, kv_heads, sets, first, chosen = sizes
    start = refs[0]
    gathered = refs[1 : 1 + sets]
    new_keys, new_values, keys_a, keys_b, values_a, values_b = refs[1 + sets : 7 + sets]
    out, query_t, scores, sums, tops, totals = refs[7 + sets :]
    queries = gathered[first : first + chosen]
    chip_rows = CORES * own_rows
    slots = keys_a.shape[0]
    count = gathered[0].shape[0]
    tokens = min(count, CHUNK_BLOCKS * chip_rows)
    blocks = tokens // chip_rows
    set_blocks = count // chip_rows
    set_lanes = tokens * group
    lanes = chosen * set_lanes
    me = lax.axis_index("ctx")
    core, chip = me % CORES, me // CORES
    factor = math.log2(math.e) / math.sqrt(LANES)
    heads = range(kv_heads)

    steps = [jnp.where(core == 0, a // CORES, b // CORES) for a, b in zip(*orders)]

    def origin(block):
        off = jnp.zeros_like(block)
        for i, step in enumerate(steps):
            off = off ^ jnp.where((block >> i) & 1 == 1, step, 0)
        return chip ^ off

    found = [0.0, 0.0, 0.0]
    for i, ref in enumerate(gathered):
        rows = ref.shape[0]
        lane = lax.broadcasted_iota(I32, (rows, LANES), 1)
        row = lax.broadcasted_iota(I32, (rows, LANES), 0)
        place = origin(row // chip_rows + i * set_blocks)
        inside = row % chip_rows
        counts = jnp.where(lane == 0, float(LANES), 1.0) * ref[:, ref.shape[1] - LANES :].astype(F32)
        counts = jnp.where((inside % own_rows == 0) & (lane < 2), counts, 0.0)
        here = place == chip
        second = inside >= own_rows
        for k, wanted in enumerate((place < chip, here & ~second, here & second)):
            found[k] = found[k] + jnp.sum(jnp.where(wanted, counts, 0.0), axis=0, keepdims=True)
    row = lax.broadcasted_iota(I32, (8, LANES), 0)
    found = jnp.where(row == 0, found[0], jnp.where(row == 1, found[1], found[2]))
    found = jnp.sum(found, axis=1, keepdims=True).astype(I32)
    before, length = found[0, 0], [found[1, 0], found[2, 0]]
    begins = [
        before + jnp.where(core == 1, length[1], 0),
        before + jnp.where(core == 0, length[0], 0),
    ]
    limits = [jnp.clip(jnp.minimum(n, start[0] - at), 0, slots) for n, at in zip(length, begins)]

    def attend_chunk(chunk, carry):
        key_row = lax.broadcasted_iota(I32, (chip_rows, lanes), 0)
        lane = lax.broadcasted_iota(I32, (chip_rows, lanes), 1)
        part = key_row // own_rows
        key_id = (chip * CORES + (core ^ part)) * own_rows + key_row % own_rows
        inside = lane % chip_rows
        block = (lane // set_lanes + first) * set_blocks + lane % set_lanes // (group * chip_rows) + chunk * blocks
        token = (origin(block) * CORES + (core ^ (inside // own_rows))) * own_rows + inside % own_rows
        causal = key_id <= token
        nothing = jnp.zeros((16 - chip_rows % 16, LANES), F32)
        fresh_scores, fresh_values = [], []

        for h in heads:
            rows = pl.ds(pl.multiple_of(chunk * tokens, tokens), tokens)
            q = jnp.concatenate(
                [
                    ref[rows, (h * group + g) * LANES : (h * group + g + 1) * LANES].astype(F32)[b * chip_rows :][:chip_rows]
                    for ref in queries
                    for b in range(blocks)
                    for g in range(group)
                ],
                axis=0,
            )
            query_t[h] = q.T.astype(BF16)
            at = pl.multiple_of((core * kv_heads + h) * LANES, LANES)

            def padded_rows(ref):
                return jnp.concatenate([ref[:, pl.ds(at, LANES)].astype(F32), nothing], 0).astype(BF16)

            fresh_values.append(padded_rows(new_values))
            fresh_scores.append(jnp.dot(padded_rows(new_keys), query_t[h], preferred_element_type=F32)[:chip_rows] * factor)

        def fold(tile, combine):
            return combine(tile.reshape(tile.shape[0] // 8, 8, lanes), axis=0)

        def each_tile(limit, body, carry):
            base, rest = 0, limit
            for rows in TILES:
                count = rest // rows

                def whole(j, carry, rows=rows, base=base):
                    return body(pl.multiple_of(base + j * rows, TILES[-1]), rows, None, carry)

                carry = lax.fori_loop(0, count, whole, carry)
                base, rest = base + count * rows, rest - count * rows
            base = pl.multiple_of(base, TILES[-1])
            for rows, need in ((TAIL, (rest > 0) & (rest <= TAIL)), (TILES[-1], rest > TAIL)):
                carry = lax.cond(need, lambda c, rows=rows: body(base, rows, rest, c), lambda c: c, carry)
            return carry

        tn = (((0,), (0,)), ((), ()))

        for s, (keys, values) in enumerate(((keys_a, values_a), (keys_b, values_b))):
            limit = limits[s]
            seen = causal & (part == s)

            def columns(h, s=s):
                return pl.ds(pl.multiple_of((core * kv_heads * LANES if s else 0) + h * LANES, LANES), LANES)

            def first_pass(base, rows, filled, peaks, keys=keys, columns=columns):
                higher = []
                for h in heads:
                    tile = jnp.dot(keys[pl.ds(base, rows), columns(h)], query_t[h], preferred_element_type=F32) * factor
                    if filled is not None:
                        tile = jnp.where(lax.broadcasted_iota(I32, (rows, lanes), 0) < filled, tile, FLOOR)
                    scores[h, pl.ds(base, rows), :] = tile
                    higher.append(jnp.maximum(peaks[h], fold(tile, jnp.max)))
                return tuple(higher)

            peaks = each_tile(limit, first_pass, tuple(jnp.where(seen, x, FLOOR) for x in fresh_scores))
            top = [jnp.max(x, axis=0, keepdims=True) for x in peaks]
            masses = []
            for h in heads:
                weight = jnp.where(seen, jnp.exp2(fresh_scores[h] - top[h]), 0.0)
                padded = jnp.concatenate([weight, jnp.zeros((16 - chip_rows % 16, lanes), F32)], 0).astype(BF16)
                sums[s, h] = lax.dot_general(fresh_values[h], padded, tn, preferred_element_type=F32)
                masses.append(weight)

            def second_pass(base, rows, filled, masses, s=s, top=top, values=values, columns=columns):
                more = []
                for h in heads:
                    weight = jnp.exp2(scores[h, pl.ds(base, rows), :] - top[h])
                    if filled is not None:
                        weight = jnp.where(lax.broadcasted_iota(I32, (rows, lanes), 0) < filled, weight, 0.0)
                    sums[s, h] += lax.dot_general(
                        values[pl.ds(base, rows), columns(h)], weight.astype(BF16), tn, preferred_element_type=F32
                    )
                    more.append(masses[h] + fold(weight, jnp.sum))
                return tuple(more)

            masses = each_tile(limit, second_pass, tuple(masses))
            for h in heads:
                tops[s, h] = top[h]
                totals[s, h] = jnp.sum(masses[h], axis=0, keepdims=True)

        for h in heads:
            top_a, top_b = tops[0, h], tops[1, h]
            top = jnp.maximum(top_a, top_b)
            scale_a = jnp.exp2(top_a - top)
            scale_b = jnp.exp2(top_b - top)
            total = jnp.maximum(totals[0, h] * scale_a + totals[1, h] * scale_b, 1.0)
            merged = sums[0, h] * (scale_a / total) + sums[1, h] * (scale_b / total)
            width = group * chip_rows
            for i in range(chosen):
                for b in range(blocks):
                    at = i * set_lanes + b * width
                    cut = slice(at, at + width)
                    place = ((i * set_blocks + chunk * blocks + b) * kv_heads + h) * width
                    encode(out, place, merged[:, cut], top[:, cut], total[:, cut])
        return carry

    chunks = count // tokens
    if chunks == 1:
        attend_chunk(0, 0)
    else:
        lax.fori_loop(0, chunks, attend_chunk, 0)


def attend(start, gathered, chosen, fresh, cache, *, own_rows, orders):
    first, end = chosen
    count = gathered[0].shape[0]
    chip_rows = CORES * own_rows
    tokens = min(count, CHUNK_BLOCKS * chip_rows)
    slots = cache[0].shape[0]
    kv_heads = cache[0].shape[1] // LANES
    heads = gathered[0].shape[1] // LANES - 1
    group = heads // kv_heads
    lanes = (end - first) * tokens * group
    padded = -(-slots // TILES[-1]) * TILES[-1]
    sizes = (own_rows, orders, group, kv_heads, len(gathered), first, end - first)
    return pl.pallas_call(
        functools.partial(attend_kernel, sizes),
        out_shape=jax.ShapeDtypeStruct((LANES + STAT_ROWS, (end - first) * count * heads), I16),
        in_specs=[SMEM] + [VMEM] * (len(gathered) + 6),
        out_specs=VMEM,
        scratch_shapes=[
            pltpu.VMEM((kv_heads, LANES, lanes), BF16),
            pltpu.VMEM((kv_heads, padded, lanes), F32),
            pltpu.VMEM((2, kv_heads, LANES, lanes), F32),
            pltpu.VMEM((2, kv_heads, 1, lanes), F32),
            pltpu.VMEM((2, kv_heads, 1, lanes), F32),
        ],
        compiler_params=pltpu.CompilerParams(vmem_limit_bytes=ATTEND_BYTES),
    )(start, *gathered, *fresh, *cache)


def merged_part(refs, dims, at):
    stats = [decode_stats(ref, dims, at) for ref in refs]
    top = functools.reduce(jnp.maximum, [x[0] for x in stats])
    masses = [x[1] * jnp.exp2(x[0] - top) for x in stats]
    total = functools.reduce(jnp.add, masses)
    values = 0.0
    for ref, mass, (_, _, unit) in zip(refs, masses, stats):
        values = values + ref[:dims, at].astype(I32).astype(F32) * (mass / total * unit)
    return values, top, total


def merge_kernel(inputs, *refs):
    parts, outs = refs[:inputs], refs[inputs:]
    dims = parts[0].shape[0] - STAT_ROWS
    width = outs[0].shape[1]
    step = min(width, 2 * LANES)
    for i, out in reversed(list(enumerate(outs))):
        for at in range(0, width, step):
            encode(out, at, *merged_part(parts, dims, slice(i * width + at, i * width + at + step)))


def merge(parts, pieces):
    rows, width = parts[0].shape
    shape = jax.ShapeDtypeStruct((rows, width // pieces), I16)
    return pl.pallas_call(
        functools.partial(merge_kernel, len(parts)),
        out_shape=(shape,) * pieces,
        in_specs=[VMEM] * len(parts),
        out_specs=(VMEM,) * pieces,
        compiler_params=SMALL,
    )(*parts)


def finish_kernel(group, inputs, *refs):
    parts, (mine, other) = refs[:inputs], refs[inputs:]
    dims = parts[0].shape[0] - STAT_ROWS
    own_rows = mine.shape[0]
    chip_rows = CORES * own_rows
    width = group * chip_rows
    for h in range(parts[0].shape[1] // width):
        values, _, _ = merged_part(parts, dims, slice(h * width, (h + 1) * width))
        rows = values.T
        for g in range(group):
            at = (h * group + g) * dims
            tokens = rows[g * chip_rows : (g + 1) * chip_rows]
            mine[:, at : at + dims] = tokens[:own_rows].astype(BF16)
            other[:, at : at + dims] = tokens[own_rows:].astype(BF16)


def finish(parts, own_rows, group):
    rows, width = parts[0].shape
    shape = jax.ShapeDtypeStruct((own_rows, width // (CORES * own_rows) * (rows - STAT_ROWS)), BF16)
    return pl.pallas_call(
        functools.partial(finish_kernel, group, len(parts)),
        out_shape=(shape, shape),
        in_specs=[VMEM] * len(parts),
        out_specs=(VMEM, VMEM),
        compiler_params=SMALL,
    )(*parts)


def place_kernel(mine, theirs, out):
    half = mine.shape[1]
    core = lax.axis_index("ctx") % CORES
    out[:, pl.ds(pl.multiple_of(core * half, LANES), half)] = mine[...]
    out[:, pl.ds(pl.multiple_of((1 - core) * half, LANES), half)] = theirs[...]


def place(mine, theirs):
    rows, half = mine.shape
    return pl.pallas_call(
        place_kernel,
        out_shape=jax.ShapeDtypeStruct((rows, CORES * half), BF16),
        in_specs=[VMEM, VMEM],
        out_specs=VMEM,
        compiler_params=SMALL,
    )(mine, theirs)


def per_device(
    queries, cache_keys, cached_value_rows, new_keys, prompt_value_rows, cache_len, prompt_start
):
    width = lax.axis_size("ctx")
    own_rows = queries.shape[0]
    group = queries.shape[1] // cache_keys.shape[1]
    bits = [CORES << i for i in range((width // CORES).bit_length() - 1)]
    orders = (tuple(bits[-1:] + bits[:-1]), tuple(bits[-2:] + bits[:-2]))
    odd = len(bits) % 2
    stages = [(0,)] * odd + [(i, i + 1) for i in range(odd, len(bits), 2)]

    def swap(x):
        return lax.ppermute(x, "ctx", [(i, i ^ 1) for i in range(width)])

    def partners(stage):
        return [
            [sum(order[bit] for k, bit in enumerate(stage) if c >> k & 1) for order in orders]
            for c in range(1, 1 << len(stage))
        ]

    def exchange(x, distance):
        return lax.ppermute(x, "ctx", [(i, i ^ distance[i % CORES]) for i in range(width)])

    def own_half(x):
        half = x.shape[1] // CORES
        return lax.dynamic_slice_in_dim(x, core * half, half, 1)

    core = lax.axis_index("ctx") % CORES
    held = join(cache_len, swap(cache_len), own_half(queries), swap(queries))
    cache_keys, cached_value_rows, new_keys, prompt_value_rows, held = lax.optimization_barrier(
        (cache_keys, cached_value_rows, new_keys, prompt_value_rows, held)
    )
    fresh = [jnp.concatenate([x, swap(x)], axis=0) for x in (new_keys, prompt_value_rows)]
    cache = [y for x in (cache_keys, cached_value_rows) for y in (own_half(x), swap(x))]
    for stage in stages:
        gathered = [held] + [exchange(held, distance) for distance in partners(stage)]
        if stage != stages[-1]:
            held = jnp.concatenate(gathered, axis=0)
    half = len(gathered) // 2
    far, near = (
        attend(prompt_start, gathered, chosen, fresh, cache, own_rows=own_rows, orders=orders)
        for chosen in ((half, 2 * half), (0, half))
    )
    last = len(bits) - 1
    parts = [near, exchange(far, partners((last,))[0])]
    for stage in [(i - 1, i) if i else (i,) for i in range(last - 1, -1, -2)]:
        parts = merge(parts, 1 << len(stage))
        parts = [parts[0]] + [exchange(x, distance) for x, distance in zip(parts[1:], partners(stage))]
    mine, other = finish(parts, own_rows, group)
    return place(mine, swap(other))


def solution(mesh):
    return jax.shard_map(
        per_device,
        mesh=mesh,
        in_specs=(
            P(("groups", "ctx"), None),
            P(("groups", "ctx"), None),
            P(("groups", "ctx"), None),
            P(("groups", "ctx"), None),
            P(("groups", "ctx"), None),
            P(("groups", "ctx")),
            P("groups"),
        ),
        out_specs=P(("groups", "ctx"), None),
        check_vma=False,
    )
```

```python
import functools
import math

import jax
import jax.numpy as jnp
from jax import lax
from jax.experimental import pallas as pl
from jax.experimental.pallas import tpu as pltpu
from jax.sharding import PartitionSpec as P

KEY_VALUE_HEADS = 4
LANES = 128
CORES = 2
FLOOR = -1e30
TILE = 256
ATTEND_BYTES = 32 << 20
STAT_ROWS = 16
CHUNK_BLOCKS = 2
STEP = 2.0**15
MARGIN = 0.9998
F32 = jnp.float32
BF16 = jnp.bfloat16
I16 = jnp.int16
I32 = jnp.int32
VMEM = pl.BlockSpec(memory_space=pltpu.VMEM)
SMEM = pl.BlockSpec(memory_space=pltpu.SMEM)
SMALL = pltpu.CompilerParams(vmem_limit_bytes=8 << 20)


def encode(out, at, values, top, total):
    dims, width = values.shape
    largest = jnp.max(jnp.abs(values), axis=0, keepdims=True)
    exponent = jnp.floor(jnp.log2(jnp.maximum(largest, 1e-30))) + 1.0
    fixed = jnp.floor(values * (jnp.exp2(15.0 - exponent) * MARGIN) + 0.5)
    size = jnp.abs(top)
    level = jnp.zeros_like(top)
    scaled = top
    for i in range(1, 9):
        above = size >= STEP**i
        level = level + jnp.where(above, 1.0, 0.0)
        scaled = scaled * jnp.where(above, 1.0 / STEP, 1.0)
    a = jnp.floor(scaled)
    rest = (scaled - a) * STEP
    b = jnp.floor(rest)
    c = jnp.floor((rest - b) * STEP)
    logs = jnp.log2(total) * 1024.0
    la = jnp.floor(logs)
    lb = jnp.floor((logs - la) * STEP)
    row = lax.broadcasted_iota(I32, (STAT_ROWS, width), 0)
    stats = jnp.zeros((STAT_ROWS, width), F32)
    for i, part in enumerate((level, a, b, c, exponent, la, lb)):
        stats = jnp.where(row == i, part, stats)
    if not isinstance(at, int):
        at = pl.multiple_of(at, LANES)
    out[:dims, pl.ds(at, width)] = fixed.astype(I32).astype(I16)
    out[dims:, pl.ds(at, width)] = stats.astype(I32).astype(I16)


def decode_stats(ref, dims, at):
    stats = ref[dims:, at].astype(I32).astype(F32)

    def part(i):
        return stats[i : i + 1, :]

    top = part(1) + (part(2) + part(3) * (1.0 / STEP)) * (1.0 / STEP)
    for i in range(1, 9):
        top = top * jnp.where(part(0) >= i, STEP, 1.0)
    total = jnp.exp2((part(5) + part(6) * (1.0 / STEP)) * (1.0 / 1024.0))
    return top, total, jnp.exp2(part(4) - 15.0) * (1.0 / MARGIN)


def join_kernel(length, length_other, mine, queries_other, out):
    rows, half = mine.shape
    core = lax.axis_index("ctx") % CORES
    other = queries_other[:, pl.ds(pl.multiple_of(core * half, LANES), half)]
    out[:, :half] = jnp.concatenate([mine[...].astype(F32), other.astype(F32)], axis=0).astype(BF16)
    lane = lax.broadcasted_iota(I32, (CORES * rows, LANES), 1)
    row = lax.broadcasted_iota(I32, (CORES * rows, LANES), 0)
    count = jnp.where(row < rows, length[0], length_other[0])
    coded = jnp.where(lane == 0, count // LANES, jnp.where(lane == 1, count % LANES, 0))
    out[:, half:] = coded.astype(F32).astype(BF16)


def join(length, length_other, mine, queries_other):
    rows, half = mine.shape
    return pl.pallas_call(
        join_kernel,
        out_shape=jax.ShapeDtypeStruct((CORES * rows, half + LANES), BF16),
        in_specs=[SMEM, SMEM, VMEM, VMEM],
        out_specs=VMEM,
        compiler_params=SMALL,
    )(length, length_other, mine, queries_other)


def attend_kernel(sizes, *refs):
    own_rows, orders, group, kv_heads, sets, first, chosen = sizes
    start = refs[0]
    gathered = refs[1 : 1 + sets]
    fresh_a, fresh_b, keys_a, keys_b, values_a, values_b = refs[1 + sets : 7 + sets]
    out, query_t, scores, sums, tops, totals = refs[7 + sets :]
    queries = gathered[first : first + chosen]
    chip_rows = CORES * own_rows
    slots = keys_a.shape[0]
    count = gathered[0].shape[0]
    tokens = min(count, CHUNK_BLOCKS * chip_rows)
    blocks = tokens // chip_rows
    set_blocks = count // chip_rows
    set_lanes = tokens * group
    lanes = chosen * set_lanes
    me = lax.axis_index("ctx")
    core, chip = me % CORES, me // CORES
    factor = math.log2(math.e) / math.sqrt(LANES)
    heads = range(kv_heads)

    steps = [jnp.where(core == 0, a // CORES, b // CORES) for a, b in zip(*orders)]

    def origin(block):
        off = jnp.zeros_like(block)
        for i, step in enumerate(steps):
            off = off ^ jnp.where((block >> i) & 1 == 1, step, 0)
        return chip ^ off

    found = [0.0, 0.0, 0.0]
    for i, ref in enumerate(gathered):
        rows = ref.shape[0]
        lane = lax.broadcasted_iota(I32, (rows, LANES), 1)
        row = lax.broadcasted_iota(I32, (rows, LANES), 0)
        place = origin(row // chip_rows + i * set_blocks)
        inside = row % chip_rows
        counts = jnp.where(lane == 0, float(LANES), 1.0) * ref[:, ref.shape[1] - LANES :].astype(F32)
        counts = jnp.where((inside % own_rows == 0) & (lane < 2), counts, 0.0)
        here = place == chip
        second = inside >= own_rows
        for k, wanted in enumerate((place < chip, here & ~second, here & second)):
            found[k] = found[k] + jnp.sum(jnp.where(wanted, counts, 0.0), axis=0, keepdims=True)
    row = lax.broadcasted_iota(I32, (8, LANES), 0)
    found = jnp.where(row == 0, found[0], jnp.where(row == 1, found[1], found[2]))
    found = jnp.sum(found, axis=1, keepdims=True).astype(I32)
    before, length = found[0, 0], [found[1, 0], found[2, 0]]
    begins = [
        before + jnp.where(core == 1, length[1], 0),
        before + jnp.where(core == 0, length[0], 0),
    ]
    limits = [jnp.clip(jnp.minimum(n, start[0] - at), 0, slots) for n, at in zip(length, begins)]

    def attend_chunk(chunk, carry):
        key_row = lax.broadcasted_iota(I32, (chip_rows, lanes), 0)
        lane = lax.broadcasted_iota(I32, (chip_rows, lanes), 1)
        part = key_row // own_rows
        key_id = (chip * CORES + (core ^ part)) * own_rows + key_row % own_rows
        inside = lane % chip_rows
        block = (lane // set_lanes + first) * set_blocks + lane % set_lanes // (group * chip_rows) + chunk * blocks
        token = (origin(block) * CORES + (core ^ (inside // own_rows))) * own_rows + inside % own_rows
        causal = key_id <= token
        nothing = jnp.zeros((16 - chip_rows % 16, LANES), F32)
        fresh_scores, fresh_values = [], []

        for h in heads:
            rows = pl.ds(pl.multiple_of(chunk * tokens, tokens), tokens)
            q = jnp.concatenate(
                [
                    ref[rows, (h * group + g) * LANES : (h * group + g + 1) * LANES].astype(F32)[b * chip_rows :][:chip_rows]
                    for ref in queries
                    for b in range(blocks)
                    for g in range(group)
                ],
                axis=0,
            )
            query_t[h] = q.T.astype(BF16)
            at = pl.multiple_of((core * kv_heads + h) * LANES, LANES)

            mine = fresh_a[:, pl.ds(at, LANES)].astype(F32)
            theirs = fresh_b[:, pl.ds(at, LANES)].astype(F32)
            new_keys = jnp.concatenate([mine[:own_rows], theirs[:own_rows], nothing], 0).astype(BF16)
            new_values = jnp.concatenate([mine[own_rows:], theirs[own_rows:], nothing], 0).astype(BF16)
            fresh_values.append(new_values)
            fresh_scores.append(jnp.dot(new_keys, query_t[h], preferred_element_type=F32)[:chip_rows] * factor)

        def fold(tile, combine):
            return combine(tile.reshape(tile.shape[0] // 8, 8, lanes), axis=0)

        tn = (((0,), (0,)), ((), ()))

        def shard(s, keys, values, tiles):
            seen = causal & (part == s)
            filled = limits[s] - (tiles - 1) * TILE

            def columns(h):
                return pl.ds(pl.multiple_of((core * kv_heads * LANES if s else 0) + h * LANES, LANES), LANES)

            pieces = [slice(0, (tiles - 1) * TILE)] * (tiles > 1) + [slice((tiles - 1) * TILE, tiles * TILE)] * (tiles > 0)
            top = []
            for h in heads:
                peak = jnp.where(seen, fresh_scores[h], FLOOR)
                for rows in pieces:
                    tile = jnp.dot(keys[rows, columns(h)], query_t[h], preferred_element_type=F32) * factor
                    if rows is pieces[-1]:
                        tile = jnp.where(lax.broadcasted_iota(I32, tile.shape, 0) < filled, tile, FLOOR)
                    scores[h, rows, :] = tile
                    peak = jnp.maximum(peak, fold(tile, jnp.max))
                top.append(jnp.max(peak, axis=0, keepdims=True))
            for h in heads:
                weight = jnp.where(seen, jnp.exp2(fresh_scores[h] - top[h]), 0.0)
                padded = jnp.concatenate([weight, jnp.zeros((16 - chip_rows % 16, lanes), F32)], 0).astype(BF16)
                summed = lax.dot_general(fresh_values[h], padded, tn, preferred_element_type=F32)
                mass = weight
                for rows in pieces:
                    weight = jnp.exp2(scores[h, rows, :] - top[h])
                    if rows is pieces[-1]:
                        weight = jnp.where(lax.broadcasted_iota(I32, weight.shape, 0) < filled, weight, 0.0)
                    summed = summed + lax.dot_general(
                        values[rows, columns(h)], weight.astype(BF16), tn, preferred_element_type=F32
                    )
                    mass = mass + fold(weight, jnp.sum)
                sums[s, h] = summed
                tops[s, h] = top[h]
                totals[s, h] = jnp.sum(mass, axis=0, keepdims=True)

        for s, (keys, values) in enumerate(((keys_a, values_a), (keys_b, values_b))):
            needed = (limits[s] + TILE - 1) // TILE
            for tiles in range(slots // TILE + 1):
                pl.when(needed == tiles)(functools.partial(shard, s, keys, values, tiles))

        for h in heads:
            top_a, top_b = tops[0, h], tops[1, h]
            top = jnp.maximum(top_a, top_b)
            scale_a = jnp.exp2(top_a - top)
            scale_b = jnp.exp2(top_b - top)
            total = jnp.maximum(totals[0, h] * scale_a + totals[1, h] * scale_b, 1.0)
            merged = sums[0, h] * (scale_a / total) + sums[1, h] * (scale_b / total)
            width = group * chip_rows
            for i in range(chosen):
                for b in range(blocks):
                    at = i * set_lanes + b * width
                    cut = slice(at, at + width)
                    place = ((i * set_blocks + chunk * blocks + b) * kv_heads + h) * width
                    encode(out, place, merged[:, cut], top[:, cut], total[:, cut])
        return carry

    chunks = count // tokens
    if chunks == 1:
        attend_chunk(0, 0)
    else:
        lax.fori_loop(0, chunks, attend_chunk, 0)


def attend(start, gathered, chosen, fresh, cache, *, own_rows, orders):
    first, end = chosen
    count = gathered[0].shape[0]
    chip_rows = CORES * own_rows
    tokens = min(count, CHUNK_BLOCKS * chip_rows)
    slots = cache[0].shape[0]
    kv_heads = cache[0].shape[1] // LANES
    heads = gathered[0].shape[1] // LANES - 1
    group = heads // kv_heads
    lanes = (end - first) * tokens * group
    sizes = (own_rows, orders, group, kv_heads, len(gathered), first, end - first)
    return pl.pallas_call(
        functools.partial(attend_kernel, sizes),
        out_shape=jax.ShapeDtypeStruct((LANES + STAT_ROWS, (end - first) * count * heads), I16),
        in_specs=[SMEM] + [VMEM] * (len(gathered) + 6),
        out_specs=VMEM,
        scratch_shapes=[
            pltpu.VMEM((kv_heads, LANES, lanes), BF16),
            pltpu.VMEM((kv_heads, slots, lanes), F32),
            pltpu.VMEM((2, kv_heads, LANES, lanes), F32),
            pltpu.VMEM((2, kv_heads, 1, lanes), F32),
            pltpu.VMEM((2, kv_heads, 1, lanes), F32),
        ],
        compiler_params=pltpu.CompilerParams(vmem_limit_bytes=ATTEND_BYTES),
    )(start, *gathered, *fresh, *cache)


def merged_part(refs, dims, at):
    stats = [decode_stats(ref, dims, at) for ref in refs]
    top = functools.reduce(jnp.maximum, [x[0] for x in stats])
    masses = [x[1] * jnp.exp2(x[0] - top) for x in stats]
    total = functools.reduce(jnp.add, masses)
    values = 0.0
    for ref, mass, (_, _, unit) in zip(refs, masses, stats):
        values = values + ref[:dims, at].astype(I32).astype(F32) * (mass / total * unit)
    return values, top, total


def merge_kernel(inputs, *refs):
    parts, outs = refs[:inputs], refs[inputs:]
    dims = parts[0].shape[0] - STAT_ROWS
    width = outs[0].shape[1]
    step = min(width, 2 * LANES)
    for i, out in reversed(list(enumerate(outs))):
        for at in range(0, width, step):
            encode(out, at, *merged_part(parts, dims, slice(i * width + at, i * width + at + step)))


def merge(parts, pieces):
    rows, width = parts[0].shape
    shape = jax.ShapeDtypeStruct((rows, width // pieces), I16)
    return pl.pallas_call(
        functools.partial(merge_kernel, len(parts)),
        out_shape=(shape,) * pieces,
        in_specs=[VMEM] * len(parts),
        out_specs=(VMEM,) * pieces,
        compiler_params=SMALL,
    )(*parts)


def finish_kernel(group, inputs, *refs):
    parts, (mine, other) = refs[:inputs], refs[inputs:]
    dims = parts[0].shape[0] - STAT_ROWS
    own_rows = mine.shape[0]
    chip_rows = CORES * own_rows
    width = group * chip_rows
    for h in range(parts[0].shape[1] // width):
        values, _, _ = merged_part(parts, dims, slice(h * width, (h + 1) * width))
        rows = values.T
        for g in range(group):
            at = (h * group + g) * dims
            tokens = rows[g * chip_rows : (g + 1) * chip_rows]
            mine[:, at : at + dims] = tokens[:own_rows].astype(BF16)
            other[:, at : at + dims] = tokens[own_rows:].astype(BF16)


def finish(parts, own_rows, group):
    rows, width = parts[0].shape
    shape = jax.ShapeDtypeStruct((own_rows, width // (CORES * own_rows) * (rows - STAT_ROWS)), BF16)
    return pl.pallas_call(
        functools.partial(finish_kernel, group, len(parts)),
        out_shape=(shape, shape),
        in_specs=[VMEM] * len(parts),
        out_specs=(VMEM, VMEM),
        compiler_params=SMALL,
    )(*parts)


def place_kernel(mine, theirs, out):
    half = mine.shape[1]
    core = lax.axis_index("ctx") % CORES
    out[:, pl.ds(pl.multiple_of(core * half, LANES), half)] = mine[...]
    out[:, pl.ds(pl.multiple_of((1 - core) * half, LANES), half)] = theirs[...]


def place(mine, theirs):
    rows, half = mine.shape
    return pl.pallas_call(
        place_kernel,
        out_shape=jax.ShapeDtypeStruct((rows, CORES * half), BF16),
        in_specs=[VMEM, VMEM],
        out_specs=VMEM,
        compiler_params=SMALL,
    )(mine, theirs)


def per_device(
    queries, cache_keys, cached_value_rows, new_keys, prompt_value_rows, cache_len, prompt_start
):
    width = lax.axis_size("ctx")
    own_rows = queries.shape[0]
    group = queries.shape[1] // cache_keys.shape[1]
    bits = [CORES << i for i in range((width // CORES).bit_length() - 1)]
    orders = (tuple(bits[-1:] + bits[:-1]), tuple(bits[-2:] + bits[:-2]))
    odd = len(bits) % 2
    stages = [(0,)] * odd + [(i, i + 1) for i in range(odd, len(bits), 2)]

    def swap(x):
        return lax.ppermute(x, "ctx", [(i, i ^ 1) for i in range(width)])

    def partners(stage):
        return [
            [sum(order[bit] for k, bit in enumerate(stage) if c >> k & 1) for order in orders]
            for c in range(1, 1 << len(stage))
        ]

    def exchange(x, distance):
        return lax.ppermute(x, "ctx", [(i, i ^ distance[i % CORES]) for i in range(width)])

    def own_half(x):
        half = x.shape[1] // CORES
        return lax.dynamic_slice_in_dim(x, core * half, half, 1)

    core = lax.axis_index("ctx") % CORES
    held = join(cache_len, swap(cache_len), own_half(queries), swap(queries))
    fresh = jnp.concatenate([new_keys, prompt_value_rows], axis=0)
    cache_keys, cached_value_rows, fresh, held = lax.optimization_barrier(
        (cache_keys, cached_value_rows, fresh, held)
    )
    fresh = [fresh, swap(fresh)]
    cache = [y for x in (cache_keys, cached_value_rows) for y in (own_half(x), swap(x))]
    for stage in stages:
        gathered = [held] + [exchange(held, distance) for distance in partners(stage)]
        if stage != stages[-1]:
            held = jnp.concatenate(gathered, axis=0)
    half = len(gathered) // 2
    far, near = (
        attend(prompt_start, gathered, chosen, fresh, cache, own_rows=own_rows, orders=orders)
        for chosen in ((half, 2 * half), (0, half))
    )
    last = len(bits) - 1
    parts = [near, exchange(far, partners((last,))[0])]
    for stage in [(i - 1, i) if i else (i,) for i in range(last - 1, -1, -2)]:
        parts = merge(parts, 1 << len(stage))
        parts = [parts[0]] + [exchange(x, distance) for x, distance in zip(parts[1:], partners(stage))]
    mine, other = finish(parts, own_rows, group)
    return place(mine, swap(other))


def solution(mesh):
    return jax.shard_map(
        per_device,
        mesh=mesh,
        in_specs=(
            P(("groups", "ctx"), None),
            P(("groups", "ctx"), None),
            P(("groups", "ctx"), None),
            P(("groups", "ctx"), None),
            P(("groups", "ctx"), None),
            P(("groups", "ctx")),
            P("groups"),
        ),
        out_specs=P(("groups", "ctx"), None),
        check_vma=False,
    )
```

```python
import functools
import math

import jax
import jax.numpy as jnp
from jax import lax
from jax.experimental import pallas as pl
from jax.experimental.pallas import tpu as pltpu
from jax.sharding import PartitionSpec as P

KEY_VALUE_HEADS = 4
LANES = 128
CORES = 2
FLOOR = -1e30
TILE = 256
ATTEND_BYTES = 32 << 20
STAT_ROWS = 16
CHUNK_BLOCKS = 2
STEP = 2.0**15
MARGIN = 0.9998
F32 = jnp.float32
BF16 = jnp.bfloat16
I16 = jnp.int16
I32 = jnp.int32
VMEM = pl.BlockSpec(memory_space=pltpu.VMEM)
SMEM = pl.BlockSpec(memory_space=pltpu.SMEM)
SMALL = pltpu.CompilerParams(vmem_limit_bytes=8 << 20)


def encode(out, at, values, top, total):
    dims, width = values.shape
    largest = jnp.max(jnp.abs(values), axis=0, keepdims=True)
    exponent = jnp.floor(jnp.log2(jnp.maximum(largest, 1e-30))) + 1.0
    fixed = jnp.floor(values * (jnp.exp2(15.0 - exponent) * MARGIN) + 0.5)
    size = jnp.abs(top)
    level = jnp.zeros_like(top)
    scaled = top
    for i in range(1, 9):
        above = size >= STEP**i
        level = level + jnp.where(above, 1.0, 0.0)
        scaled = scaled * jnp.where(above, 1.0 / STEP, 1.0)
    a = jnp.floor(scaled)
    rest = (scaled - a) * STEP
    b = jnp.floor(rest)
    c = jnp.floor((rest - b) * STEP)
    logs = jnp.log2(total) * 1024.0
    la = jnp.floor(logs)
    lb = jnp.floor((logs - la) * STEP)
    row = lax.broadcasted_iota(I32, (STAT_ROWS, width), 0)
    stats = jnp.zeros((STAT_ROWS, width), F32)
    for i, part in enumerate((level, a, b, c, exponent, la, lb)):
        stats = jnp.where(row == i, part, stats)
    if not isinstance(at, int):
        at = pl.multiple_of(at, LANES)
    out[:dims, pl.ds(at, width)] = fixed.astype(I32).astype(I16)
    out[dims:, pl.ds(at, width)] = stats.astype(I32).astype(I16)


def decode_stats(ref, dims, at):
    stats = ref[dims:, at].astype(I32).astype(F32)

    def part(i):
        return stats[i : i + 1, :]

    top = part(1) + (part(2) + part(3) * (1.0 / STEP)) * (1.0 / STEP)
    for i in range(1, 9):
        top = top * jnp.where(part(0) >= i, STEP, 1.0)
    total = jnp.exp2((part(5) + part(6) * (1.0 / STEP)) * (1.0 / 1024.0))
    return top, total, jnp.exp2(part(4) - 15.0) * (1.0 / MARGIN)


def join_kernel(length, length_other, start, mine, queries_other, out):
    rows, half = mine.shape
    core = lax.axis_index("ctx") % CORES
    other = queries_other[:, pl.ds(pl.multiple_of(core * half, LANES), half)]
    out[:, :half] = jnp.concatenate([mine[...].astype(F32), other.astype(F32)], axis=0).astype(BF16)
    lane = lax.broadcasted_iota(I32, (CORES * rows, LANES), 1)
    row = lax.broadcasted_iota(I32, (CORES * rows, LANES), 0)
    count = jnp.where(row < rows, length[0], length_other[0])
    digits = (count // LANES, count % LANES, start[0] // LANES**2, start[0] // LANES % LANES, start[0] % LANES)
    coded = jnp.zeros_like(count)
    for i, digit in enumerate(digits):
        coded = jnp.where(lane == i, digit, coded)
    out[:, half:] = coded.astype(F32).astype(BF16)


def join(length, length_other, start, mine, queries_other):
    rows, half = mine.shape
    return pl.pallas_call(
        join_kernel,
        out_shape=jax.ShapeDtypeStruct((CORES * rows, half + LANES), BF16),
        in_specs=[SMEM, SMEM, SMEM, VMEM, VMEM],
        out_specs=VMEM,
        compiler_params=SMALL,
    )(length, length_other, start, mine, queries_other)


def attend_kernel(sizes, *refs):
    own_rows, orders, group, kv_heads, sets, first, chosen = sizes
    gathered = refs[:sets]
    fresh_a, fresh_b, keys_a, keys_b, values_a, values_b = refs[sets : 6 + sets]
    out, query_t, scores, sums, tops, totals = refs[6 + sets :]
    queries = gathered[first : first + chosen]
    chip_rows = CORES * own_rows
    slots = keys_a.shape[0]
    count = gathered[0].shape[0]
    tokens = min(count, CHUNK_BLOCKS * chip_rows)
    blocks = tokens // chip_rows
    set_blocks = count // chip_rows
    set_lanes = tokens * group
    lanes = chosen * set_lanes
    me = lax.axis_index("ctx")
    core, chip = me % CORES, me // CORES
    factor = math.log2(math.e) / math.sqrt(LANES)
    heads = range(kv_heads)

    steps = [jnp.where(core == 0, a // CORES, b // CORES) for a, b in zip(*orders)]

    def origin(block):
        off = jnp.zeros_like(block)
        for i, step in enumerate(steps):
            off = off ^ jnp.where((block >> i) & 1 == 1, step, 0)
        return chip ^ off

    found = [0.0, 0.0, 0.0, 0.0]
    for i, ref in enumerate(gathered):
        rows = ref.shape[0]
        lane = lax.broadcasted_iota(I32, (rows, LANES), 1)
        row = lax.broadcasted_iota(I32, (rows, LANES), 0)
        place = origin(row // chip_rows + i * set_blocks)
        inside = row % chip_rows
        unit = jnp.where((lane == 0) | (lane == 3), float(LANES), jnp.where(lane == 2, float(LANES**2), 1.0))
        counts = jnp.where(inside % own_rows == 0, unit * ref[:, ref.shape[1] - LANES :].astype(F32), 0.0)
        of_length, of_start = lane < 2, (lane >= 2) & (lane < 5)
        here = place == chip
        second = inside >= own_rows
        chosen_rows = (of_length & (place < chip), of_length & here & ~second, of_length & here & second)
        for k, wanted in enumerate(chosen_rows + (of_start & here & ~second,)):
            found[k] = found[k] + jnp.sum(jnp.where(wanted, counts, 0.0), axis=0, keepdims=True)
    row = lax.broadcasted_iota(I32, (8, LANES), 0)
    found = functools.reduce(lambda x, k: jnp.where(row == k, found[k], x), range(4), jnp.zeros((8, LANES), F32))
    found = jnp.sum(found, axis=1, keepdims=True).astype(I32)
    before, length, start = found[0, 0], [found[1, 0], found[2, 0]], found[3, 0]
    begins = [
        before + jnp.where(core == 1, length[1], 0),
        before + jnp.where(core == 0, length[0], 0),
    ]
    limits = [jnp.clip(jnp.minimum(n, start - at), 0, slots) for n, at in zip(length, begins)]

    def attend_chunk(chunk, carry):
        key_row = lax.broadcasted_iota(I32, (chip_rows, lanes), 0)
        lane = lax.broadcasted_iota(I32, (chip_rows, lanes), 1)
        part = key_row // own_rows
        key_id = (chip * CORES + (core ^ part)) * own_rows + key_row % own_rows
        inside = lane % chip_rows
        block = (lane // set_lanes + first) * set_blocks + lane % set_lanes // (group * chip_rows) + chunk * blocks
        token = (origin(block) * CORES + (core ^ (inside // own_rows))) * own_rows + inside % own_rows
        causal = key_id <= token
        nothing = jnp.zeros((16 - chip_rows % 16, LANES), F32)
        fresh_scores, fresh_values = [], []

        for h in heads:
            rows = pl.ds(pl.multiple_of(chunk * tokens, tokens), tokens)
            q = jnp.concatenate(
                [
                    ref[rows, (h * group + g) * LANES : (h * group + g + 1) * LANES].astype(F32)[b * chip_rows :][:chip_rows]
                    for ref in queries
                    for b in range(blocks)
                    for g in range(group)
                ],
                axis=0,
            )
            query_t[h] = q.T.astype(BF16)
            at = pl.multiple_of((core * kv_heads + h) * LANES, LANES)

            mine = fresh_a[:, pl.ds(at, LANES)].astype(F32)
            theirs = fresh_b[:, pl.ds(at, LANES)].astype(F32)
            new_keys = jnp.concatenate([mine[:own_rows], theirs[:own_rows], nothing], 0).astype(BF16)
            new_values = jnp.concatenate([mine[own_rows:], theirs[own_rows:], nothing], 0).astype(BF16)
            fresh_values.append(new_values)
            fresh_scores.append(jnp.dot(new_keys, query_t[h], preferred_element_type=F32)[:chip_rows] * factor)

        def fold(tile, combine):
            return combine(tile.reshape(tile.shape[0] // 8, 8, lanes), axis=0)

        tn = (((0,), (0,)), ((), ()))

        def shard(s, keys, values, tiles):
            seen = causal & (part == s)
            filled = limits[s] - (tiles - 1) * TILE

            def columns(h):
                return pl.ds(pl.multiple_of((core * kv_heads * LANES if s else 0) + h * LANES, LANES), LANES)

            pieces = [slice(0, (tiles - 1) * TILE)] * (tiles > 1) + [slice((tiles - 1) * TILE, tiles * TILE)] * (tiles > 0)
            top = []
            for h in heads:
                peak = jnp.where(seen, fresh_scores[h], FLOOR)
                for rows in pieces:
                    tile = jnp.dot(keys[rows, columns(h)], query_t[h], preferred_element_type=F32) * factor
                    if rows is pieces[-1]:
                        tile = jnp.where(lax.broadcasted_iota(I32, tile.shape, 0) < filled, tile, FLOOR)
                    scores[h, rows, :] = tile
                    peak = jnp.maximum(peak, fold(tile, jnp.max))
                top.append(jnp.max(peak, axis=0, keepdims=True))
            for h in heads:
                weight = jnp.where(seen, jnp.exp2(fresh_scores[h] - top[h]), 0.0)
                padded = jnp.concatenate([weight, jnp.zeros((16 - chip_rows % 16, lanes), F32)], 0).astype(BF16)
                summed = lax.dot_general(fresh_values[h], padded, tn, preferred_element_type=F32)
                mass = weight
                for rows in pieces:
                    weight = jnp.exp2(scores[h, rows, :] - top[h])
                    if rows is pieces[-1]:
                        weight = jnp.where(lax.broadcasted_iota(I32, weight.shape, 0) < filled, weight, 0.0)
                    summed = summed + lax.dot_general(
                        values[rows, columns(h)], weight.astype(BF16), tn, preferred_element_type=F32
                    )
                    mass = mass + fold(weight, jnp.sum)
                sums[s, h] = summed
                tops[s, h] = top[h]
                totals[s, h] = jnp.sum(mass, axis=0, keepdims=True)

        for s, (keys, values) in enumerate(((keys_a, values_a), (keys_b, values_b))):
            needed = (limits[s] + TILE - 1) // TILE
            for tiles in range(slots // TILE + 1):
                pl.when(needed == tiles)(functools.partial(shard, s, keys, values, tiles))

        for h in heads:
            top_a, top_b = tops[0, h], tops[1, h]
            top = jnp.maximum(top_a, top_b)
            scale_a = jnp.exp2(top_a - top)
            scale_b = jnp.exp2(top_b - top)
            total = jnp.maximum(totals[0, h] * scale_a + totals[1, h] * scale_b, 1.0)
            merged = sums[0, h] * (scale_a / total) + sums[1, h] * (scale_b / total)
            width = group * chip_rows
            for i in range(chosen):
                for b in range(blocks):
                    at = i * set_lanes + b * width
                    cut = slice(at, at + width)
                    place = ((i * set_blocks + chunk * blocks + b) * kv_heads + h) * width
                    encode(out, place, merged[:, cut], top[:, cut], total[:, cut])
        return carry

    chunks = count // tokens
    if chunks == 1:
        attend_chunk(0, 0)
    else:
        lax.fori_loop(0, chunks, attend_chunk, 0)


def attend(gathered, chosen, fresh, cache, *, own_rows, orders):
    first, end = chosen
    count = gathered[0].shape[0]
    chip_rows = CORES * own_rows
    tokens = min(count, CHUNK_BLOCKS * chip_rows)
    slots = cache[0].shape[0]
    kv_heads = cache[0].shape[1] // LANES
    heads = gathered[0].shape[1] // LANES - 1
    group = heads // kv_heads
    lanes = (end - first) * tokens * group
    sizes = (own_rows, orders, group, kv_heads, len(gathered), first, end - first)
    return pl.pallas_call(
        functools.partial(attend_kernel, sizes),
        out_shape=jax.ShapeDtypeStruct((LANES + STAT_ROWS, (end - first) * count * heads), I16),
        in_specs=[VMEM] * (len(gathered) + 6),
        out_specs=VMEM,
        scratch_shapes=[
            pltpu.VMEM((kv_heads, LANES, lanes), BF16),
            pltpu.VMEM((kv_heads, slots, lanes), F32),
            pltpu.VMEM((2, kv_heads, LANES, lanes), F32),
            pltpu.VMEM((2, kv_heads, 1, lanes), F32),
            pltpu.VMEM((2, kv_heads, 1, lanes), F32),
        ],
        compiler_params=pltpu.CompilerParams(vmem_limit_bytes=ATTEND_BYTES),
    )(*gathered, *fresh, *cache)


def merged_part(refs, dims, at):
    stats = [decode_stats(ref, dims, at) for ref in refs]
    top = functools.reduce(jnp.maximum, [x[0] for x in stats])
    masses = [x[1] * jnp.exp2(x[0] - top) for x in stats]
    total = functools.reduce(jnp.add, masses)
    values = 0.0
    for ref, mass, (_, _, unit) in zip(refs, masses, stats):
        values = values + ref[:dims, at].astype(I32).astype(F32) * (mass / total * unit)
    return values, top, total


def merge_kernel(inputs, *refs):
    parts, outs = refs[:inputs], refs[inputs:]
    dims = parts[0].shape[0] - STAT_ROWS
    width = outs[0].shape[1]
    step = min(width, 2 * LANES)
    for i, out in reversed(list(enumerate(outs))):
        for at in range(0, width, step):
            encode(out, at, *merged_part(parts, dims, slice(i * width + at, i * width + at + step)))


def merge(parts, pieces):
    rows, width = parts[0].shape
    shape = jax.ShapeDtypeStruct((rows, width // pieces), I16)
    return pl.pallas_call(
        functools.partial(merge_kernel, len(parts)),
        out_shape=(shape,) * pieces,
        in_specs=[VMEM] * len(parts),
        out_specs=(VMEM,) * pieces,
        compiler_params=SMALL,
    )(*parts)


def finish_kernel(group, inputs, *refs):
    parts, (mine, other) = refs[:inputs], refs[inputs:]
    dims = parts[0].shape[0] - STAT_ROWS
    own_rows = mine.shape[0]
    chip_rows = CORES * own_rows
    width = group * chip_rows
    for h in range(parts[0].shape[1] // width):
        values, _, _ = merged_part(parts, dims, slice(h * width, (h + 1) * width))
        rows = values.T
        for g in range(group):
            at = (h * group + g) * dims
            tokens = rows[g * chip_rows : (g + 1) * chip_rows]
            mine[:, at : at + dims] = tokens[:own_rows].astype(BF16)
            other[:, at : at + dims] = tokens[own_rows:].astype(BF16)


def finish(parts, own_rows, group):
    rows, width = parts[0].shape
    shape = jax.ShapeDtypeStruct((own_rows, width // (CORES * own_rows) * (rows - STAT_ROWS)), BF16)
    return pl.pallas_call(
        functools.partial(finish_kernel, group, len(parts)),
        out_shape=(shape, shape),
        in_specs=[VMEM] * len(parts),
        out_specs=(VMEM, VMEM),
        compiler_params=SMALL,
    )(*parts)


def place_kernel(mine, theirs, out):
    half = mine.shape[1]
    core = lax.axis_index("ctx") % CORES
    out[:, pl.ds(pl.multiple_of(core * half, LANES), half)] = mine[...]
    out[:, pl.ds(pl.multiple_of((1 - core) * half, LANES), half)] = theirs[...]


def place(mine, theirs):
    rows, half = mine.shape
    return pl.pallas_call(
        place_kernel,
        out_shape=jax.ShapeDtypeStruct((rows, CORES * half), BF16),
        in_specs=[VMEM, VMEM],
        out_specs=VMEM,
        compiler_params=SMALL,
    )(mine, theirs)


def per_device(
    queries, cache_keys, cached_value_rows, new_keys, prompt_value_rows, cache_len, prompt_start
):
    width = lax.axis_size("ctx")
    own_rows = queries.shape[0]
    group = queries.shape[1] // cache_keys.shape[1]
    bits = [CORES << i for i in range((width // CORES).bit_length() - 1)]
    orders = (tuple(bits[-1:] + bits[:-1]), tuple(bits[-2:] + bits[:-2]))
    odd = len(bits) % 2
    stages = [(0,)] * odd + [(i, i + 1) for i in range(odd, len(bits), 2)]

    def swap(x):
        return lax.ppermute(x, "ctx", [(i, i ^ 1) for i in range(width)])

    def partners(stage):
        return [
            [sum(order[bit] for k, bit in enumerate(stage) if c >> k & 1) for order in orders]
            for c in range(1, 1 << len(stage))
        ]

    def exchange(x, distance):
        return lax.ppermute(x, "ctx", [(i, i ^ distance[i % CORES]) for i in range(width)])

    def own_half(x):
        half = x.shape[1] // CORES
        return lax.dynamic_slice_in_dim(x, core * half, half, 1)

    core = lax.axis_index("ctx") % CORES
    held = join(cache_len, swap(cache_len), prompt_start, own_half(queries), swap(queries))
    cache_keys, cached_value_rows, held = lax.optimization_barrier((cache_keys, cached_value_rows, held))
    cache = [y for x in (cache_keys, cached_value_rows) for y in (own_half(x), swap(x))]
    for stage in stages:
        gathered = [held] + [exchange(held, distance) for distance in partners(stage)]
        if stage != stages[-1]:
            held = jnp.concatenate(gathered, axis=0)
    gathered[-1], new_keys, prompt_value_rows = lax.optimization_barrier((gathered[-1], new_keys, prompt_value_rows))
    fresh = jnp.concatenate([new_keys, prompt_value_rows], axis=0)
    fresh = [fresh, swap(fresh)]
    half = len(gathered) // 2
    far, near = (
        attend(gathered, chosen, fresh, cache, own_rows=own_rows, orders=orders)
        for chosen in ((half, 2 * half), (0, half))
    )
    last = len(bits) - 1
    parts = [near, exchange(far, partners((last,))[0])]
    for stage in [(i - 1, i) if i else (i,) for i in range(last - 1, -1, -2)]:
        parts = merge(parts, 1 << len(stage))
        parts = [parts[0]] + [exchange(x, distance) for x, distance in zip(parts[1:], partners(stage))]
    mine, other = finish(parts, own_rows, group)
    return place(mine, swap(other))


def solution(mesh):
    return jax.shard_map(
        per_device,
        mesh=mesh,
        in_specs=(
            P(("groups", "ctx"), None),
            P(("groups", "ctx"), None),
            P(("groups", "ctx"), None),
            P(("groups", "ctx"), None),
            P(("groups", "ctx"), None),
            P(("groups", "ctx")),
            P("groups"),
        ),
        out_specs=P(("groups", "ctx"), None),
        check_vma=False,
    )
```

```python
import functools
import math

import jax
import jax.numpy as jnp
from jax import lax
from jax.experimental import pallas as pl
from jax.experimental.pallas import tpu as pltpu
from jax.sharding import PartitionSpec as P

KEY_VALUE_HEADS = 4
LANES = 128
CORES = 2
FLOOR = -1e30
TILE = 256
ATTEND_BYTES = 32 << 20
STAT_ROWS = 16
CHUNK_BLOCKS = 2
STEP = 2.0**15
MARGIN = 0.9998
F32 = jnp.float32
BF16 = jnp.bfloat16
I16 = jnp.int16
I32 = jnp.int32
VMEM = pl.BlockSpec(memory_space=pltpu.VMEM)
SMEM = pl.BlockSpec(memory_space=pltpu.SMEM)
SMALL = pltpu.CompilerParams(vmem_limit_bytes=8 << 20)


def encode(out, at, values, top, total):
    dims, width = values.shape
    largest = jnp.max(jnp.abs(values), axis=0, keepdims=True)
    exponent = jnp.floor(jnp.log2(jnp.maximum(largest, 1e-30))) + 1.0
    fixed = jnp.floor(values * (jnp.exp2(15.0 - exponent) * MARGIN) + 0.5)
    size = jnp.abs(top)
    level = jnp.zeros_like(top)
    scaled = top
    for i in range(1, 9):
        above = size >= STEP**i
        level = level + jnp.where(above, 1.0, 0.0)
        scaled = scaled * jnp.where(above, 1.0 / STEP, 1.0)
    a = jnp.floor(scaled)
    rest = (scaled - a) * STEP
    b = jnp.floor(rest)
    c = jnp.floor((rest - b) * STEP)
    logs = jnp.log2(total) * 1024.0
    la = jnp.floor(logs)
    lb = jnp.floor((logs - la) * STEP)
    row = lax.broadcasted_iota(I32, (STAT_ROWS, width), 0)
    stats = jnp.zeros((STAT_ROWS, width), F32)
    for i, part in enumerate((level, a, b, c, exponent, la, lb)):
        stats = jnp.where(row == i, part, stats)
    if not isinstance(at, int):
        at = pl.multiple_of(at, LANES)
    out[:dims, pl.ds(at, width)] = fixed.astype(I32).astype(I16)
    out[dims:, pl.ds(at, width)] = stats.astype(I32).astype(I16)


def decode_stats(ref, dims, at):
    stats = ref[dims:, at].astype(I32).astype(F32)

    def part(i):
        return stats[i : i + 1, :]

    top = part(1) + (part(2) + part(3) * (1.0 / STEP)) * (1.0 / STEP)
    for i in range(1, 9):
        top = top * jnp.where(part(0) >= i, STEP, 1.0)
    total = jnp.exp2((part(5) + part(6) * (1.0 / STEP)) * (1.0 / 1024.0))
    return top, total, jnp.exp2(part(4) - 15.0) * (1.0 / MARGIN)


def join_kernel(length, length_other, start, mine, queries_other, out):
    rows, half = mine.shape
    core = lax.axis_index("ctx") % CORES
    other = queries_other[:, pl.ds(pl.multiple_of(core * half, LANES), half)]
    out[:, :half] = jnp.concatenate([mine[...].astype(F32), other.astype(F32)], axis=0).astype(BF16)
    lane = lax.broadcasted_iota(I32, (CORES * rows, LANES), 1)
    row = lax.broadcasted_iota(I32, (CORES * rows, LANES), 0)
    count = jnp.where(row < rows, length[0], length_other[0])
    digits = (count // LANES, count % LANES, start[0] // LANES**2, start[0] // LANES % LANES, start[0] % LANES)
    coded = jnp.zeros_like(count)
    for i, digit in enumerate(digits):
        coded = jnp.where(lane == i, digit, coded)
    out[:, half:] = coded.astype(F32).astype(BF16)


def join(length, length_other, start, mine, queries_other):
    rows, half = mine.shape
    return pl.pallas_call(
        join_kernel,
        out_shape=jax.ShapeDtypeStruct((CORES * rows, half + LANES), BF16),
        in_specs=[SMEM, SMEM, SMEM, VMEM, VMEM],
        out_specs=VMEM,
        compiler_params=SMALL,
    )(length, length_other, start, mine, queries_other)


def attend_kernel(sizes, *refs):
    own_rows, orders, group, kv_heads, sets, first, chosen = sizes
    gathered = refs[:sets]
    fresh_a, fresh_b, keys_a, keys_b, values_a, values_b = refs[sets : 6 + sets]
    out, query_t, scores, sums, tops, totals = refs[6 + sets :]
    queries = gathered[first : first + chosen]
    chip_rows = CORES * own_rows
    slots = keys_a.shape[0]
    count = gathered[0].shape[0]
    tokens = min(count, CHUNK_BLOCKS * chip_rows)
    blocks = tokens // chip_rows
    set_blocks = count // chip_rows
    set_lanes = tokens * group
    lanes = chosen * set_lanes
    me = lax.axis_index("ctx")
    core, chip = me % CORES, me // CORES
    factor = math.log2(math.e) / math.sqrt(LANES)
    heads = range(kv_heads)

    steps = [jnp.where(core == 0, a // CORES, b // CORES) for a, b in zip(*orders)]

    def origin(block):
        off = jnp.zeros_like(block)
        for i, step in enumerate(steps):
            off = off ^ jnp.where((block >> i) & 1 == 1, step, 0)
        return chip ^ off

    found = [0.0, 0.0, 0.0, 0.0]
    for i, ref in enumerate(gathered):
        rows = ref.shape[0]
        lane = lax.broadcasted_iota(I32, (rows, LANES), 1)
        row = lax.broadcasted_iota(I32, (rows, LANES), 0)
        place = origin(row // chip_rows + i * set_blocks)
        inside = row % chip_rows
        unit = jnp.where((lane == 0) | (lane == 3), float(LANES), jnp.where(lane == 2, float(LANES**2), 1.0))
        counts = jnp.where(inside % own_rows == 0, unit * ref[:, ref.shape[1] - LANES :].astype(F32), 0.0)
        of_length, of_start = lane < 2, (lane >= 2) & (lane < 5)
        here = place == chip
        second = inside >= own_rows
        chosen_rows = (of_length & (place < chip), of_length & here & ~second, of_length & here & second)
        for k, wanted in enumerate(chosen_rows + (of_start & here & ~second,)):
            found[k] = found[k] + jnp.sum(jnp.where(wanted, counts, 0.0), axis=0, keepdims=True)
    row = lax.broadcasted_iota(I32, (8, LANES), 0)
    found = functools.reduce(lambda x, k: jnp.where(row == k, found[k], x), range(4), jnp.zeros((8, LANES), F32))
    found = jnp.sum(found, axis=1, keepdims=True).astype(I32)
    before, length, start = found[0, 0], [found[1, 0], found[2, 0]], found[3, 0]
    begins = [
        before + jnp.where(core == 1, length[1], 0),
        before + jnp.where(core == 0, length[0], 0),
    ]
    limits = [jnp.clip(jnp.minimum(n, start - at), 0, slots) for n, at in zip(length, begins)]

    def attend_chunk(chunk, carry):
        key_row = lax.broadcasted_iota(I32, (chip_rows, lanes), 0)
        lane = lax.broadcasted_iota(I32, (chip_rows, lanes), 1)
        part = key_row // own_rows
        key_id = (chip * CORES + (core ^ part)) * own_rows + key_row % own_rows
        inside = lane % chip_rows
        block = (lane // set_lanes + first) * set_blocks + lane % set_lanes // (group * chip_rows) + chunk * blocks
        token = (origin(block) * CORES + (core ^ (inside // own_rows))) * own_rows + inside % own_rows
        causal = key_id <= token
        nothing = jnp.zeros((16 - chip_rows % 16, LANES), F32)
        fresh_scores, fresh_values = [], []

        for h in heads:
            rows = pl.ds(pl.multiple_of(chunk * tokens, tokens), tokens)
            q = jnp.concatenate(
                [
                    ref[rows, (h * group + g) * LANES : (h * group + g + 1) * LANES].astype(F32)[b * chip_rows :][:chip_rows]
                    for ref in queries
                    for b in range(blocks)
                    for g in range(group)
                ],
                axis=0,
            )
            query_t[h] = q.T.astype(BF16)
            at = pl.multiple_of((core * kv_heads + h) * LANES, LANES)

            mine = fresh_a[:, pl.ds(at, LANES)].astype(F32)
            theirs = fresh_b[:, pl.ds(at, LANES)].astype(F32)
            new_keys = jnp.concatenate([mine[:own_rows], theirs[:own_rows], nothing], 0).astype(BF16)
            new_values = jnp.concatenate([mine[own_rows:], theirs[own_rows:], nothing], 0).astype(BF16)
            fresh_values.append(new_values)
            fresh_scores.append(jnp.dot(new_keys, query_t[h], preferred_element_type=F32)[:chip_rows] * factor)

        def fold(tile, combine):
            return combine(tile.reshape(tile.shape[0] // 8, 8, lanes), axis=0)

        tn = (((0,), (0,)), ((), ()))

        def shard(s, keys, values, tiles):
            seen = causal & (part == s)
            filled = limits[s] - (tiles - 1) * TILE

            def columns(h):
                return pl.ds(pl.multiple_of((core * kv_heads * LANES if s else 0) + h * LANES, LANES), LANES)

            pieces = [slice(0, (tiles - 1) * TILE)] * (tiles > 1) + [slice((tiles - 1) * TILE, tiles * TILE)] * (tiles > 0)
            top = []
            for h in heads:
                peak = jnp.where(seen, fresh_scores[h], FLOOR)
                for rows in pieces:
                    tile = jnp.dot(keys[rows, columns(h)], query_t[h], preferred_element_type=F32) * factor
                    if rows is pieces[-1]:
                        tile = jnp.where(lax.broadcasted_iota(I32, tile.shape, 0) < filled, tile, FLOOR)
                    scores[h, rows, :] = tile
                    peak = jnp.maximum(peak, fold(tile, jnp.max))
                top.append(jnp.max(peak, axis=0, keepdims=True))
            for h in heads:
                weight = jnp.where(seen, jnp.exp2(fresh_scores[h] - top[h]), 0.0)
                padded = jnp.concatenate([weight, jnp.zeros((16 - chip_rows % 16, lanes), F32)], 0).astype(BF16)
                summed = lax.dot_general(fresh_values[h], padded, tn, preferred_element_type=F32)
                mass = weight
                for rows in pieces:
                    weight = jnp.exp2(scores[h, rows, :] - top[h])
                    if rows is pieces[-1]:
                        weight = jnp.where(lax.broadcasted_iota(I32, weight.shape, 0) < filled, weight, 0.0)
                    summed = summed + lax.dot_general(
                        values[rows, columns(h)], weight.astype(BF16), tn, preferred_element_type=F32
                    )
                    mass = mass + fold(weight, jnp.sum)
                sums[s, h] = summed
                tops[s, h] = top[h]
                totals[s, h] = jnp.sum(mass, axis=0, keepdims=True)

        for s, (keys, values) in enumerate(((keys_a, values_a), (keys_b, values_b))):
            needed = (limits[s] + TILE - 1) // TILE
            for tiles in range(slots // TILE + 1):
                pl.when(needed == tiles)(functools.partial(shard, s, keys, values, tiles))

        for h in heads:
            top_a, top_b = tops[0, h], tops[1, h]
            top = jnp.maximum(top_a, top_b)
            scale_a = jnp.exp2(top_a - top)
            scale_b = jnp.exp2(top_b - top)
            total = jnp.maximum(totals[0, h] * scale_a + totals[1, h] * scale_b, 1.0)
            merged = sums[0, h] * (scale_a / total) + sums[1, h] * (scale_b / total)
            width = group * chip_rows
            for i in range(chosen):
                for b in range(blocks):
                    at = i * set_lanes + b * width
                    cut = slice(at, at + width)
                    place = ((i * set_blocks + chunk * blocks + b) * kv_heads + h) * width
                    encode(out, place, merged[:, cut], top[:, cut], total[:, cut])
        return carry

    chunks = count // tokens
    if chunks == 1:
        attend_chunk(0, 0)
    else:
        lax.fori_loop(0, chunks, attend_chunk, 0)


def attend(gathered, chosen, fresh, cache, *, own_rows, orders):
    first, end = chosen
    count = gathered[0].shape[0]
    chip_rows = CORES * own_rows
    tokens = min(count, CHUNK_BLOCKS * chip_rows)
    slots = cache[0].shape[0]
    kv_heads = cache[0].shape[1] // LANES
    heads = gathered[0].shape[1] // LANES - 1
    group = heads // kv_heads
    lanes = (end - first) * tokens * group
    sizes = (own_rows, orders, group, kv_heads, len(gathered), first, end - first)
    return pl.pallas_call(
        functools.partial(attend_kernel, sizes),
        out_shape=jax.ShapeDtypeStruct((LANES + STAT_ROWS, (end - first) * count * heads), I16),
        in_specs=[VMEM] * (len(gathered) + 6),
        out_specs=VMEM,
        scratch_shapes=[
            pltpu.VMEM((kv_heads, LANES, lanes), BF16),
            pltpu.VMEM((kv_heads, slots, lanes), F32),
            pltpu.VMEM((2, kv_heads, LANES, lanes), F32),
            pltpu.VMEM((2, kv_heads, 1, lanes), F32),
            pltpu.VMEM((2, kv_heads, 1, lanes), F32),
        ],
        compiler_params=pltpu.CompilerParams(vmem_limit_bytes=ATTEND_BYTES),
    )(*gathered, *fresh, *cache)


def merged_part(refs, dims, at):
    stats = [decode_stats(ref, dims, at) for ref in refs]
    top = functools.reduce(jnp.maximum, [x[0] for x in stats])
    masses = [x[1] * jnp.exp2(x[0] - top) for x in stats]
    total = functools.reduce(jnp.add, masses)
    values = 0.0
    for ref, mass, (_, _, unit) in zip(refs, masses, stats):
        values = values + ref[:dims, at].astype(I32).astype(F32) * (mass / total * unit)
    return values, top, total


def merge_kernel(inputs, *refs):
    parts, outs = refs[:inputs], refs[inputs:]
    dims = parts[0].shape[0] - STAT_ROWS
    width = outs[0].shape[1]
    step = min(width, 2 * LANES)
    for i, out in reversed(list(enumerate(outs))):
        for at in range(0, width, step):
            encode(out, at, *merged_part(parts, dims, slice(i * width + at, i * width + at + step)))


def merge(parts, pieces):
    rows, width = parts[0].shape
    shape = jax.ShapeDtypeStruct((rows, width // pieces), I16)
    return pl.pallas_call(
        functools.partial(merge_kernel, len(parts)),
        out_shape=(shape,) * pieces,
        in_specs=[VMEM] * len(parts),
        out_specs=(VMEM,) * pieces,
        compiler_params=SMALL,
    )(*parts)


def finish_kernel(group, inputs, *refs):
    parts, (mine, other) = refs[:inputs], refs[inputs:]
    dims = parts[0].shape[0] - STAT_ROWS
    own_rows = mine.shape[0]
    chip_rows = CORES * own_rows
    width = group * chip_rows
    for h in range(parts[0].shape[1] // width):
        values, _, _ = merged_part(parts, dims, slice(h * width, (h + 1) * width))
        rows = values.T
        for g in range(group):
            at = (h * group + g) * dims
            tokens = rows[g * chip_rows : (g + 1) * chip_rows]
            mine[:, at : at + dims] = tokens[:own_rows].astype(BF16)
            other[:, at : at + dims] = tokens[own_rows:].astype(BF16)


def finish(parts, own_rows, group):
    rows, width = parts[0].shape
    shape = jax.ShapeDtypeStruct((own_rows, width // (CORES * own_rows) * (rows - STAT_ROWS)), BF16)
    return pl.pallas_call(
        functools.partial(finish_kernel, group, len(parts)),
        out_shape=(shape, shape),
        in_specs=[VMEM] * len(parts),
        out_specs=(VMEM, VMEM),
        compiler_params=SMALL,
    )(*parts)


def place_kernel(mine, theirs, out):
    half = mine.shape[1]
    core = lax.axis_index("ctx") % CORES
    out[:, pl.ds(pl.multiple_of(core * half, LANES), half)] = mine[...]
    out[:, pl.ds(pl.multiple_of((1 - core) * half, LANES), half)] = theirs[...]


def place(mine, theirs):
    rows, half = mine.shape
    return pl.pallas_call(
        place_kernel,
        out_shape=jax.ShapeDtypeStruct((rows, CORES * half), BF16),
        in_specs=[VMEM, VMEM],
        out_specs=VMEM,
        compiler_params=SMALL,
    )(mine, theirs)


def per_device(
    queries, cache_keys, cached_value_rows, new_keys, prompt_value_rows, cache_len, prompt_start
):
    width = lax.axis_size("ctx")
    own_rows = queries.shape[0]
    group = queries.shape[1] // cache_keys.shape[1]
    bits = [CORES << i for i in range((width // CORES).bit_length() - 1)]
    orders = (tuple(bits[-1:] + bits[:-1]), tuple(bits[-2:] + bits[:-2]))
    odd = len(bits) % 2
    stages = [(0,)] * odd + [(i, i + 1) for i in range(odd, len(bits), 2)]

    def swap(x):
        return lax.ppermute(x, "ctx", [(i, i ^ 1) for i in range(width)])

    def partners(stage):
        return [
            [sum(order[bit] for k, bit in enumerate(stage) if c >> k & 1) for order in orders]
            for c in range(1, 1 << len(stage))
        ]

    def exchange(x, distance):
        return lax.ppermute(x, "ctx", [(i, i ^ distance[i % CORES]) for i in range(width)])

    def own_half(x):
        half = x.shape[1] // CORES
        return lax.dynamic_slice_in_dim(x, core * half, half, 1)

    core = lax.axis_index("ctx") % CORES
    held = join(cache_len, swap(cache_len), prompt_start, own_half(queries), swap(queries))
    cache_keys, cached_value_rows, held = lax.optimization_barrier((cache_keys, cached_value_rows, held))
    cache = [y for x in (cache_keys, cached_value_rows) for y in (own_half(x), swap(x))]
    for stage in stages:
        gathered = [held] + [exchange(held, distance) for distance in partners(stage)]
        if stage != stages[-1]:
            held = jnp.concatenate(gathered, axis=0)
    gathered[-1], cache[0], cache[2], new_keys, prompt_value_rows = lax.optimization_barrier(
        (gathered[-1], cache[0], cache[2], new_keys, prompt_value_rows)
    )
    fresh = jnp.concatenate([new_keys, prompt_value_rows], axis=0)
    fresh = [fresh, swap(fresh)]
    half = len(gathered) // 2
    far, near = (
        attend(gathered, chosen, fresh, cache, own_rows=own_rows, orders=orders)
        for chosen in ((half, 2 * half), (0, half))
    )
    last = len(bits) - 1
    parts = [near, exchange(far, partners((last,))[0])]
    for stage in [(i - 1, i) if i else (i,) for i in range(last - 1, -1, -2)]:
        parts = merge(parts, 1 << len(stage))
        parts = [parts[0]] + [exchange(x, distance) for x, distance in zip(parts[1:], partners(stage))]
    mine, other = finish(parts, own_rows, group)
    return place(mine, swap(other))


def solution(mesh):
    return jax.shard_map(
        per_device,
        mesh=mesh,
        in_specs=(
            P(("groups", "ctx"), None),
            P(("groups", "ctx"), None),
            P(("groups", "ctx"), None),
            P(("groups", "ctx"), None),
            P(("groups", "ctx"), None),
            P(("groups", "ctx")),
            P("groups"),
        ),
        out_specs=P(("groups", "ctx"), None),
        check_vma=False,
    )
```

```python
import functools
import math

import jax
import jax.numpy as jnp
from jax import lax
from jax.experimental import pallas as pl
from jax.experimental.pallas import tpu as pltpu
from jax.sharding import PartitionSpec as P

KEY_VALUE_HEADS = 4
LANES = 128
CORES = 2
FLOOR = -1e30
TILE = 256
ATTEND_BYTES = 32 << 20
STAT_ROWS = 16
CHUNK_BLOCKS = 2
STEP = 2.0**15
MARGIN = 0.9998
F32 = jnp.float32
BF16 = jnp.bfloat16
I16 = jnp.int16
I32 = jnp.int32
VMEM = pl.BlockSpec(memory_space=pltpu.VMEM)
SMEM = pl.BlockSpec(memory_space=pltpu.SMEM)
SMALL = pltpu.CompilerParams(vmem_limit_bytes=8 << 20)


def encode(out, at, values, top, total):
    dims, width = values.shape
    largest = jnp.max(jnp.abs(values), axis=0, keepdims=True)
    exponent = jnp.floor(jnp.log2(jnp.maximum(largest, 1e-30))) + 1.0
    fixed = jnp.floor(values * (jnp.exp2(15.0 - exponent) * MARGIN) + 0.5)
    size = jnp.abs(top)
    level = jnp.zeros_like(top)
    scaled = top
    for i in range(1, 9):
        above = size >= STEP**i
        level = level + jnp.where(above, 1.0, 0.0)
        scaled = scaled * jnp.where(above, 1.0 / STEP, 1.0)
    a = jnp.floor(scaled)
    rest = (scaled - a) * STEP
    b = jnp.floor(rest)
    c = jnp.floor((rest - b) * STEP)
    logs = jnp.log2(total) * 1024.0
    la = jnp.floor(logs)
    lb = jnp.floor((logs - la) * STEP)
    row = lax.broadcasted_iota(I32, (STAT_ROWS, width), 0)
    stats = jnp.zeros((STAT_ROWS, width), F32)
    for i, part in enumerate((level, a, b, c, exponent, la, lb)):
        stats = jnp.where(row == i, part, stats)
    if not isinstance(at, int):
        at = pl.multiple_of(at, LANES)
    out[:dims, pl.ds(at, width)] = fixed.astype(I32).astype(I16)
    out[dims:, pl.ds(at, width)] = stats.astype(I32).astype(I16)


def decode_stats(ref, dims, at):
    stats = ref[dims:, at].astype(I32).astype(F32)

    def part(i):
        return stats[i : i + 1, :]

    top = part(1) + (part(2) + part(3) * (1.0 / STEP)) * (1.0 / STEP)
    for i in range(1, 9):
        top = top * jnp.where(part(0) >= i, STEP, 1.0)
    total = jnp.exp2((part(5) + part(6) * (1.0 / STEP)) * (1.0 / 1024.0))
    return top, total, jnp.exp2(part(4) - 15.0) * (1.0 / MARGIN)


def join_kernel(length, length_other, mine, queries_other, out):
    rows, half = mine.shape
    core = lax.axis_index("ctx") % CORES
    other = queries_other[:, pl.ds(pl.multiple_of(core * half, LANES), half)]
    out[:, :half] = jnp.concatenate([mine[...].astype(F32), other.astype(F32)], axis=0).astype(BF16)
    lane = lax.broadcasted_iota(I32, (CORES * rows, LANES), 1)
    row = lax.broadcasted_iota(I32, (CORES * rows, LANES), 0)
    count = jnp.where(row < rows, length[0], length_other[0])
    coded = jnp.where(lane == 0, count // LANES, jnp.where(lane == 1, count % LANES, 0))
    out[:, half:] = coded.astype(F32).astype(BF16)


def join(length, length_other, mine, queries_other):
    rows, half = mine.shape
    return pl.pallas_call(
        join_kernel,
        out_shape=jax.ShapeDtypeStruct((CORES * rows, half + LANES), BF16),
        in_specs=[SMEM, SMEM, VMEM, VMEM],
        out_specs=VMEM,
        compiler_params=SMALL,
    )(length, length_other, mine, queries_other)


def attend_kernel(sizes, *refs):
    own_rows, orders, group, kv_heads, sets, first, chosen = sizes
    start = refs[0]
    gathered = refs[1 : 1 + sets]
    fresh_a, fresh_b, keys_a, keys_b, values_a, values_b = refs[1 + sets : 7 + sets]
    out, query_t, scores, sums, tops, totals = refs[7 + sets :]
    queries = gathered[first : first + chosen]
    chip_rows = CORES * own_rows
    slots = keys_a.shape[0]
    count = gathered[0].shape[0]
    tokens = min(count, CHUNK_BLOCKS * chip_rows)
    blocks = tokens // chip_rows
    set_blocks = count // chip_rows
    set_lanes = tokens * group
    lanes = chosen * set_lanes
    me = lax.axis_index("ctx")
    core, chip = me % CORES, me // CORES
    factor = math.log2(math.e) / math.sqrt(LANES)
    heads = range(kv_heads)

    steps = [jnp.where(core == 0, a // CORES, b // CORES) for a, b in zip(*orders)]

    def origin(block):
        off = jnp.zeros_like(block)
        for i, step in enumerate(steps):
            off = off ^ jnp.where((block >> i) & 1 == 1, step, 0)
        return chip ^ off

    found = [0.0, 0.0, 0.0]
    for i, ref in enumerate(gathered):
        rows = ref.shape[0]
        lane = lax.broadcasted_iota(I32, (rows, LANES), 1)
        row = lax.broadcasted_iota(I32, (rows, LANES), 0)
        place = origin(row // chip_rows + i * set_blocks)
        inside = row % chip_rows
        counts = jnp.where(lane == 0, float(LANES), 1.0) * ref[:, ref.shape[1] - LANES :].astype(F32)
        counts = jnp.where((inside % own_rows == 0) & (lane < 2), counts, 0.0)
        here = place == chip
        second = inside >= own_rows
        for k, wanted in enumerate((place < chip, here & ~second, here & second)):
            found[k] = found[k] + jnp.sum(jnp.where(wanted, counts, 0.0), axis=0, keepdims=True)
    row = lax.broadcasted_iota(I32, (8, LANES), 0)
    found = functools.reduce(lambda x, k: jnp.where(row == k, found[k], x), range(3), jnp.zeros((8, LANES), F32))
    found = jnp.sum(found, axis=1, keepdims=True).astype(I32)
    before, length = found[0, 0], [found[1, 0], found[2, 0]]
    begins = [
        before + jnp.where(core == 1, length[1], 0),
        before + jnp.where(core == 0, length[0], 0),
    ]
    limits = [jnp.clip(jnp.minimum(n, start[0] - at), 0, slots) for n, at in zip(length, begins)]

    def attend_chunk(chunk, carry):
        key_row = lax.broadcasted_iota(I32, (chip_rows, lanes), 0)
        lane = lax.broadcasted_iota(I32, (chip_rows, lanes), 1)
        part = key_row // own_rows
        key_id = (chip * CORES + (core ^ part)) * own_rows + key_row % own_rows
        inside = lane % chip_rows
        block = (lane // set_lanes + first) * set_blocks + lane % set_lanes // (group * chip_rows) + chunk * blocks
        token = (origin(block) * CORES + (core ^ (inside // own_rows))) * own_rows + inside % own_rows
        causal = key_id <= token
        nothing = jnp.zeros((16 - chip_rows % 16, LANES), F32)
        fresh_scores, fresh_values = [], []

        for h in heads:
            rows = pl.ds(pl.multiple_of(chunk * tokens, tokens), tokens)
            q = jnp.concatenate(
                [
                    ref[rows, (h * group + g) * LANES : (h * group + g + 1) * LANES].astype(F32)[b * chip_rows :][:chip_rows]
                    for ref in queries
                    for b in range(blocks)
                    for g in range(group)
                ],
                axis=0,
            )
            query_t[h] = q.T.astype(BF16)
            at = pl.multiple_of((core * kv_heads + h) * LANES, LANES)

            mine = fresh_a[:, pl.ds(at, LANES)].astype(F32)
            theirs = fresh_b[:, pl.ds(at, LANES)].astype(F32)
            new_keys = jnp.concatenate([mine[:own_rows], theirs[:own_rows], nothing], 0).astype(BF16)
            new_values = jnp.concatenate([mine[own_rows:], theirs[own_rows:], nothing], 0).astype(BF16)
            fresh_values.append(new_values)
            fresh_scores.append(jnp.dot(new_keys, query_t[h], preferred_element_type=F32)[:chip_rows] * factor)

        def fold(tile, combine):
            return combine(tile.reshape(tile.shape[0] // 8, 8, lanes), axis=0)

        tn = (((0,), (0,)), ((), ()))

        def shard(s, keys, values, tiles):
            seen = causal & (part == s)
            filled = limits[s] - (tiles - 1) * TILE

            def columns(h):
                return pl.ds(pl.multiple_of((core * kv_heads * LANES if s else 0) + h * LANES, LANES), LANES)

            pieces = [slice(0, (tiles - 1) * TILE)] * (tiles > 1) + [slice((tiles - 1) * TILE, tiles * TILE)] * (tiles > 0)
            top = []
            for h in heads:
                peak = jnp.where(seen, fresh_scores[h], FLOOR)
                for rows in pieces:
                    tile = jnp.dot(keys[rows, columns(h)], query_t[h], preferred_element_type=F32) * factor
                    if rows is pieces[-1]:
                        tile = jnp.where(lax.broadcasted_iota(I32, tile.shape, 0) < filled, tile, FLOOR)
                    scores[h, rows, :] = tile
                    peak = jnp.maximum(peak, fold(tile, jnp.max))
                top.append(jnp.max(peak, axis=0, keepdims=True))
            for h in heads:
                weight = jnp.where(seen, jnp.exp2(fresh_scores[h] - top[h]), 0.0)
                padded = jnp.concatenate([weight, jnp.zeros((16 - chip_rows % 16, lanes), F32)], 0).astype(BF16)
                summed = lax.dot_general(fresh_values[h], padded, tn, preferred_element_type=F32)
                mass = weight
                for rows in pieces:
                    weight = jnp.exp2(scores[h, rows, :] - top[h])
                    if rows is pieces[-1]:
                        weight = jnp.where(lax.broadcasted_iota(I32, weight.shape, 0) < filled, weight, 0.0)
                    summed = summed + lax.dot_general(
                        values[rows, columns(h)], weight.astype(BF16), tn, preferred_element_type=F32
                    )
                    mass = mass + fold(weight, jnp.sum)
                sums[s, h] = summed
                tops[s, h] = top[h]
                totals[s, h] = jnp.sum(mass, axis=0, keepdims=True)

        for s, (keys, values) in enumerate(((keys_a, values_a), (keys_b, values_b))):
            needed = (limits[s] + TILE - 1) // TILE
            for tiles in range(slots // TILE + 1):
                pl.when(needed == tiles)(functools.partial(shard, s, keys, values, tiles))

        for h in heads:
            top_a, top_b = tops[0, h], tops[1, h]
            top = jnp.maximum(top_a, top_b)
            scale_a = jnp.exp2(top_a - top)
            scale_b = jnp.exp2(top_b - top)
            total = jnp.maximum(totals[0, h] * scale_a + totals[1, h] * scale_b, 1.0)
            merged = sums[0, h] * (scale_a / total) + sums[1, h] * (scale_b / total)
            width = group * chip_rows
            for i in range(chosen):
                for b in range(blocks):
                    at = i * set_lanes + b * width
                    cut = slice(at, at + width)
                    place = ((i * set_blocks + chunk * blocks + b) * kv_heads + h) * width
                    encode(out, place, merged[:, cut], top[:, cut], total[:, cut])
        return carry

    chunks = count // tokens
    if chunks == 1:
        attend_chunk(0, 0)
    else:
        lax.fori_loop(0, chunks, attend_chunk, 0)


def attend(start, gathered, chosen, fresh, cache, *, own_rows, orders):
    first, end = chosen
    count = gathered[0].shape[0]
    chip_rows = CORES * own_rows
    tokens = min(count, CHUNK_BLOCKS * chip_rows)
    slots = cache[0].shape[0]
    kv_heads = cache[0].shape[1] // LANES
    heads = gathered[0].shape[1] // LANES - 1
    group = heads // kv_heads
    lanes = (end - first) * tokens * group
    sizes = (own_rows, orders, group, kv_heads, len(gathered), first, end - first)
    return pl.pallas_call(
        functools.partial(attend_kernel, sizes),
        out_shape=jax.ShapeDtypeStruct((LANES + STAT_ROWS, (end - first) * count * heads), I16),
        in_specs=[SMEM] + [VMEM] * (len(gathered) + 6),
        out_specs=VMEM,
        scratch_shapes=[
            pltpu.VMEM((kv_heads, LANES, lanes), BF16),
            pltpu.VMEM((kv_heads, slots, lanes), F32),
            pltpu.VMEM((2, kv_heads, LANES, lanes), F32),
            pltpu.VMEM((2, kv_heads, 1, lanes), F32),
            pltpu.VMEM((2, kv_heads, 1, lanes), F32),
        ],
        compiler_params=pltpu.CompilerParams(vmem_limit_bytes=ATTEND_BYTES),
    )(start, *gathered, *fresh, *cache)


def merged_part(refs, dims, at):
    stats = [decode_stats(ref, dims, at) for ref in refs]
    top = functools.reduce(jnp.maximum, [x[0] for x in stats])
    masses = [x[1] * jnp.exp2(x[0] - top) for x in stats]
    total = functools.reduce(jnp.add, masses)
    values = 0.0
    for ref, mass, (_, _, unit) in zip(refs, masses, stats):
        values = values + ref[:dims, at].astype(I32).astype(F32) * (mass / total * unit)
    return values, top, total


def merge_kernel(inputs, *refs):
    parts, outs = refs[:inputs], refs[inputs:]
    dims = parts[0].shape[0] - STAT_ROWS
    width = outs[0].shape[1]
    step = min(width, 2 * LANES)
    for i, out in reversed(list(enumerate(outs))):
        for at in range(0, width, step):
            encode(out, at, *merged_part(parts, dims, slice(i * width + at, i * width + at + step)))


def merge(parts, pieces):
    rows, width = parts[0].shape
    shape = jax.ShapeDtypeStruct((rows, width // pieces), I16)
    return pl.pallas_call(
        functools.partial(merge_kernel, len(parts)),
        out_shape=(shape,) * pieces,
        in_specs=[VMEM] * len(parts),
        out_specs=(VMEM,) * pieces,
        compiler_params=SMALL,
    )(*parts)


def finish_kernel(group, inputs, *refs):
    parts, (mine, other) = refs[:inputs], refs[inputs:]
    dims = parts[0].shape[0] - STAT_ROWS
    own_rows = mine.shape[0]
    chip_rows = CORES * own_rows
    width = group * chip_rows
    for h in range(parts[0].shape[1] // width):
        values, _, _ = merged_part(parts, dims, slice(h * width, (h + 1) * width))
        rows = values.T
        for g in range(group):
            at = (h * group + g) * dims
            tokens = rows[g * chip_rows : (g + 1) * chip_rows]
            mine[:, at : at + dims] = tokens[:own_rows].astype(BF16)
            other[:, at : at + dims] = tokens[own_rows:].astype(BF16)


def finish(parts, own_rows, group):
    rows, width = parts[0].shape
    shape = jax.ShapeDtypeStruct((own_rows, width // (CORES * own_rows) * (rows - STAT_ROWS)), BF16)
    return pl.pallas_call(
        functools.partial(finish_kernel, group, len(parts)),
        out_shape=(shape, shape),
        in_specs=[VMEM] * len(parts),
        out_specs=(VMEM, VMEM),
        compiler_params=SMALL,
    )(*parts)


def place_kernel(mine, theirs, out):
    half = mine.shape[1]
    core = lax.axis_index("ctx") % CORES
    out[:, pl.ds(pl.multiple_of(core * half, LANES), half)] = mine[...]
    out[:, pl.ds(pl.multiple_of((1 - core) * half, LANES), half)] = theirs[...]


def place(mine, theirs):
    rows, half = mine.shape
    return pl.pallas_call(
        place_kernel,
        out_shape=jax.ShapeDtypeStruct((rows, CORES * half), BF16),
        in_specs=[VMEM, VMEM],
        out_specs=VMEM,
        compiler_params=SMALL,
    )(mine, theirs)


def per_device(
    queries, cache_keys, cached_value_rows, new_keys, prompt_value_rows, cache_len, prompt_start
):
    width = lax.axis_size("ctx")
    own_rows = queries.shape[0]
    group = queries.shape[1] // cache_keys.shape[1]
    bits = [CORES << i for i in range((width // CORES).bit_length() - 1)]
    orders = (tuple(bits[-1:] + bits[:-1]), tuple(bits[-2:] + bits[:-2]))
    odd = len(bits) % 2
    stages = [(0,)] * odd + [(i, i + 1) for i in range(odd, len(bits), 2)]

    def swap(x):
        return lax.ppermute(x, "ctx", [(i, i ^ 1) for i in range(width)])

    def partners(stage):
        return [
            [sum(order[bit] for k, bit in enumerate(stage) if c >> k & 1) for order in orders]
            for c in range(1, 1 << len(stage))
        ]

    def exchange(x, distance):
        return lax.ppermute(x, "ctx", [(i, i ^ distance[i % CORES]) for i in range(width)])

    def own_half(x):
        half = x.shape[1] // CORES
        return lax.dynamic_slice_in_dim(x, core * half, half, 1)

    core = lax.axis_index("ctx") % CORES
    held = join(cache_len, swap(cache_len), own_half(queries), swap(queries))
    cache_keys, cached_value_rows, held = lax.optimization_barrier((cache_keys, cached_value_rows, held))
    cache = [y for x in (cache_keys, cached_value_rows) for y in (own_half(x), swap(x))]
    for stage in stages:
        gathered = [held] + [exchange(held, distance) for distance in partners(stage)]
        if stage != stages[-1]:
            held = jnp.concatenate(gathered, axis=0)
    cache[0], cache[2], prompt_start = lax.optimization_barrier((cache[0], cache[2], prompt_start))
    gathered[-1], cache[0], cache[2], new_keys, prompt_value_rows = lax.optimization_barrier(
        (gathered[-1], cache[0], cache[2], new_keys, prompt_value_rows)
    )
    fresh = jnp.concatenate([new_keys, prompt_value_rows], axis=0)
    fresh = [fresh, swap(fresh)]
    half = len(gathered) // 2
    far, near = (
        attend(prompt_start, gathered, chosen, fresh, cache, own_rows=own_rows, orders=orders)
        for chosen in ((half, 2 * half), (0, half))
    )
    last = len(bits) - 1
    parts = [near, exchange(far, partners((last,))[0])]
    for stage in [(i - 1, i) if i else (i,) for i in range(last - 1, -1, -2)]:
        parts = merge(parts, 1 << len(stage))
        parts = [parts[0]] + [exchange(x, distance) for x, distance in zip(parts[1:], partners(stage))]
    mine, other = finish(parts, own_rows, group)
    return place(mine, swap(other))


def solution(mesh):
    return jax.shard_map(
        per_device,
        mesh=mesh,
        in_specs=(
            P(("groups", "ctx"), None),
            P(("groups", "ctx"), None),
            P(("groups", "ctx"), None),
            P(("groups", "ctx"), None),
            P(("groups", "ctx"), None),
            P(("groups", "ctx")),
            P("groups"),
        ),
        out_specs=P(("groups", "ctx"), None),
        check_vma=False,
    )
```

```python
import functools
import math

import jax
import jax.numpy as jnp
from jax import lax
from jax.experimental import pallas as pl
from jax.experimental.pallas import tpu as pltpu
from jax.sharding import PartitionSpec as P

KEY_VALUE_HEADS = 4
LANES = 128
CORES = 2
FLOOR = -1e30
TILE = 256
ATTEND_BYTES = 32 << 20
STAT_ROWS = 16
CHUNK_BLOCKS = 2
STEP = 2.0**15
MARGIN = 0.9998
F32 = jnp.float32
BF16 = jnp.bfloat16
I16 = jnp.int16
I32 = jnp.int32
VMEM = pl.BlockSpec(memory_space=pltpu.VMEM)
SMEM = pl.BlockSpec(memory_space=pltpu.SMEM)
SMALL = pltpu.CompilerParams(vmem_limit_bytes=8 << 20)


def encode(out, at, values, top, total):
    dims, width = values.shape
    largest = jnp.max(jnp.abs(values), axis=0, keepdims=True)
    exponent = jnp.floor(jnp.log2(jnp.maximum(largest, 1e-30))) + 1.0
    fixed = jnp.floor(values * (jnp.exp2(15.0 - exponent) * MARGIN) + 0.5)
    size = jnp.abs(top)
    level = jnp.zeros_like(top)
    scaled = top
    for i in range(1, 9):
        above = size >= STEP**i
        level = level + jnp.where(above, 1.0, 0.0)
        scaled = scaled * jnp.where(above, 1.0 / STEP, 1.0)
    a = jnp.floor(scaled)
    rest = (scaled - a) * STEP
    b = jnp.floor(rest)
    c = jnp.floor((rest - b) * STEP)
    logs = jnp.log2(total) * 1024.0
    la = jnp.floor(logs)
    lb = jnp.floor((logs - la) * STEP)
    row = lax.broadcasted_iota(I32, (STAT_ROWS, width), 0)
    stats = jnp.zeros((STAT_ROWS, width), F32)
    for i, part in enumerate((level, a, b, c, exponent, la, lb)):
        stats = jnp.where(row == i, part, stats)
    if not isinstance(at, int):
        at = pl.multiple_of(at, LANES)
    out[:dims, pl.ds(at, width)] = fixed.astype(I32).astype(I16)
    out[dims:, pl.ds(at, width)] = stats.astype(I32).astype(I16)


def decode_stats(ref, dims, at):
    stats = ref[dims:, at].astype(I32).astype(F32)

    def part(i):
        return stats[i : i + 1, :]

    top = part(1) + (part(2) + part(3) * (1.0 / STEP)) * (1.0 / STEP)
    for i in range(1, 9):
        top = top * jnp.where(part(0) >= i, STEP, 1.0)
    total = jnp.exp2((part(5) + part(6) * (1.0 / STEP)) * (1.0 / 1024.0))
    return top, total, jnp.exp2(part(4) - 15.0) * (1.0 / MARGIN)


def join_kernel(length, length_other, mine, queries_other, out):
    rows, half = mine.shape
    core = lax.axis_index("ctx") % CORES
    other = queries_other[:, pl.ds(pl.multiple_of(core * half, LANES), half)]
    out[:, :half] = jnp.concatenate([mine[...].astype(F32), other.astype(F32)], axis=0).astype(BF16)
    lane = lax.broadcasted_iota(I32, (CORES * rows, LANES), 1)
    row = lax.broadcasted_iota(I32, (CORES * rows, LANES), 0)
    count = jnp.where(row < rows, length[0], length_other[0])
    coded = jnp.where(lane == 0, count // LANES, jnp.where(lane == 1, count % LANES, 0))
    out[:, half:] = coded.astype(F32).astype(BF16)


def join(length, length_other, mine, queries_other):
    rows, half = mine.shape
    return pl.pallas_call(
        join_kernel,
        out_shape=jax.ShapeDtypeStruct((CORES * rows, half + LANES), BF16),
        in_specs=[SMEM, SMEM, VMEM, VMEM],
        out_specs=VMEM,
        compiler_params=SMALL,
    )(length, length_other, mine, queries_other)


def attend_kernel(sizes, *refs):
    own_rows, orders, group, kv_heads, sets, first, chosen = sizes
    start = refs[0]
    gathered = refs[1 : 1 + sets]
    fresh_a, fresh_b, keys_a, keys_b, values_a, values_b = refs[1 + sets : 7 + sets]
    out, query_t, scores, sums, tops, totals = refs[7 + sets :]
    queries = gathered[first : first + chosen]
    chip_rows = CORES * own_rows
    slots = keys_a.shape[0]
    count = gathered[0].shape[0]
    tokens = min(count, CHUNK_BLOCKS * chip_rows)
    blocks = tokens // chip_rows
    set_blocks = count // chip_rows
    set_lanes = tokens * group
    lanes = chosen * set_lanes
    me = lax.axis_index("ctx")
    core, chip = me % CORES, me // CORES
    factor = math.log2(math.e) / math.sqrt(LANES)
    heads = range(kv_heads)

    steps = [jnp.where(core == 0, a // CORES, b // CORES) for a, b in zip(*orders)]

    def origin(block):
        off = jnp.zeros_like(block)
        for i, step in enumerate(steps):
            off = off ^ jnp.where((block >> i) & 1 == 1, step, 0)
        return chip ^ off

    found = [0.0, 0.0, 0.0]
    for i, ref in enumerate(gathered):
        rows = ref.shape[0]
        lane = lax.broadcasted_iota(I32, (rows, LANES), 1)
        row = lax.broadcasted_iota(I32, (rows, LANES), 0)
        place = origin(row // chip_rows + i * set_blocks)
        inside = row % chip_rows
        counts = jnp.where(lane == 0, float(LANES), 1.0) * ref[:, ref.shape[1] - LANES :].astype(F32)
        counts = jnp.where((inside % own_rows == 0) & (lane < 2), counts, 0.0)
        here = place == chip
        second = inside >= own_rows
        for k, wanted in enumerate((place < chip, here & ~second, here & second)):
            found[k] = found[k] + jnp.sum(jnp.where(wanted, counts, 0.0), axis=0, keepdims=True)
    row = lax.broadcasted_iota(I32, (8, LANES), 0)
    found = functools.reduce(lambda x, k: jnp.where(row == k, found[k], x), range(3), jnp.zeros((8, LANES), F32))
    found = jnp.sum(found, axis=1, keepdims=True).astype(I32)
    before, length = found[0, 0], [found[1, 0], found[2, 0]]
    begins = [
        before + jnp.where(core == 1, length[1], 0),
        before + jnp.where(core == 0, length[0], 0),
    ]
    limits = [jnp.clip(jnp.minimum(n, start[0] - at), 0, slots) for n, at in zip(length, begins)]

    def attend_chunk(chunk, carry):
        key_row = lax.broadcasted_iota(I32, (chip_rows, lanes), 0)
        lane = lax.broadcasted_iota(I32, (chip_rows, lanes), 1)
        part = key_row // own_rows
        key_id = (chip * CORES + (core ^ part)) * own_rows + key_row % own_rows
        inside = lane % chip_rows
        block = (lane // set_lanes + first) * set_blocks + lane % set_lanes // (group * chip_rows) + chunk * blocks
        token = (origin(block) * CORES + (core ^ (inside // own_rows))) * own_rows + inside % own_rows
        causal = key_id <= token
        nothing = jnp.zeros((16 - chip_rows % 16, LANES), F32)
        fresh_scores, fresh_values = [], []

        for h in heads:
            rows = pl.ds(pl.multiple_of(chunk * tokens, tokens), tokens)
            q = jnp.concatenate(
                [
                    ref[rows, (h * group + g) * LANES : (h * group + g + 1) * LANES].astype(F32)[b * chip_rows :][:chip_rows]
                    for ref in queries
                    for b in range(blocks)
                    for g in range(group)
                ],
                axis=0,
            )
            query_t[h] = q.T.astype(BF16)
            at = pl.multiple_of((core * kv_heads + h) * LANES, LANES)

            mine = fresh_a[:, pl.ds(at, LANES)].astype(F32)
            theirs = fresh_b[:, pl.ds(at, LANES)].astype(F32)
            new_keys = jnp.concatenate([mine[:own_rows], theirs[:own_rows], nothing], 0).astype(BF16)
            new_values = jnp.concatenate([mine[own_rows:], theirs[own_rows:], nothing], 0).astype(BF16)
            fresh_values.append(new_values)
            fresh_scores.append(jnp.dot(new_keys, query_t[h], preferred_element_type=F32)[:chip_rows] * factor)

        def fold(tile, combine):
            return combine(tile.reshape(tile.shape[0] // 8, 8, lanes), axis=0)

        tn = (((0,), (0,)), ((), ()))

        def shard(s, keys, values, tiles):
            seen = causal & (part == s)
            filled = limits[s] - (tiles - 1) * TILE

            def columns(h):
                return pl.ds(pl.multiple_of((core * kv_heads * LANES if s else 0) + h * LANES, LANES), LANES)

            pieces = [slice(0, (tiles - 1) * TILE)] * (tiles > 1) + [slice((tiles - 1) * TILE, tiles * TILE)] * (tiles > 0)
            top = []
            for h in heads:
                peak = jnp.where(seen, fresh_scores[h], FLOOR)
                for rows in pieces:
                    tile = jnp.dot(keys[rows, columns(h)], query_t[h], preferred_element_type=F32) * factor
                    if rows is pieces[-1]:
                        tile = jnp.where(lax.broadcasted_iota(I32, tile.shape, 0) < filled, tile, FLOOR)
                    scores[h, rows, :] = tile
                    peak = jnp.maximum(peak, fold(tile, jnp.max))
                top.append(jnp.max(peak, axis=0, keepdims=True))
            for h in heads:
                weight = jnp.where(seen, jnp.exp2(fresh_scores[h] - top[h]), 0.0)
                padded = jnp.concatenate([weight, jnp.zeros((16 - chip_rows % 16, lanes), F32)], 0).astype(BF16)
                summed = lax.dot_general(fresh_values[h], padded, tn, preferred_element_type=F32)
                mass = weight
                for rows in pieces:
                    weight = jnp.exp2(scores[h, rows, :] - top[h])
                    if rows is pieces[-1]:
                        weight = jnp.where(lax.broadcasted_iota(I32, weight.shape, 0) < filled, weight, 0.0)
                    summed = summed + lax.dot_general(
                        values[rows, columns(h)], weight.astype(BF16), tn, preferred_element_type=F32
                    )
                    mass = mass + fold(weight, jnp.sum)
                sums[s, h] = summed
                tops[s, h] = top[h]
                totals[s, h] = jnp.sum(mass, axis=0, keepdims=True)

        for s, (keys, values) in enumerate(((keys_a, values_a), (keys_b, values_b))):
            needed = (limits[s] + TILE - 1) // TILE
            for tiles in range(slots // TILE + 1):
                pl.when(needed == tiles)(functools.partial(shard, s, keys, values, tiles))

        for h in heads:
            top_a, top_b = tops[0, h], tops[1, h]
            top = jnp.maximum(top_a, top_b)
            scale_a = jnp.exp2(top_a - top)
            scale_b = jnp.exp2(top_b - top)
            total = jnp.maximum(totals[0, h] * scale_a + totals[1, h] * scale_b, 1.0)
            merged = sums[0, h] * (scale_a / total) + sums[1, h] * (scale_b / total)
            width = group * chip_rows
            for i in range(chosen):
                for b in range(blocks):
                    at = i * set_lanes + b * width
                    cut = slice(at, at + width)
                    place = ((i * set_blocks + chunk * blocks + b) * kv_heads + h) * width
                    encode(out, place, merged[:, cut], top[:, cut], total[:, cut])
        return carry

    chunks = count // tokens
    if chunks == 1:
        attend_chunk(0, 0)
    else:
        lax.fori_loop(0, chunks, attend_chunk, 0)


def attend(start, gathered, chosen, fresh, cache, *, own_rows, orders):
    first, end = chosen
    count = gathered[0].shape[0]
    chip_rows = CORES * own_rows
    tokens = min(count, CHUNK_BLOCKS * chip_rows)
    slots = cache[0].shape[0]
    kv_heads = cache[0].shape[1] // LANES
    heads = gathered[0].shape[1] // LANES - 1
    group = heads // kv_heads
    lanes = (end - first) * tokens * group
    sizes = (own_rows, orders, group, kv_heads, len(gathered), first, end - first)
    return pl.pallas_call(
        functools.partial(attend_kernel, sizes),
        out_shape=jax.ShapeDtypeStruct((LANES + STAT_ROWS, (end - first) * count * heads), I16),
        in_specs=[SMEM] + [VMEM] * (len(gathered) + 6),
        out_specs=VMEM,
        scratch_shapes=[
            pltpu.VMEM((kv_heads, LANES, lanes), BF16),
            pltpu.VMEM((kv_heads, slots, lanes), F32),
            pltpu.VMEM((2, kv_heads, LANES, lanes), F32),
            pltpu.VMEM((2, kv_heads, 1, lanes), F32),
            pltpu.VMEM((2, kv_heads, 1, lanes), F32),
        ],
        compiler_params=pltpu.CompilerParams(vmem_limit_bytes=ATTEND_BYTES),
    )(start, *gathered, *fresh, *cache)


def merged_part(refs, dims, at):
    stats = [decode_stats(ref, dims, at) for ref in refs]
    top = functools.reduce(jnp.maximum, [x[0] for x in stats])
    masses = [x[1] * jnp.exp2(x[0] - top) for x in stats]
    total = functools.reduce(jnp.add, masses)
    values = 0.0
    for ref, mass, (_, _, unit) in zip(refs, masses, stats):
        values = values + ref[:dims, at].astype(I32).astype(F32) * (mass / total * unit)
    return values, top, total


def merge_kernel(inputs, *refs):
    parts, outs = refs[:inputs], refs[inputs:]
    dims = parts[0].shape[0] - STAT_ROWS
    width = outs[0].shape[1]
    step = min(width, 2 * LANES)
    for i, out in reversed(list(enumerate(outs))):
        for at in range(0, width, step):
            encode(out, at, *merged_part(parts, dims, slice(i * width + at, i * width + at + step)))


def merge(parts, pieces):
    rows, width = parts[0].shape
    shape = jax.ShapeDtypeStruct((rows, width // pieces), I16)
    return pl.pallas_call(
        functools.partial(merge_kernel, len(parts)),
        out_shape=(shape,) * pieces,
        in_specs=[VMEM] * len(parts),
        out_specs=(VMEM,) * pieces,
        compiler_params=SMALL,
    )(*parts)


def finish_kernel(group, inputs, *refs):
    parts, (mine, other) = refs[:inputs], refs[inputs:]
    dims = parts[0].shape[0] - STAT_ROWS
    own_rows = mine.shape[0]
    chip_rows = CORES * own_rows
    width = group * chip_rows
    for h in range(parts[0].shape[1] // width):
        values, _, _ = merged_part(parts, dims, slice(h * width, (h + 1) * width))
        rows = values.T
        for g in range(group):
            at = (h * group + g) * dims
            tokens = rows[g * chip_rows : (g + 1) * chip_rows]
            mine[:, at : at + dims] = tokens[:own_rows].astype(BF16)
            other[:, at : at + dims] = tokens[own_rows:].astype(BF16)


def finish(parts, own_rows, group):
    rows, width = parts[0].shape
    shape = jax.ShapeDtypeStruct((own_rows, width // (CORES * own_rows) * (rows - STAT_ROWS)), BF16)
    return pl.pallas_call(
        functools.partial(finish_kernel, group, len(parts)),
        out_shape=(shape, shape),
        in_specs=[VMEM] * len(parts),
        out_specs=(VMEM, VMEM),
        compiler_params=SMALL,
    )(*parts)


def place_kernel(mine, theirs, out):
    half = mine.shape[1]
    core = lax.axis_index("ctx") % CORES
    out[:, pl.ds(pl.multiple_of(core * half, LANES), half)] = mine[...]
    out[:, pl.ds(pl.multiple_of((1 - core) * half, LANES), half)] = theirs[...]


def place(mine, theirs):
    rows, half = mine.shape
    return pl.pallas_call(
        place_kernel,
        out_shape=jax.ShapeDtypeStruct((rows, CORES * half), BF16),
        in_specs=[VMEM, VMEM],
        out_specs=VMEM,
        compiler_params=SMALL,
    )(mine, theirs)


def per_device(
    queries, cache_keys, cached_value_rows, new_keys, prompt_value_rows, cache_len, prompt_start
):
    width = lax.axis_size("ctx")
    own_rows = queries.shape[0]
    group = queries.shape[1] // cache_keys.shape[1]
    bits = [CORES << i for i in range((width // CORES).bit_length() - 1)]
    orders = (tuple(bits[-1:] + bits[:-1]), tuple(bits[-2:] + bits[:-2]))
    odd = len(bits) % 2
    stages = [(0,)] * odd + [(i, i + 1) for i in range(odd, len(bits), 2)]

    def swap(x):
        return lax.ppermute(x, "ctx", [(i, i ^ 1) for i in range(width)])

    def partners(stage):
        return [
            [sum(order[bit] for k, bit in enumerate(stage) if c >> k & 1) for order in orders]
            for c in range(1, 1 << len(stage))
        ]

    def exchange(x, distance):
        return lax.ppermute(x, "ctx", [(i, i ^ distance[i % CORES]) for i in range(width)])

    def own_half(x):
        half = x.shape[1] // CORES
        return lax.dynamic_slice_in_dim(x, core * half, half, 1)

    core = lax.axis_index("ctx") % CORES
    held = join(cache_len, swap(cache_len), own_half(queries), swap(queries))
    cache_keys, cached_value_rows, held = lax.optimization_barrier((cache_keys, cached_value_rows, held))
    cache = [y for x in (cache_keys, cached_value_rows) for y in (own_half(x), swap(x))]
    for stage in stages:
        gathered = [held] + [exchange(held, distance) for distance in partners(stage)]
        if stage != stages[-1]:
            held = jnp.concatenate(gathered, axis=0)
    cache[0], cache[2], prompt_start = lax.optimization_barrier((cache[0], cache[2], prompt_start))
    gathered[-1], cache[0], cache[2], new_keys, prompt_value_rows = lax.optimization_barrier(
        (gathered[-1], cache[0], cache[2], new_keys, prompt_value_rows)
    )
    fresh = jnp.concatenate([new_keys, prompt_value_rows], axis=0)
    fresh = [fresh, swap(fresh)]
    half = len(gathered) // 2
    far, near = (
        attend(prompt_start, gathered, chosen, fresh, cache, own_rows=own_rows, orders=orders)
        for chosen in ((half, 2 * half), (0, half))
    )
    last = len(bits) - 1
    parts = [near, exchange(far, partners((last,))[0])]
    for stage in [(i - 1, i) if i else (i,) for i in range(last - 1, -1, -2)]:
        parts = merge(parts, 1 << len(stage))
        sent = list(zip(parts[1:], partners(stage)))
        parts = [parts[0]] + [exchange(x, distance) for x, distance in sent[1:] + sent[:1]]
    mine, other = finish(parts, own_rows, group)
    return place(mine, swap(other))


def solution(mesh):
    return jax.shard_map(
        per_device,
        mesh=mesh,
        in_specs=(
            P(("groups", "ctx"), None),
            P(("groups", "ctx"), None),
            P(("groups", "ctx"), None),
            P(("groups", "ctx"), None),
            P(("groups", "ctx"), None),
            P(("groups", "ctx")),
            P("groups"),
        ),
        out_specs=P(("groups", "ctx"), None),
        check_vma=False,
    )
```

```python
import functools
import math

import jax
import jax.numpy as jnp
from jax import lax
from jax.experimental import pallas as pl
from jax.experimental.pallas import tpu as pltpu
from jax.sharding import PartitionSpec as P

KEY_VALUE_HEADS = 4
LANES = 128
CORES = 2
FLOOR = -1e30
TILE = 256
ATTEND_BYTES = 32 << 20
STAT_ROWS = 16
CHUNK_BLOCKS = 2
STEP = 2.0**15
MARGIN = 0.9998
F32 = jnp.float32
BF16 = jnp.bfloat16
I16 = jnp.int16
I32 = jnp.int32
VMEM = pl.BlockSpec(memory_space=pltpu.VMEM)
SMEM = pl.BlockSpec(memory_space=pltpu.SMEM)
SMALL = pltpu.CompilerParams(vmem_limit_bytes=8 << 20)


def encode(out, at, values, top, total):
    dims, width = values.shape
    largest = jnp.max(jnp.abs(values), axis=0, keepdims=True)
    exponent = jnp.floor(jnp.log2(jnp.maximum(largest, 1e-30))) + 1.0
    fixed = jnp.floor(values * (jnp.exp2(15.0 - exponent) * MARGIN) + 0.5)
    size = jnp.abs(top)
    level = jnp.zeros_like(top)
    scaled = top
    for i in range(1, 9):
        above = size >= STEP**i
        level = level + jnp.where(above, 1.0, 0.0)
        scaled = scaled * jnp.where(above, 1.0 / STEP, 1.0)
    a = jnp.floor(scaled)
    rest = (scaled - a) * STEP
    b = jnp.floor(rest)
    c = jnp.floor((rest - b) * STEP)
    logs = jnp.log2(total) * 1024.0
    la = jnp.floor(logs)
    lb = jnp.floor((logs - la) * STEP)
    row = lax.broadcasted_iota(I32, (STAT_ROWS, width), 0)
    stats = jnp.zeros((STAT_ROWS, width), F32)
    for i, part in enumerate((level, a, b, c, exponent, la, lb)):
        stats = jnp.where(row == i, part, stats)
    if not isinstance(at, int):
        at = pl.multiple_of(at, LANES)
    out[:dims, pl.ds(at, width)] = fixed.astype(I32).astype(I16)
    out[dims:, pl.ds(at, width)] = stats.astype(I32).astype(I16)


def decode_stats(ref, dims, at):
    stats = ref[dims:, at].astype(I32).astype(F32)

    def part(i):
        return stats[i : i + 1, :]

    top = part(1) + (part(2) + part(3) * (1.0 / STEP)) * (1.0 / STEP)
    for i in range(1, 9):
        top = top * jnp.where(part(0) >= i, STEP, 1.0)
    total = jnp.exp2((part(5) + part(6) * (1.0 / STEP)) * (1.0 / 1024.0))
    return top, total, jnp.exp2(part(4) - 15.0) * (1.0 / MARGIN)


def join_kernel(length, length_other, mine, queries_other, out):
    rows, half = mine.shape
    core = lax.axis_index("ctx") % CORES
    other = queries_other[:, pl.ds(pl.multiple_of(core * half, LANES), half)]
    out[:, :half] = jnp.concatenate([mine[...].astype(F32), other.astype(F32)], axis=0).astype(BF16)
    lane = lax.broadcasted_iota(I32, (CORES * rows, LANES), 1)
    row = lax.broadcasted_iota(I32, (CORES * rows, LANES), 0)
    count = jnp.where(row < rows, length[0], length_other[0])
    coded = jnp.where(lane == 0, count // LANES, jnp.where(lane == 1, count % LANES, 0))
    out[:, half:] = coded.astype(F32).astype(BF16)


def join(length, length_other, mine, queries_other):
    rows, half = mine.shape
    return pl.pallas_call(
        join_kernel,
        out_shape=jax.ShapeDtypeStruct((CORES * rows, half + LANES), BF16),
        in_specs=[SMEM, SMEM, VMEM, VMEM],
        out_specs=VMEM,
        compiler_params=SMALL,
    )(length, length_other, mine, queries_other)


def attend_kernel(sizes, *refs):
    own_rows, orders, group, kv_heads, sets, first, chosen = sizes
    start = refs[0]
    gathered = refs[1 : 1 + sets]
    fresh_a, fresh_b, keys_a, keys_b, values_a, values_b = refs[1 + sets : 7 + sets]
    out, query_t, scores, sums, tops, totals = refs[7 + sets :]
    queries = gathered[first : first + chosen]
    chip_rows = CORES * own_rows
    slots = keys_a.shape[0]
    count = gathered[0].shape[0]
    tokens = min(count, CHUNK_BLOCKS * chip_rows)
    blocks = tokens // chip_rows
    set_blocks = count // chip_rows
    set_lanes = tokens * group
    lanes = chosen * set_lanes
    me = lax.axis_index("ctx")
    core, chip = me % CORES, me // CORES
    factor = math.log2(math.e) / math.sqrt(LANES)
    heads = range(kv_heads)

    steps = [jnp.where(core == 0, a // CORES, b // CORES) for a, b in zip(*orders)]

    def origin(block):
        off = jnp.zeros_like(block)
        for i, step in enumerate(steps):
            off = off ^ jnp.where((block >> i) & 1 == 1, step, 0)
        return chip ^ off

    found = [0.0, 0.0, 0.0]
    for i, ref in enumerate(gathered):
        rows = ref.shape[0]
        lane = lax.broadcasted_iota(I32, (rows, LANES), 1)
        row = lax.broadcasted_iota(I32, (rows, LANES), 0)
        place = origin(row // chip_rows + i * set_blocks)
        inside = row % chip_rows
        counts = jnp.where(lane == 0, float(LANES), 1.0) * ref[:, ref.shape[1] - LANES :].astype(F32)
        counts = jnp.where((inside % own_rows == 0) & (lane < 2), counts, 0.0)
        here = place == chip
        second = inside >= own_rows
        for k, wanted in enumerate((place < chip, here & ~second, here & second)):
            found[k] = found[k] + jnp.sum(jnp.where(wanted, counts, 0.0), axis=0, keepdims=True)
    row = lax.broadcasted_iota(I32, (8, LANES), 0)
    found = functools.reduce(lambda x, k: jnp.where(row == k, found[k], x), range(3), jnp.zeros((8, LANES), F32))
    found = jnp.sum(found, axis=1, keepdims=True).astype(I32)
    before, length = found[0, 0], [found[1, 0], found[2, 0]]
    begins = [
        before + jnp.where(core == 1, length[1], 0),
        before + jnp.where(core == 0, length[0], 0),
    ]
    limits = [jnp.clip(jnp.minimum(n, start[0] - at), 0, slots) for n, at in zip(length, begins)]

    def attend_chunk(chunk, carry):
        key_row = lax.broadcasted_iota(I32, (chip_rows, lanes), 0)
        lane = lax.broadcasted_iota(I32, (chip_rows, lanes), 1)
        part = key_row // own_rows
        key_id = (chip * CORES + (core ^ part)) * own_rows + key_row % own_rows
        inside = lane % chip_rows
        block = (lane // set_lanes + first) * set_blocks + lane % set_lanes // (group * chip_rows) + chunk * blocks
        token = (origin(block) * CORES + (core ^ (inside // own_rows))) * own_rows + inside % own_rows
        causal = key_id <= token
        nothing = jnp.zeros((16 - chip_rows % 16, LANES), F32)
        fresh_scores, fresh_values = [], []

        for h in heads:
            rows = pl.ds(pl.multiple_of(chunk * tokens, tokens), tokens)
            q = jnp.concatenate(
                [
                    ref[rows, (h * group + g) * LANES : (h * group + g + 1) * LANES].astype(F32)[b * chip_rows :][:chip_rows]
                    for ref in queries
                    for b in range(blocks)
                    for g in range(group)
                ],
                axis=0,
            )
            query_t[h] = q.T.astype(BF16)
            at = pl.multiple_of((core * kv_heads + h) * LANES, LANES)

            mine = fresh_a[:, pl.ds(at, LANES)].astype(F32)
            theirs = fresh_b[:, pl.ds(at, LANES)].astype(F32)
            new_keys = jnp.concatenate([mine[:own_rows], theirs[:own_rows], nothing], 0).astype(BF16)
            new_values = jnp.concatenate([mine[own_rows:], theirs[own_rows:], nothing], 0).astype(BF16)
            fresh_values.append(new_values)
            fresh_scores.append(jnp.dot(new_keys, query_t[h], preferred_element_type=F32)[:chip_rows] * factor)

        def fold(tile, combine):
            return combine(tile.reshape(tile.shape[0] // 8, 8, lanes), axis=0)

        tn = (((0,), (0,)), ((), ()))

        def shard(s, keys, values, tiles):
            seen = causal & (part == s)
            filled = limits[s] - (tiles - 1) * TILE

            def columns(h):
                return pl.ds(pl.multiple_of((core * kv_heads * LANES if s else 0) + h * LANES, LANES), LANES)

            pieces = [slice(0, (tiles - 1) * TILE)] * (tiles > 1) + [slice((tiles - 1) * TILE, tiles * TILE)] * (tiles > 0)
            top = []
            for h in heads:
                peak = jnp.where(seen, fresh_scores[h], FLOOR)
                for rows in pieces:
                    tile = jnp.dot(keys[rows, columns(h)], query_t[h], preferred_element_type=F32) * factor
                    if rows is pieces[-1]:
                        tile = jnp.where(lax.broadcasted_iota(I32, tile.shape, 0) < filled, tile, FLOOR)
                    scores[h, rows, :] = tile
                    peak = jnp.maximum(peak, fold(tile, jnp.max))
                top.append(jnp.max(peak, axis=0, keepdims=True))
            for h in heads:
                weight = jnp.where(seen, jnp.exp2(fresh_scores[h] - top[h]), 0.0)
                padded = jnp.concatenate([weight, jnp.zeros((16 - chip_rows % 16, lanes), F32)], 0).astype(BF16)
                summed = lax.dot_general(fresh_values[h], padded, tn, preferred_element_type=F32)
                mass = weight
                for rows in pieces:
                    weight = jnp.exp2(scores[h, rows, :] - top[h])
                    if rows is pieces[-1]:
                        weight = jnp.where(lax.broadcasted_iota(I32, weight.shape, 0) < filled, weight, 0.0)
                    summed = summed + lax.dot_general(
                        values[rows, columns(h)], weight.astype(BF16), tn, preferred_element_type=F32
                    )
                    mass = mass + fold(weight, jnp.sum)
                sums[s, h] = summed
                tops[s, h] = top[h]
                totals[s, h] = jnp.sum(mass, axis=0, keepdims=True)

        for s, (keys, values) in enumerate(((keys_a, values_a), (keys_b, values_b))):
            needed = (limits[s] + TILE - 1) // TILE
            for tiles in range(slots // TILE + 1):
                pl.when(needed == tiles)(functools.partial(shard, s, keys, values, tiles))

        for h in heads:
            top_a, top_b = tops[0, h], tops[1, h]
            top = jnp.maximum(top_a, top_b)
            scale_a = jnp.exp2(top_a - top)
            scale_b = jnp.exp2(top_b - top)
            total = jnp.maximum(totals[0, h] * scale_a + totals[1, h] * scale_b, 1.0)
            merged = sums[0, h] * (scale_a / total) + sums[1, h] * (scale_b / total)
            width = group * chip_rows
            for i in range(chosen):
                for b in range(blocks):
                    at = i * set_lanes + b * width
                    cut = slice(at, at + width)
                    place = ((i * set_blocks + chunk * blocks + b) * kv_heads + h) * width
                    encode(out, place, merged[:, cut], top[:, cut], total[:, cut])
        return carry

    chunks = count // tokens
    if chunks == 1:
        attend_chunk(0, 0)
    else:
        lax.fori_loop(0, chunks, attend_chunk, 0)


def attend(start, gathered, chosen, fresh, cache, *, own_rows, orders):
    first, end = chosen
    count = gathered[0].shape[0]
    chip_rows = CORES * own_rows
    tokens = min(count, CHUNK_BLOCKS * chip_rows)
    slots = cache[0].shape[0]
    kv_heads = cache[0].shape[1] // LANES
    heads = gathered[0].shape[1] // LANES - 1
    group = heads // kv_heads
    lanes = (end - first) * tokens * group
    sizes = (own_rows, orders, group, kv_heads, len(gathered), first, end - first)
    return pl.pallas_call(
        functools.partial(attend_kernel, sizes),
        out_shape=jax.ShapeDtypeStruct((LANES + STAT_ROWS, (end - first) * count * heads), I16),
        in_specs=[SMEM] + [VMEM] * (len(gathered) + 6),
        out_specs=VMEM,
        scratch_shapes=[
            pltpu.VMEM((kv_heads, LANES, lanes), BF16),
            pltpu.VMEM((kv_heads, slots, lanes), F32),
            pltpu.VMEM((2, kv_heads, LANES, lanes), F32),
            pltpu.VMEM((2, kv_heads, 1, lanes), F32),
            pltpu.VMEM((2, kv_heads, 1, lanes), F32),
        ],
        compiler_params=pltpu.CompilerParams(vmem_limit_bytes=ATTEND_BYTES),
    )(start, *gathered, *fresh, *cache)


def merged_part(refs, dims, at):
    stats = [decode_stats(ref, dims, at) for ref in refs]
    top = functools.reduce(jnp.maximum, [x[0] for x in stats])
    masses = [x[1] * jnp.exp2(x[0] - top) for x in stats]
    total = functools.reduce(jnp.add, masses)
    values = 0.0
    for ref, mass, (_, _, unit) in zip(refs, masses, stats):
        values = values + ref[:dims, at].astype(I32).astype(F32) * (mass / total * unit)
    return values, top, total


def merge_kernel(inputs, *refs):
    parts, outs = refs[:inputs], refs[inputs:]
    dims = parts[0].shape[0] - STAT_ROWS
    width = outs[0].shape[1]
    step = min(width, 2 * LANES)
    for i, out in reversed(list(enumerate(outs))):
        for at in range(0, width, step):
            encode(out, at, *merged_part(parts, dims, slice(i * width + at, i * width + at + step)))


def merge(parts, pieces):
    rows, width = parts[0].shape
    shape = jax.ShapeDtypeStruct((rows, width // pieces), I16)
    return pl.pallas_call(
        functools.partial(merge_kernel, len(parts)),
        out_shape=(shape,) * pieces,
        in_specs=[VMEM] * len(parts),
        out_specs=(VMEM,) * pieces,
        compiler_params=SMALL,
    )(*parts)


def finish_kernel(group, inputs, *refs):
    parts, (mine, other) = refs[:inputs], refs[inputs:]
    dims = parts[0].shape[0] - STAT_ROWS
    own_rows = mine.shape[0]
    chip_rows = CORES * own_rows
    width = group * chip_rows
    for h in range(parts[0].shape[1] // width):
        values, _, _ = merged_part(parts, dims, slice(h * width, (h + 1) * width))
        rows = values.T
        for g in range(group):
            at = (h * group + g) * dims
            tokens = rows[g * chip_rows : (g + 1) * chip_rows]
            mine[:, at : at + dims] = tokens[:own_rows].astype(BF16)
            other[:, at : at + dims] = tokens[own_rows:].astype(BF16)


def finish(parts, own_rows, group):
    rows, width = parts[0].shape
    shape = jax.ShapeDtypeStruct((own_rows, width // (CORES * own_rows) * (rows - STAT_ROWS)), BF16)
    return pl.pallas_call(
        functools.partial(finish_kernel, group, len(parts)),
        out_shape=(shape, shape),
        in_specs=[VMEM] * len(parts),
        out_specs=(VMEM, VMEM),
        compiler_params=SMALL,
    )(*parts)


def place_kernel(mine, theirs, out):
    half = mine.shape[1]
    core = lax.axis_index("ctx") % CORES
    out[:, pl.ds(pl.multiple_of(core * half, LANES), half)] = mine[...]
    out[:, pl.ds(pl.multiple_of((1 - core) * half, LANES), half)] = theirs[...]


def place(mine, theirs):
    rows, half = mine.shape
    return pl.pallas_call(
        place_kernel,
        out_shape=jax.ShapeDtypeStruct((rows, CORES * half), BF16),
        in_specs=[VMEM, VMEM],
        out_specs=VMEM,
        compiler_params=SMALL,
    )(mine, theirs)


def per_device(
    queries, cache_keys, cached_value_rows, new_keys, prompt_value_rows, cache_len, prompt_start
):
    width = lax.axis_size("ctx")
    own_rows = queries.shape[0]
    group = queries.shape[1] // cache_keys.shape[1]
    bits = [CORES << i for i in range((width // CORES).bit_length() - 1)]
    orders = (tuple(bits[-1:] + bits[:-1]), tuple(bits[-2:] + bits[:-2]))
    odd = len(bits) % 2
    stages = [(0,)] * odd + [(i, i + 1) for i in range(odd, len(bits), 2)]

    def swap(x):
        return lax.ppermute(x, "ctx", [(i, i ^ 1) for i in range(width)])

    def partners(stage):
        return [
            [sum(order[bit] for k, bit in enumerate(stage) if c >> k & 1) for order in orders]
            for c in range(1, 1 << len(stage))
        ]

    def exchange(x, distance):
        return lax.ppermute(x, "ctx", [(i, i ^ distance[i % CORES]) for i in range(width)])

    def own_half(x):
        half = x.shape[1] // CORES
        return lax.dynamic_slice_in_dim(x, core * half, half, 1)

    core = lax.axis_index("ctx") % CORES
    held = join(cache_len, swap(cache_len), own_half(queries), swap(queries))
    cache_keys, cached_value_rows, held = lax.optimization_barrier((cache_keys, cached_value_rows, held))
    cache = [y for x in (cache_keys, cached_value_rows) for y in (own_half(x), swap(x))]
    for stage in stages:
        distances = partners(stage)
        came = [exchange(held, distance) for distance in distances[1:] + distances[:1]]
        gathered = [held] + came[-1:] + came[:-1]
        if stage != stages[-1]:
            held = jnp.concatenate(gathered, axis=0)
    cache[0], cache[2], prompt_start = lax.optimization_barrier((cache[0], cache[2], prompt_start))
    gathered[-1], cache[0], cache[2], new_keys, prompt_value_rows = lax.optimization_barrier(
        (gathered[-1], cache[0], cache[2], new_keys, prompt_value_rows)
    )
    fresh = jnp.concatenate([new_keys, prompt_value_rows], axis=0)
    fresh = [fresh, swap(fresh)]
    half = len(gathered) // 2
    far, near = (
        attend(prompt_start, gathered, chosen, fresh, cache, own_rows=own_rows, orders=orders)
        for chosen in ((half, 2 * half), (0, half))
    )
    last = len(bits) - 1
    parts = [near, exchange(far, partners((last,))[0])]
    for stage in [(i - 1, i) if i else (i,) for i in range(last - 1, -1, -2)]:
        parts = merge(parts, 1 << len(stage))
        sent = list(zip(parts[1:], partners(stage)))
        parts = [parts[0]] + [exchange(x, distance) for x, distance in sent[1:] + sent[:1]]
    mine, other = finish(parts, own_rows, group)
    return place(mine, swap(other))


def solution(mesh):
    return jax.shard_map(
        per_device,
        mesh=mesh,
        in_specs=(
            P(("groups", "ctx"), None),
            P(("groups", "ctx"), None),
            P(("groups", "ctx"), None),
            P(("groups", "ctx"), None),
            P(("groups", "ctx"), None),
            P(("groups", "ctx")),
            P("groups"),
        ),
        out_specs=P(("groups", "ctx"), None),
        check_vma=False,
    )
```
